32 devices in a mesh: rep: 4 (over z), grp: 8 (over y, x, core).
Axes of the slice: x: 2, y: 2, z: 4, core: 2. Of those that a mesh axis runs over, the one named last changes fastest.
Arguments:
- tokens: bfloat16 [192, 197, 768], P(('rep', 'grp')), may hold values from -6 to 6
- cotangent: bfloat16 [192, 197, 768], P(('rep', 'grp')), may hold values from -6 to 6
- heads_in: bfloat16 [768, 2304], P('grp'), may hold values from -0.3125 to 0.3125
- heads_out: bfloat16 [768, 768], P('grp'), may hold values from -0.875 to 0.875
- slot_router: bfloat16 [768, 4], P('grp'), may hold values from -0.109375 to 0.109375
- first_gain: bfloat16 [768], P('grp'), may hold values from 0.5 to 1.5
- second_gain: bfloat16 [768], P('grp'), may hold values from 0.5 to 1.5
- expert_in: bfloat16 [8, 768, 1536], P('grp'), may hold values from -3 to 3
- expert_out: bfloat16 [8, 1536, 768], P('grp'), may hold values from -0.21875 to 0.21875
Outputs:
- output: bfloat16 [192, 197, 768], P(('rep', 'grp'))
- token_grad: bfloat16 [192, 197, 768], P(('rep', 'grp'))
- heads_in_grad: float32 [768, 2304], P('grp')
- heads_out_grad: float32 [768, 768], P('grp')
- router_grad: float32 [768, 4], P('grp')
- first_gain_grad: float32 [768], P('grp')
- second_gain_grad: float32 [768], P('grp')
- expert_in_grad: float32 [8, 768, 1536], P('grp')
- expert_out_grad: float32 [8, 1536, 768], P('grp')
The draws below stay inside these ranges and needn't reach their ends.
All inputs are finite; a program needn't handle non-finite values.
Results may differ from the reference program's by a relative error of at most 0.019.
Values may be sent and summed in bfloat16 or wider, within the bound.
No kernel may reach another device: no remote copies, remote signals or barrier semaphores. Data moves between devices by JAX's collectives and lax.ppermute only.
A program may use at most 192 MiB of HBM per device.

```python
import jax
import jax.numpy as jnp
from jax import lax

D = 768
HEADS = 12
HEAD_DIM = 64
EXP_HID = 3072
SEQ = 197
IMG_DEV = 6
EXPERTS = 4
HALF = 1536
IMAGES = 192


def level_of(rng, shape, cuts, least, top_value):
    level = 1.0
    for position, shards_of in cuts:
        steps = jax.random.uniform(jax.random.fold_in(jax.random.fold_in(rng, 6), position), (shards_of,), jnp.float32, least / len(cuts), top_value / len(cuts))
        level = level * jnp.repeat(jnp.exp(steps), shape[position] // shards_of).reshape((-1,) + (1,) * (len(shape) - 1 - position))
    return level


def noise(key, dims, scale, limit, cuts=(), dtype=jnp.bfloat16):
    values = jax.random.normal(key, dims, jnp.float32) * scale
    if len(cuts) > 0:
        values = level_of(key, dims, cuts, -0.22, 0.18) * values
    return jnp.clip(values, min=-limit, max=limit).astype(dtype)


def setup_inputs(seed: int = 0) -> dict:
    key_of = jax.random.split(jax.random.key(seed), 10)
    tokens = noise(key_of[0], (IMAGES, SEQ, D), 1.0, 6.0, ((0, 32),))
    cotangent = noise(key_of[1], (IMAGES, SEQ, D), 1.0, 6.0, ((0, 32),))
    heads_in = noise(key_of[2], (D, 3 * D), (D // 2) ** -0.5, 0.3125, ((0, 8),))
    heads_out = noise(key_of[3], (D, D), (D // 16) ** -0.5, 0.875, ((0, 8),))
    slot_router = noise(key_of[4], (D, EXPERTS), (4 * D) ** -0.5, 0.109375, ((0, 8),))
    first_gain = jnp.clip(1.0 + 0.1 * jax.random.normal(key_of[5], (D,), jnp.float32), 0.5, 1.5).astype(jnp.bfloat16)
    second_gain = jnp.clip(1.0 + 0.1 * jax.random.normal(key_of[6], (D,), jnp.float32), 0.5, 1.5).astype(jnp.bfloat16)
    expert_in = noise(key_of[7], (2 * EXPERTS, D, HALF), 4 ** -0.5, 3.0, ((0, 8),))
    expert_out = noise(key_of[8], (2 * EXPERTS, HALF, D), (max(1, EXP_HID // EXPERTS)) ** -0.5, 0.21875, ((0, 8),))
    return {"tokens": tokens, "cotangent": cotangent, "heads_in": heads_in, "heads_out": heads_out, "slot_router": slot_router, "first_gain": first_gain, "second_gain": second_gain, "expert_in": expert_in, "expert_out": expert_out}


@jax.custom_vjp
def low(v):
    return lax.optimization_barrier(v.astype(jnp.bfloat16)).astype(jnp.float32)

@jax.custom_vjp
def low_back(v):
    return v

def low_keep(v):
    return (low(v), None)

def low_pass(kept, grad):
    return (grad,)

def back_keep(v):
    return (v, None)

def back_low(kept, grad):
    return (low(grad),)
low.defvjp(low_keep, low_pass)
low_back.defvjp(back_keep, back_low)

def product(form, left, right):
    return jnp.einsum(form, left, right, precision=lax.Precision.HIGHEST)

def normalize(values, gain):
    center = values - lax.optimization_barrier(jnp.mean(values, axis=-1, keepdims=True))
    spread = lax.optimization_barrier(jnp.mean(center * center, axis=-1, keepdims=True))
    return center * lax.rsqrt(spread + 1e-06) * gain

def block(pictures, heads_in, heads_out, slot_router, first_gain, second_gain, expert_in, expert_out):
    count = pictures.shape[0]
    act_one = low(normalize(pictures, first_gain))
    joint = low_back(low(product('bnd,df->bnf', act_one, heads_in)))
    split = joint.reshape(count, SEQ, 3, HEADS, HEAD_DIM)
    scores = low_back(product('bqhe,bkhe->bhqk', split[:, :, 0], split[:, :, 1]) * HEAD_DIM ** (-0.5))
    probs = low(jax.nn.softmax(scores, axis=-1))
    mixed = product('bhqk,bkhe->bqhe', probs, split[:, :, 2]).reshape(count, SEQ, D)
    mixed = low_back(low(mixed))
    attended = low_back(product('bnd,de->bne', mixed, heads_out))
    resid = pictures + attended
    act_two = low(normalize(resid, second_gain))
    logits = low_back(product('bnd,de->bne', act_two, slot_router))
    dispatch = low(jax.nn.softmax(logits, axis=1))
    combine = low(jax.nn.softmax(logits, axis=2))
    slots = low_back(low(product('bne,bnd->bed', dispatch, act_two)))
    copies = jnp.stack([low_back(slots), low_back(slots)], axis=2)
    pre = low_back(product('bejd,ejdh->bejh', copies, expert_in.reshape(EXPERTS, 2, D, HALF)))
    hidden = low(jax.nn.gelu(pre, approximate=True))
    parts = low(product('bejh,ejhd->bejd', hidden, expert_out.reshape(EXPERTS, 2, HALF, D)))
    summed = low_back(low(lax.optimization_barrier(jnp.sum(parts, axis=2))))
    return resid + product('bne,bed->bnd', combine, summed)

def forward(tokens, heads_in, heads_out, slot_router, first_gain, second_gain, expert_in, expert_out):
    blocks = tokens.reshape(IMAGES // IMG_DEV, IMG_DEV, SEQ, D)

    def one_block(pictures):
        return block(pictures, heads_in, heads_out, slot_router, first_gain, second_gain, expert_in, expert_out)
    result = lax.map(jax.checkpoint(one_block), blocks)
    return result.reshape(IMAGES, SEQ, D)

def reference(tokens, cotangent, heads_in, heads_out, slot_router, first_gain, second_gain, expert_in, expert_out):
    floats = [a.astype(jnp.float32) for a in (tokens, heads_in, heads_out, slot_router, first_gain, second_gain, expert_in, expert_out)]
    result, pullback = jax.vjp(forward, *floats)
    grads = pullback(cotangent.astype(jnp.float32))
    return (result.astype(jnp.bfloat16), grads[0].astype(jnp.bfloat16), grads[1], grads[2], grads[3], grads[4], grads[5], grads[6], grads[7])
```

```python
import jax
import jax.numpy as jnp
from jax import lax
from jax.sharding import PartitionSpec as P

HEADS = 12


def swap(values, axis, size, bit):
    return lax.ppermute(values, axis, [(place, place ^ bit) for place in range(size)])


def bits_of(size):
    bit, bits = 1, []
    while bit < size:
        bits.append(bit)
        bit *= 2
    return bits


def reorder(blocks):
    size = blocks.shape[0]
    me = lax.axis_index("grp")
    for bit in bits_of(size):
        pairs = blocks.reshape((size // (2 * bit), 2, bit) + blocks.shape[1:])
        odd = (me & bit) > 0
        low, high = pairs[:, 0], pairs[:, 1]
        pairs = jnp.stack([jnp.where(odd, high, low), jnp.where(odd, low, high)], axis=1)
        blocks = pairs.reshape(blocks.shape)
    return blocks


def gather_part(values, bits, size):
    held = values[None]
    order = [0]
    for bit in bits:
        held = jnp.concatenate([held, swap(held, "grp", size, bit)])
        order = order + [place ^ bit for place in order]
    return held, order


def gather_rows(values, size):
    bits = bits_of(size)
    rows = values.shape[0]
    half = rows // 2
    first, order_a = gather_part(values[:half], bits[1:], size)
    second, order_b = gather_part(values[half:], bits[1:][::-1], size)
    first = jnp.stack([first[order_a.index(p)] for p in sorted(order_a)])
    second = jnp.stack([second[order_b.index(p)] for p in sorted(order_b)])
    both = jnp.concatenate([first, second], axis=1)
    other = swap(both, "grp", size, 1)
    return jnp.stack([both, other], axis=1).reshape(size, rows, -1)


def whole_rows(relative, size):
    return reorder(relative).reshape(-1, relative.shape[-1])


def halve(values, size, bits):
    for bit in bits:
        keep = [(p, v) for p, v in values if not p & bit]
        give = dict((p, v) for p, v in values if p & bit)
        sent = swap(jnp.stack([give[p | bit] for p, _ in keep]), "grp", size, bit)
        values = [(p, (v.astype(jnp.float32) + sent[i].astype(jnp.float32)).astype(jnp.bfloat16)) for i, (p, v) in enumerate(keep)]
    return values


def scatter_sum(relative, size):
    bits = bits_of(size)
    start = [(p, relative[p]) for p in range(size)]
    start = halve(start, size, [1])
    cut = relative.shape[-1] // 256 * 128
    first = halve([(p, v[:, :cut]) for p, v in start], size, bits[1:])
    second = halve([(p, v[:, cut:]) for p, v in start], size, bits[1:][::-1])
    return jnp.concatenate([first[0][1], second[0][1]], axis=-1)


def sum_rep(values, size):
    total = values
    for bit in ([1, 3] if size == 4 else bits_of(size)):
        total = (total.astype(jnp.float32) + swap(total, "rep", size, bit).astype(jnp.float32)).astype(jnp.bfloat16)
    return total


def mult(form, left, right):
    return jnp.einsum(form, left, right, preferred_element_type=jnp.float32)


def layer_stats(values):
    center = values - jnp.mean(values, axis=-1, keepdims=True)
    spread = jnp.mean(center * center, axis=-1, keepdims=True)
    factor = lax.rsqrt(spread + 1e-06)
    return (center * factor, factor)


def norm_back(grad_norm, gain, normed, factor):
    scaled = grad_norm * gain
    inner = (
        scaled
        - jnp.mean(scaled, axis=-1, keepdims=True)
        - normed * jnp.mean(scaled * normed, axis=-1, keepdims=True)
    )
    return (factor * inner, jnp.sum(grad_norm * normed, axis=(0, 1)))


def activate(values):
    return jax.nn.gelu(values, approximate=True)


def per_device(
    tokens,
    cotangent,
    heads_in,
    heads_out,
    slot_router,
    first_gain,
    second_gain,
    expert_in,
    expert_out,
):
    images, places, features = tokens.shape
    head_count = HEADS
    head_size = features // head_count
    scaling = head_size ** (-0.5)
    group = slot_router.shape[1] * 2
    small = jnp.concatenate([slot_router, first_gain[:, None], second_gain[:, None]], axis=1)
    small = jnp.pad(small, ((0, 0), (0, 128 - small.shape[1])))
    count_e = slot_router.shape[1]
    one = whole_rows(gather_rows(jnp.concatenate([heads_in, small], axis=1), group), group)
    full_out = whole_rows(gather_rows(heads_out, group), group)
    full_in, small = one[:, : heads_in.shape[1]], one[:, heads_in.shape[1] :]
    full_router, gain_a, gain_b = small[:, :count_e], small[:, count_e], small[:, count_e + 1]
    gain_one = gain_a.astype(jnp.float32)
    gain_two = gain_b.astype(jnp.float32)
    source = tokens.astype(jnp.float32)
    normed_one, factor_one = layer_stats(source)
    act_one = (normed_one * gain_one).astype(jnp.bfloat16)
    joint = mult("bnd,df->bnf", act_one, full_in).astype(jnp.bfloat16)
    split = joint.reshape(images, places, 3, head_count, head_size)
    query, keys, values = (split[:, :, 0], split[:, :, 1], split[:, :, 2])
    scores = mult("bqhe,bkhe->bhqk", query, keys) * scaling
    maximum = jnp.max(scores, axis=-1, keepdims=True)
    logsum = maximum + jnp.log(jnp.sum(jnp.exp(scores - maximum), axis=-1, keepdims=True))
    probs = jnp.exp(scores - logsum).astype(jnp.bfloat16)
    mixed = (
        mult("bhqk,bkhe->bqhe", probs, values)
        .reshape(images, places, features)
        .astype(jnp.bfloat16)
    )
    resid = source + mult("bnd,de->bne", mixed, full_out)
    normed_two, factor_two = layer_stats(resid)
    act_two = (normed_two * gain_two).astype(jnp.bfloat16)
    logits = mult("bnd,de->bne", act_two, full_router)
    dispatch = jax.nn.softmax(logits, axis=1)
    combine = jax.nn.softmax(logits, axis=2)
    disp_low = dispatch.astype(jnp.bfloat16)
    comb_low = combine.astype(jnp.bfloat16)
    slots = mult("bne,bnd->bed", disp_low, act_two).astype(jnp.bfloat16)
    grad_sum = mult("bne,bnd->bed", comb_low, cotangent).astype(jnp.bfloat16)
    packed = jnp.repeat(jnp.concatenate([slots, grad_sum], axis=2), 2, axis=1)
    received = lax.all_to_all(packed, "grp", split_axis=1, concat_axis=0, tiled=True)
    received = received.reshape(-1, 2 * features)
    piece_in = expert_in[0]
    piece_out = expert_out[0]
    rows, arriving = received[:, :features], received[:, features:]
    pre = jnp.dot(rows, piece_in, preferred_element_type=jnp.float32)
    hidden, gelu_back = jax.vjp(activate, pre)
    part = jnp.dot(hidden.astype(jnp.bfloat16), piece_out, preferred_element_type=jnp.float32).astype(jnp.bfloat16)
    grad_hidden = mult("rd,hd->rh", arriving, piece_out)
    grad_pre = gelu_back(grad_hidden)[0].astype(jnp.bfloat16)
    grad_rows = mult("rh,dh->rd", grad_pre, piece_in).astype(jnp.bfloat16)
    back = jnp.concatenate([part, grad_rows], axis=1).reshape(-1, 1, 2 * features)
    returned = lax.all_to_all(back, "grp", split_axis=0, concat_axis=1, tiled=True)
    summed = jnp.sum(
        returned.astype(jnp.float32).reshape(images, -1, 2, 2 * features), axis=2
    ).astype(jnp.bfloat16)
    expert_sum, grad_slots = summed[..., :features], summed[..., features:]
    every = lax.all_gather(received, "rep", axis=0, tiled=True)
    rows, arriving = every[:, :features], every[:, features:]
    pre = jnp.dot(rows, piece_in, preferred_element_type=jnp.float32)
    hidden, gelu_back = jax.vjp(activate, pre)
    grad_hidden = mult("rd,hd->rh", arriving, piece_out)
    grad_pre = gelu_back(grad_hidden)[0].astype(jnp.bfloat16)
    grad_piece_out = mult("rh,rd->hd", hidden.astype(jnp.bfloat16), arriving)
    grad_piece_in = mult("rd,rh->dh", rows, grad_pre)
    output = (resid + mult("bne,bed->bnd", comb_low, expert_sum)).astype(jnp.bfloat16)
    back_in, back_out, back_router = full_in, full_out, full_router
    grad_comb = mult("bnd,bed->bne", cotangent, expert_sum)
    expert_in_term = grad_piece_in[None]
    expert_out_term = grad_piece_out[None]
    grad_disp = mult("bnd,bed->bne", act_two, grad_slots)
    grad_act_two = mult("bne,bed->bnd", disp_low, grad_slots)
    grad_logits = combine * (grad_comb - jnp.sum(grad_comb * combine, axis=2, keepdims=True))
    grad_logits = grad_logits + dispatch * (
        grad_disp - jnp.sum(grad_disp * dispatch, axis=1, keepdims=True)
    )
    grad_logits = grad_logits.astype(jnp.bfloat16)
    grad_router = mult("bnd,bne->de", act_two, grad_logits)
    grad_act_two = grad_act_two + mult("bne,de->bnd", grad_logits, back_router)
    grad_resid_norm, grad_gain_two = norm_back(grad_act_two, gain_two, normed_two, factor_two)
    grad_resid = cotangent.astype(jnp.float32) + grad_resid_norm
    grad_att = grad_resid.astype(jnp.bfloat16)
    grad_heads_out = mult("bnd,bne->de", mixed, grad_att)
    grad_mixed = mult("bne,de->bnd", grad_att, back_out).astype(jnp.bfloat16)
    grad_mixed = grad_mixed.reshape(images, places, head_count, head_size)
    again_scores = mult("bqhe,bkhe->bhqk", query, keys) * scaling
    prob_full = jnp.exp(again_scores - logsum)
    grad_values = mult("bhqk,bqhe->bkhe", prob_full.astype(jnp.bfloat16), grad_mixed)
    grad_probs = mult("bqhe,bkhe->bhqk", grad_mixed, values)
    grad_scores = prob_full * (grad_probs - jnp.sum(prob_full * grad_probs, axis=-1, keepdims=True))
    grad_scores = grad_scores.astype(jnp.bfloat16)
    grad_query = mult("bhqk,bkhe->bqhe", grad_scores, keys) * scaling
    grad_keys = mult("bhqk,bqhe->bkhe", grad_scores, query) * scaling
    grad_joint = jnp.stack([grad_query, grad_keys, grad_values], axis=2).reshape(
        images, places, 3 * features
    )
    grad_joint = grad_joint.astype(jnp.bfloat16)
    grad_heads_in = mult("bnd,bnf->df", act_one, grad_joint)
    grad_act_one = mult("bnf,df->bnd", grad_joint, back_in)
    grad_source, grad_gain_one = norm_back(grad_act_one, gain_one, normed_one, factor_one)
    token_grad = (grad_resid + grad_source).astype(jnp.bfloat16)
    width = heads_in.shape[1]

    def lined(parts):
        joined = jnp.concatenate(parts, axis=1)
        spare = -joined.shape[1] % 128
        joined = jnp.pad(joined, ((0, 0), (0, spare))).astype(jnp.bfloat16)
        blocks = joined.reshape(group, -1, joined.shape[1])
        return reorder(blocks)

    reps = lax.axis_size("rep")
    early = lined([grad_heads_out, grad_router, grad_gain_two[:, None]])
    early = sum_rep(scatter_sum(early, group), reps).astype(jnp.float32)
    late = lined([grad_heads_in, grad_gain_one[:, None]])
    late = sum_rep(scatter_sum(late, group), reps).astype(jnp.float32)
    shares = (
        late[:, :width],
        early[:, :features],
        early[:, features : features + count_e],
        late[:, width],
        early[:, features + count_e],
    )
    expert_in_grad, expert_out_grad = expert_in_term, expert_out_term
    return (
        output,
        token_grad,
        shares[0],
        shares[1],
        shares[2],
        shares[3],
        shares[4],
        expert_in_grad,
        expert_out_grad,
    )


def solution(mesh):
    in_specs = (
        P(("rep", "grp"), None),
        P(("rep", "grp"), None),
        P("grp"),
        P("grp"),
        P("grp"),
        P("grp"),
        P("grp"),
        P("grp", None),
        P("grp", None),
    )
    out_specs = (
        P(("rep", "grp"), None),
        P(("rep", "grp"), None),
        P("grp"),
        P("grp"),
        P("grp"),
        P("grp"),
        P("grp"),
        P("grp", None),
        P("grp", None),
    )
    return jax.shard_map(
        per_device, mesh=mesh, in_specs=in_specs, out_specs=out_specs, check_vma=False
    )
```

```python
import functools

import jax
import jax.numpy as jnp
from jax import lax
from jax.experimental import pallas as pl
from jax.experimental.pallas import tpu as pltpu
from jax.sharding import PartitionSpec as P

HEADS = 12
LANES = 128
F32 = jnp.float32
BF16 = jnp.bfloat16
LOW = -1e30
VMEM_BYTES = 56 * 1024 * 1024

NN = (((1,), (0,)), ((), ()))
NT = (((1,), (1,)), ((), ()))
TN = (((0,), (0,)), ((), ()))


def dot(left, right, form=NN):
    return lax.dot_general(left, right, form, preferred_element_type=F32)


def swap(values, axis, size, bit):
    return lax.ppermute(values, axis, [(place, place ^ bit) for place in range(size)])


def bits_of(size):
    bit, bits = 1, []
    while bit < size:
        bits.append(bit)
        bit *= 2
    return bits


def flip_blocks(blocks, place):
    size = blocks.shape[0]
    for bit in bits_of(size):
        pairs = blocks.reshape((size // (2 * bit), 2, bit) + blocks.shape[1:])
        odd = (place & bit) > 0
        low, high = pairs[:, 0], pairs[:, 1]
        pairs = jnp.stack([jnp.where(odd, high, low), jnp.where(odd, low, high)], axis=1)
        blocks = pairs.reshape(blocks.shape)
    return blocks


def gather_part(values, bits, size):
    held = values[None]
    order = [0]
    for bit in bits:
        held = jnp.concatenate([held, swap(held, "grp", size, bit)])
        order = order + [place ^ bit for place in order]
    return jnp.stack([held[order.index(place)] for place in sorted(order)])


def gather_rows(values, size):
    bits = bits_of(size)
    rows = values.shape[0]
    half = rows // 2
    first = gather_part(values[:half], bits[1:], size)
    second = gather_part(values[half:], bits[1:][::-1], size)
    both = jnp.concatenate([first, second], axis=1)
    other = swap(both, "grp", size, 1)
    return jnp.stack([both, other], axis=1).reshape(size, rows, -1)


def add_low(left, right):
    return (left.astype(F32) + right.astype(F32)).astype(BF16)


def halve(values, size, bits):
    for bit in bits:
        keep = [(p, v) for p, v in values if not p & bit]
        give = dict((p, v) for p, v in values if p & bit)
        sent = swap(jnp.stack([give[p | bit] for p, _ in keep]), "grp", size, bit)
        values = [(p, add_low(v, sent[i])) for i, (p, v) in enumerate(keep)]
    return values


def scatter_sum(relative, size):
    bits = bits_of(size)
    start = halve([(p, relative[p]) for p in range(size)], size, [1])
    cut = relative.shape[-1] // 256 * 128
    first = halve([(p, v[:, :cut]) for p, v in start], size, bits[1:])
    second = halve([(p, v[:, cut:]) for p, v in start], size, bits[1:][::-1])
    return jnp.concatenate([first[0][1], second[0][1]], axis=-1)


def sum_rep(values, size):
    total = values
    for bit in [1, 3] if size == 4 else bits_of(size):
        total = add_low(total, swap(total, "rep", size, bit))
    return total


def iota(shape, axis):
    return lax.broadcasted_iota(jnp.int32, shape, axis)


def normalize(values):
    center = values - jnp.mean(values, axis=-1, keepdims=True)
    factor = lax.rsqrt(jnp.mean(center * center, axis=-1, keepdims=True) + 1e-06)
    return center * factor, factor


def norm_back(grad_norm, gain, normed, factor):
    scaled = grad_norm * gain
    inner = (
        scaled
        - jnp.mean(scaled, axis=-1, keepdims=True)
        - normed * jnp.mean(scaled * normed, axis=-1, keepdims=True)
    )
    return factor * inner


def place_rows(order_ref, source_ref, target_ref):
    rows = source_ref.shape[1]
    for k in range(source_ref.shape[0]):
        start = pl.multiple_of(order_ref[k] * rows, 32)
        target_ref[pl.ds(start, rows), :] = source_ref[k]


def attend_body(first, places, order_ref, source_ref, gain_ref, w_ref, *refs):
    if first:
        act_ref, joint_ref, prob_ref, mixed_ref, weight = refs
    else:
        joint_ref, prob_ref, mixed_ref, weight = refs

    @pl.when(pl.program_id(0) == 0)
    def _():
        place_rows(order_ref, w_ref, weight)

    if first:
        normed, _ = normalize(source_ref[0].astype(F32))
        act = (normed * gain_ref[...]).astype(BF16)
        act_ref[0] = act
    else:
        act = source_ref[0]
    joint = dot(act, weight[...]).astype(BF16)
    joint_ref[0] = joint
    tall = act.shape[0]
    third = joint.shape[1] // 3
    low = iota((tall, LANES), 1) < LANES // 2
    inside = iota((tall, LANES), 0) < places
    seen = iota((tall, tall), 1) < places
    for pair in range(third // LANES):
        query, keys, values = (
            joint[:, part * third + pair * LANES : part * third + (pair + 1) * LANES]
            for part in range(3)
        )
        query = query * 0.125
        outs = []
        for side in range(2):
            mine = low if side == 0 else ~low
            scores = dot(jnp.where(mine, query, 0), keys, NT)
            scores = jnp.where(seen, scores, LOW)
            power = jnp.exp(scores - jnp.max(scores, axis=1, keepdims=True))
            prob = (power * (1.0 / jnp.sum(power, axis=1, keepdims=True))).astype(BF16)
            prob_ref[0, 2 * pair + side] = prob
            outs.append(dot(prob, values))
        mixed = jnp.where(inside, jnp.where(low, outs[0], outs[1]), 0.0)
        mixed_ref[0, :, pair * LANES : (pair + 1) * LANES] = mixed.astype(BF16)


def spec_image(shape):
    count = len(shape)
    return pl.BlockSpec((1,) + shape[1:], lambda i: (i,) + (0,) * (count - 1))


def spec_whole(shape):
    count = len(shape)
    return pl.BlockSpec(shape, lambda i: (0,) * count)


SMEM = pl.BlockSpec(memory_space=pltpu.SMEM)


def params():
    return pltpu.CompilerParams(vmem_limit_bytes=VMEM_BYTES)


def cost(flops, data):
    return pl.CostEstimate(flops=int(flops), bytes_accessed=int(data), transcendentals=0)


def attend(first, places, order, source, gain, w):
    images, tall, features = source.shape
    width = w.shape[-1]
    heads = width // 3 // 64
    shapes = [
        ((images, tall, width), BF16),
        ((images, heads, tall, tall), BF16),
        ((images, tall, width // 3), BF16),
    ]
    if first:
        shapes = [((images, tall, features), BF16)] + shapes
    return pl.pallas_call(
        functools.partial(attend_body, first, places),
        grid=(images,),
        in_specs=[SMEM, spec_image(source.shape), spec_whole(gain.shape), spec_whole(w.shape)],
        out_specs=[spec_image(s) for s, _ in shapes],
        out_shape=[jax.ShapeDtypeStruct(s, t) for s, t in shapes],
        scratch_shapes=[pltpu.VMEM((features, width), BF16)],
        compiler_params=params(),
        cost_estimate=cost(2 * images * tall * features * width * 3, 8e6),
        name="attend",
    )(order, source, gain, w)


def softmaxes(logits, places, experts):
    rows = iota(logits.shape, 0) < places
    lanes = iota(logits.shape, 1) < experts
    tall = jnp.where(rows, logits, LOW)
    tall = jnp.exp(tall - jnp.max(tall, axis=0, keepdims=True))
    dispatch = tall / jnp.sum(tall, axis=0, keepdims=True)
    wide = jnp.where(lanes, logits, LOW)
    wide = jnp.exp(wide - jnp.max(wide, axis=1, keepdims=True))
    combine = wide / jnp.sum(wide, axis=1, keepdims=True)
    return dispatch, combine


def route_body(
    places, experts, order_ref, token_ref, cot_ref, m0, m1, m2, w_ref, gain_ref, router_ref,
    resid_ref, logit_ref, packed_ref, weight,
):
    @pl.when(pl.program_id(0) == 0)
    def _():
        place_rows(order_ref, w_ref, weight)

    resid = token_ref[0].astype(F32)
    part = m0.shape[-1]
    for c, mixed in enumerate((m0, m1, m2)):
        resid = resid + dot(mixed[0], weight[c * part : (c + 1) * part, :])
    resid_ref[0] = resid
    normed, _ = normalize(resid)
    act = (normed * gain_ref[...]).astype(BF16)
    logits = dot(act, router_ref[...])
    logit_ref[0] = logits
    dispatch, combine = softmaxes(logits, places, experts)
    features = act.shape[1]
    rows = packed_ref.shape[1]
    packed_ref[0, :, :features] = dot(dispatch.astype(BF16), act, TN)[:rows].astype(BF16)
    packed_ref[0, :, features:] = dot(combine.astype(BF16), cot_ref[0], TN)[:rows].astype(BF16)


def route(places, experts, slot_rows, order, tokens, cot, mixed, w, gain, router):
    images, tall, features = tokens.shape
    shapes = [
        ((images, tall, features), F32),
        ((images, tall, LANES), F32),
        ((images, slot_rows, 2 * features), BF16),
    ]
    return pl.pallas_call(
        functools.partial(route_body, places, experts),
        grid=(images,),
        in_specs=[SMEM, spec_image(tokens.shape), spec_image(cot.shape)]
        + [spec_image(m.shape) for m in mixed]
        + [spec_whole(w.shape), spec_whole(gain.shape), spec_whole(router.shape)],
        out_specs=[spec_image(s) for s, _ in shapes],
        out_shape=[jax.ShapeDtypeStruct(s, t) for s, t in shapes],
        scratch_shapes=[pltpu.VMEM((features, features), BF16)],
        compiler_params=params(),
        cost_estimate=cost(4 * images * tall * features * features, 8e6),
        name="route",
    )(order, tokens, cot, *mixed, w, gain, router)


def gelu_parts(values):
    scale, cubic = 0.7978845608028654, 0.044715
    square = values * values
    bent = jnp.tanh(scale * values * (1.0 + cubic * square))
    half = 0.5 * (1.0 + bent)
    slope = half + 0.5 * values * (1.0 - bent * bent) * scale * (1.0 + 3.0 * cubic * square)
    return values * half, slope


def expert_body(rows_ref, in_ref, out_ref, back_ref):
    features = in_ref.shape[0]
    rows, arriving = rows_ref[:, :features], rows_ref[:, features:]
    total = jnp.zeros((rows.shape[0], features), F32)
    grad_total = total
    step = 512
    for start in range(0, in_ref.shape[1], step):
        w_in = in_ref[:, start : start + step]
        w_out = out_ref[start : start + step, :]
        hidden, slope = gelu_parts(dot(rows, w_in))
        grad_pre = (dot(arriving, w_out, NT) * slope).astype(BF16)
        total = total + dot(hidden.astype(BF16), w_out)
        grad_total = grad_total + dot(grad_pre, w_in, NT)
    back_ref[:, :features] = total.astype(BF16)
    back_ref[:, features:] = grad_total.astype(BF16)


def expert(rows, piece_in, piece_out):
    return pl.pallas_call(
        expert_body,
        grid=(1,),
        in_specs=[spec_whole(rows.shape), spec_whole(piece_in.shape), spec_whole(piece_out.shape)],
        out_specs=spec_whole(rows.shape),
        out_shape=jax.ShapeDtypeStruct(rows.shape, BF16),
        compiler_params=params(),
        cost_estimate=cost(8 * 256 * piece_in.size, 5e6),
        name="expert",
    )(rows, piece_in, piece_out)


def expert_grad_body(rows_ref, in_ref, out_ref, grad_in_ref, grad_out_ref):
    features = in_ref.shape[0]
    rows, arriving = rows_ref[:, :features], rows_ref[:, features:]
    hidden, slope = gelu_parts(dot(rows, in_ref[...]))
    grad_pre = (dot(arriving, out_ref[...], NT) * slope).astype(BF16)
    grad_in_ref[...] = dot(rows, grad_pre, TN)
    grad_out_ref[...] = dot(hidden.astype(BF16), arriving, TN)


def expert_grad(rows, piece_in, piece_out):
    features, hidden = piece_in.shape
    step = 512
    wide = pl.BlockSpec((features, step), lambda i: (0, i))
    high = pl.BlockSpec((step, features), lambda i: (i, 0))
    return pl.pallas_call(
        expert_grad_body,
        grid=(hidden // step,),
        in_specs=[spec_whole(rows.shape), wide, high],
        out_specs=[wide, high],
        out_shape=[
            jax.ShapeDtypeStruct(piece_in.shape, F32),
            jax.ShapeDtypeStruct(piece_out.shape, F32),
        ],
        compiler_params=params(),
        cost_estimate=cost(8 * rows.shape[0] * piece_in.size, 14e6),
        name="expert_grad",
    )(rows, piece_in, piece_out)


def back_body(
    places, experts, order_ref, resid_ref, logit_ref, cot_ref, m0, m1, m2, summed_ref, w_ref, gain_ref,
    router_ref, output_ref, att_ref, grad_mixed_ref, grad_w_ref, weight, slots, total, side, gain_sum,
):
    step = pl.program_id(0)
    features = gain_ref.shape[1]

    @pl.when(step == 0)
    def _():
        place_rows(order_ref, w_ref, weight)
        slots[...] = jnp.zeros_like(slots)
        total[...] = jnp.zeros_like(total)
        side[...] = jnp.zeros_like(side)
        gain_sum[...] = jnp.zeros_like(gain_sum)

    rows = summed_ref.shape[1]
    slots[:rows, :] = summed_ref[0]
    expert_sum, grad_slots = slots[:, :features], slots[:, features:]
    resid = resid_ref[0]
    cot = cot_ref[0]
    gain = gain_ref[...]
    router = router_ref[...]
    dispatch, combine = softmaxes(logit_ref[0], places, experts)
    output = resid + dot(combine.astype(BF16), expert_sum)
    output_ref[0] = output[:places].astype(BF16)
    normed, factor = normalize(resid)
    act = (normed * gain).astype(BF16)
    grad_comb = dot(cot, expert_sum, NT)
    grad_disp = dot(act, grad_slots, NT)
    grad_logits = combine * (grad_comb - jnp.sum(grad_comb * combine, axis=1, keepdims=True))
    grad_logits = grad_logits + dispatch * (
        grad_disp - jnp.sum(grad_disp * dispatch, axis=0, keepdims=True)
    )
    grad_logits = grad_logits.astype(BF16)
    grad_act = dot(dispatch.astype(BF16), grad_slots) + dot(grad_logits, router, NT)
    side[...] += dot(act, grad_logits, TN)
    gain_sum[...] += jnp.sum(grad_act * normed, axis=0, keepdims=True)
    att = (cot.astype(F32) + norm_back(grad_act, gain, normed, factor)).astype(BF16)
    att_ref[0] = att
    grad_mixed_ref[0] = dot(att, weight[...], NT).astype(BF16)
    part = m0.shape[-1]
    for c, mixed in enumerate((m0, m1, m2)):
        total[c * part : (c + 1) * part, :] += dot(mixed[0], att, TN)

    @pl.when(step == pl.num_programs(0) - 1)
    def _():
        turned = jnp.broadcast_to(gain_sum[...], (LANES, features)).T
        lane = iota((features, LANES), 1)
        slot = iota((LANES, LANES), 0)
        slot = jnp.where(slot < experts, slot ^ order_ref[grad_w_ref.shape[0]], slot)
        swapped = jnp.where(slot == iota((LANES, LANES), 1), 1.0, 0.0).astype(BF16)
        side[...] = jnp.where(lane == experts, turned, dot(side[...].astype(BF16), swapped))
        block = grad_w_ref.shape[1]
        for k in range(grad_w_ref.shape[0]):
            start = pl.multiple_of(order_ref[k] * block, 32)
            grad_w_ref[k, :, :features] = total[pl.ds(start, block), :].astype(BF16)
            grad_w_ref[k, :, features:] = side[pl.ds(start, block), :].astype(BF16)


def back(places, experts, order, resid, logits, cot, mixed, summed, w, gain, router):
    images, tall, features = resid.shape
    shapes = [
        ((images, places, features), BF16),
        ((images, tall, features), BF16),
        ((images, tall, features), BF16),
    ]
    grad_w = (w.shape[0], w.shape[1], features + LANES)
    return pl.pallas_call(
        functools.partial(back_body, places, experts),
        grid=(images,),
        in_specs=[SMEM, spec_image(resid.shape), spec_image(logits.shape), spec_image(cot.shape)]
        + [spec_image(m.shape) for m in mixed]
        + [spec_image(summed.shape)]
        + [spec_whole(w.shape), spec_whole(gain.shape), spec_whole(router.shape)],
        out_specs=[spec_image(s) for s, _ in shapes] + [spec_whole(grad_w)],
        out_shape=[jax.ShapeDtypeStruct(s, t) for s, t in shapes]
        + [jax.ShapeDtypeStruct(grad_w, BF16)],
        scratch_shapes=[
            pltpu.VMEM((features, features), BF16),
            pltpu.VMEM((LANES, 2 * features), BF16),
            pltpu.VMEM((features, features), F32),
            pltpu.VMEM((features, LANES), F32),
            pltpu.VMEM((1, features), F32),
        ],
        compiler_params=params(),
        cost_estimate=cost(8 * images * tall * features * features, 16e6),
        name="back",
    )(order, resid, logits, cot, *mixed, summed, w, gain, router)


def attend_back_body(order_ref, joint_ref, prob_ref, grad_ref, mixed_ref, act_ref, out_ref, grad_w_ref, total):
    step = pl.program_id(0)

    @pl.when(step == 0)
    def _():
        total[...] = jnp.zeros_like(total)

    tall, width = joint_ref.shape[1:]
    third = width // 3
    low = iota((tall, LANES), 1) < LANES // 2
    for pair in range(third // LANES):
        query, keys, values = (
            joint_ref[0, :, part * third + pair * LANES : part * third + (pair + 1) * LANES]
            for part in range(3)
        )
        grad = grad_ref[0, :, pair * LANES : (pair + 1) * LANES]
        product = grad.astype(F32) * mixed_ref[0, :, pair * LANES : (pair + 1) * LANES].astype(F32)
        grads = []
        for side in range(2):
            mine = low if side == 0 else ~low
            prob = prob_ref[0, 2 * pair + side]
            inner = jnp.sum(jnp.where(mine, product, 0.0), axis=1, keepdims=True)
            grad_prob = dot(jnp.where(mine, grad, 0), values, NT)
            grad_scores = (prob.astype(F32) * (grad_prob - inner) * 0.125).astype(BF16)
            grads.append(
                (dot(grad_scores, keys), dot(grad_scores, query, TN), dot(prob, grad, TN))
            )
        for part in range(3):
            joined = jnp.where(low, grads[0][part], grads[1][part]).astype(BF16)
            out_ref[0, :, part * third + pair * LANES : part * third + (pair + 1) * LANES] = joined
    total[...] += dot(act_ref[0], out_ref[0], TN)

    @pl.when(step == pl.num_programs(0) - 1)
    def _():
        block = grad_w_ref.shape[1]
        for k in range(grad_w_ref.shape[0]):
            start = pl.multiple_of(order_ref[k] * block, 32)
            grad_w_ref[k] = total[pl.ds(start, block), :].astype(BF16)


def attend_back(blocks, chunk, order, joint, prob, grad_mixed, mixed, act):
    images, tall, width = joint.shape
    features = act.shape[-1]
    third = width // 3
    grad_w = (blocks, features // blocks, width)
    return pl.pallas_call(
        attend_back_body,
        grid=(images,),
        in_specs=[
            SMEM,
            spec_image(joint.shape),
            spec_image(prob.shape),
            pl.BlockSpec((1, tall, third), lambda i: (i, 0, chunk)),
            spec_image(mixed.shape),
            spec_image(act.shape),
        ],
        out_specs=[spec_image(joint.shape), spec_whole(grad_w)],
        out_shape=[
            jax.ShapeDtypeStruct(joint.shape, BF16),
            jax.ShapeDtypeStruct(grad_w, BF16),
        ],
        scratch_shapes=[pltpu.VMEM((features, width), F32)],
        compiler_params=params(),
        cost_estimate=cost(2 * images * tall * features * width * 5, 16e6),
        name="attend_back",
    )(order, joint, prob, grad_mixed, mixed, act)


def finish_body(places, order_ref, token_ref, att_ref, j0, j1, j2, w0, w1, w2, gain_ref, out_ref, s0, s1, s2):
    @pl.when(pl.program_id(0) == 0)
    def _():
        for source, target in ((w0, s0), (w1, s1), (w2, s2)):
            place_rows(order_ref, source, target)

    grad_act = dot(j0[0], s0[...], NT) + dot(j1[0], s1[...], NT) + dot(j2[0], s2[...], NT)
    normed, factor = normalize(token_ref[0].astype(F32))
    result = att_ref[0].astype(F32) + norm_back(grad_act, gain_ref[...], normed, factor)
    out_ref[0] = result[:places].astype(BF16)


def finish(places, order, tokens, att, joints, weights, gain):
    images, tall, features = tokens.shape
    shape = (images, places, features)
    return pl.pallas_call(
        functools.partial(finish_body, places),
        grid=(images,),
        in_specs=[SMEM, spec_image(tokens.shape), spec_image(att.shape)]
        + [spec_image(j.shape) for j in joints]
        + [spec_whole(w.shape) for w in weights]
        + [spec_whole(gain.shape)],
        out_specs=spec_image(shape),
        out_shape=jax.ShapeDtypeStruct(shape, BF16),
        scratch_shapes=[pltpu.VMEM((features, w.shape[-1]), BF16) for w in weights],
        compiler_params=params(),
        cost_estimate=cost(6 * images * tall * features * features, 12e6),
        name="finish",
    )(order, tokens, att, *joints, *weights, gain)


def per_device(
    tokens, cotangent, heads_in, heads_out, slot_router, first_gain, second_gain, expert_in, expert_out
):
    images, places, features = tokens.shape
    experts = slot_router.shape[1]
    group = lax.axis_size("grp")
    reps = lax.axis_size("rep")
    me = lax.axis_index("grp")
    own_rows = heads_in.shape[0]
    direct = own_rows % 32 == 0
    blocks = group if direct else 8
    order = jnp.arange(blocks, dtype=jnp.int32)
    if direct:
        order = order ^ me
    chip = me // 2
    order = jnp.concatenate([order, chip[None]])
    tall = -(-places // 16) * 16
    slot_rows = -(-experts // 16) * 16
    chunks = 3
    part = features // chunks

    def gathered(values):
        relative = gather_rows(values, group)
        if direct:
            return relative
        return flip_blocks(relative, me).reshape(blocks, features // blocks, -1)

    def scattered(placed):
        if not direct:
            placed = flip_blocks(placed.reshape(group, own_rows, -1), me)
        return sum_rep(scatter_sum(placed, group), reps)

    def in_order(relative):
        if direct:
            relative = flip_blocks(relative, me)
        return relative.reshape(features, -1)

    small = jnp.concatenate([slot_router, first_gain[:, None], second_gain[:, None]], axis=1)
    small = jnp.pad(small, ((0, 0), (0, LANES - small.shape[1])))
    columns = heads_in.reshape(own_rows, 3, chunks, part)
    pieces = [columns[:, :, c].reshape(own_rows, 3 * part) for c in range(chunks)]
    start = gathered(jnp.concatenate([pieces[0], small], axis=1))
    rest = gathered(jnp.concatenate(pieces[1:] + [heads_out], axis=1))
    wide = 3 * part
    weights = [start[..., :wide], rest[..., :wide], rest[..., wide : 2 * wide]]
    full_out = rest[..., 2 * wide :]
    small = in_order(start[..., wide:])
    gain_one = small[:, experts].astype(F32)[None]
    gain_two = small[:, experts + 1].astype(F32)[None]
    router = flip_blocks(small[:, :experts].T, chip).T
    router = jnp.pad(router, ((0, 0), (0, LANES - experts)))

    grow = ((0, 0), (0, tall - places), (0, 0))
    source = jnp.pad(tokens, grow)
    cot = jnp.pad(cotangent, grow)

    act, joint, prob, mixed = attend(True, places, order, source, gain_one, weights[0])
    joints, probs, mixes = [joint], [prob], [mixed]
    for c in range(1, chunks):
        joint, prob, mixed = attend(False, places, order, act, gain_one, weights[c])
        joints.append(joint)
        probs.append(prob)
        mixes.append(mixed)
    resid, logits, packed = route(
        places, experts, slot_rows, order, source, cot, mixes, full_out, gain_two, router
    )

    leaving = packed[:, :experts].transpose(1, 0, 2)
    arrived = jnp.stack(
        [leaving[0]] + [swap(leaving[k], "grp", group, 2 * k) for k in range(1, experts)]
    )
    arrived = jnp.stack([arrived, swap(arrived, "grp", group, 1)])
    received = arrived.reshape(2 * experts * images, 2 * features)
    piece_in, piece_out = expert_in[0], expert_out[0]
    result = expert(received, piece_in, piece_out).reshape(2, experts, images, 2 * features)
    both = add_low(result[0], swap(result[1], "grp", group, 1))
    summed = jnp.stack(
        [both[0]] + [swap(both[k], "grp", group, 2 * k) for k in range(1, experts)], axis=1
    )
    summed = jnp.pad(summed, ((0, 0), (0, slot_rows - experts), (0, 0)))

    every = jnp.concatenate(
        [received]
        + [
            lax.ppermute(received, "rep", [(i, (i + k) % reps) for i in range(reps)])
            for k in range(1, reps)
        ]
    )

    output, att, grad_mixed, grad_out = back(
        places, experts, order, resid, logits, cot, mixes, summed, full_out, gain_two, router
    )
    early = scattered(grad_out).astype(F32)
    grad_joints, shares = [], []
    for c in range(chunks):
        grad_joint, grad_w = attend_back(
            blocks, c, order, joints[c], probs[c], grad_mixed, mixes[c], act
        )
        grad_joints.append(grad_joint)
        shares.append(scattered(grad_w).astype(F32))
    expert_in_grad, expert_out_grad = expert_grad(every, piece_in, piece_out)
    token_grad = finish(places, order, source, att, grad_joints, weights, gain_one)

    late = jnp.stack([share.reshape(own_rows, 3, part) for share in shares], axis=2)
    late = late.reshape(own_rows, 3 * features)
    gain_one_grad = jnp.sum(late * heads_in.astype(F32), axis=1) / first_gain.astype(F32)
    return (
        output,
        token_grad,
        late,
        early[:, :features],
        early[:, features : features + experts],
        gain_one_grad,
        early[:, features + experts],
        expert_in_grad[None],
        expert_out_grad[None],
    )


def solution(mesh):
    token_spec = P(("rep", "grp"), None, None)
    matrix, vector, stack = P("grp", None), P("grp"), P("grp", None, None)
    return jax.shard_map(
        per_device,
        mesh=mesh,
        in_specs=(token_spec, token_spec, matrix, matrix, matrix, vector, vector, stack, stack),
        out_specs=(token_spec, token_spec, matrix, matrix, matrix, vector, vector, stack, stack),
        check_vma=False,
    )
```

```python
import functools

import jax
import jax.numpy as jnp
from jax import lax
from jax.experimental import pallas as pl
from jax.experimental.pallas import tpu as pltpu
from jax.sharding import PartitionSpec as P

HEADS = 12
LANES = 128
F32 = jnp.float32
BF16 = jnp.bfloat16
LOW = -1e30
VMEM_BYTES = 56 * 1024 * 1024

NN = (((1,), (0,)), ((), ()))
NT = (((1,), (1,)), ((), ()))
TN = (((0,), (0,)), ((), ()))


def dot(left, right, form=NN):
    return lax.dot_general(left, right, form, preferred_element_type=F32)


def swap(values, axis, size, bit):
    return lax.ppermute(values, axis, [(place, place ^ bit) for place in range(size)])


def bits_of(size):
    bit, bits = 1, []
    while bit < size:
        bits.append(bit)
        bit *= 2
    return bits


def flip_blocks(blocks, place):
    size = blocks.shape[0]
    for bit in bits_of(size):
        pairs = blocks.reshape((size // (2 * bit), 2, bit) + blocks.shape[1:])
        odd = (place & bit) > 0
        low, high = pairs[:, 0], pairs[:, 1]
        pairs = jnp.stack([jnp.where(odd, high, low), jnp.where(odd, low, high)], axis=1)
        blocks = pairs.reshape(blocks.shape)
    return blocks


def after(values, *others):
    return lax.optimization_barrier((values, others))[0]


def gather_stage(held, size, bit):
    return jnp.concatenate([held, swap(held, "grp", size, bit)])


def join_halves(first, second):
    second = jnp.stack([second[0], second[2], second[1], second[3]])
    return jnp.concatenate([first, second], axis=1)


def add_low(*terms):
    return sum(term.astype(F32) for term in terms).astype(BF16)


def spread_sum(keep, give):
    got = swap(give, "grp", 8, 1)
    sums = [add_low(keep[k], got[k]) for k in range(4)]
    return sums[0], [swap(sums[k], "grp", 8, 2 * k) for k in range(1, 4)], sums


def iota(shape, axis):
    return lax.broadcasted_iota(jnp.int32, shape, axis)


def normalize(values):
    center = values - jnp.mean(values, axis=-1, keepdims=True)
    factor = lax.rsqrt(jnp.mean(center * center, axis=-1, keepdims=True) + 1e-06)
    return center * factor, factor


def norm_back(scaled, normed, factor):
    inner = (
        scaled
        - jnp.mean(scaled, axis=-1, keepdims=True)
        - normed * jnp.mean(scaled * normed, axis=-1, keepdims=True)
    )
    return factor * inner


def place_rows(order_ref, source_ref, target_ref):
    blocks = source_ref.shape[0]
    rows = target_ref.shape[0] // blocks
    for k in range(blocks):
        start = pl.multiple_of(order_ref[k] * rows, 32)
        target_ref[pl.ds(start, rows), :] = source_ref[k, :rows]


def store_blocks(order_ref, source, keep_ref, give_ref, columns):
    half, rows = keep_ref.shape[:2]
    for k in range(2 * half):
        start = pl.multiple_of(order_ref[2 * half + k] * rows, 32)
        target = keep_ref if k < half else give_ref
        target[k % half, :, columns] = source[pl.ds(start, rows), :].astype(BF16)


def gather_small(order_ref, w_ref, rows, small_ref):
    blocks, high, _ = w_ref.shape
    block = small_ref.shape[1] // blocks
    total = jnp.zeros(small_ref.shape, F32)
    lane = iota((LANES, small_ref.shape[1]), 0)
    place = iota((LANES, small_ref.shape[1]), 1)
    for k in range(blocks):
        fits = (place == order_ref[k] * block + lane) & (lane < block)
        total = total + dot(w_ref[k, rows:high, :LANES], jnp.where(fits, 1.0, 0.0).astype(BF16))
    small_ref[...] = total


def attend_body(first, places, order_ref, source_ref, w_ref, *refs):
    if first:
        act_ref, small_ref, joint_ref, prob_ref, mixed_ref, weight = refs
    else:
        joint_ref, prob_ref, mixed_ref, weight = refs

    @pl.when(pl.program_id(0) == 0)
    def _():
        place_rows(order_ref, w_ref, weight)
        if first:
            gather_small(order_ref, w_ref, weight.shape[0] // w_ref.shape[0], small_ref)

    if first:
        normed, _ = normalize(source_ref[0].astype(F32))
        act = (normed * small_ref[0:1, :]).astype(BF16)
        act_ref[0] = act
    else:
        act = source_ref[0]
    joint = dot(act, weight[...]).astype(BF16)
    joint_ref[0] = joint
    tall = act.shape[0]
    third = joint.shape[1] // 3
    low = iota((tall, LANES), 1) < LANES // 2
    inside = iota((tall, LANES), 0) < places
    seen = iota((tall, tall), 1) < places
    for pair in range(third // LANES):
        query, keys, values = (
            joint[:, part * third + pair * LANES : part * third + (pair + 1) * LANES]
            for part in range(3)
        )
        query = query * 0.125
        outs = []
        for side in range(2):
            mine = low if side == 0 else ~low
            scores = dot(jnp.where(mine, query, 0), keys, NT)
            scores = jnp.where(seen, scores, LOW)
            power = jnp.exp(scores - jnp.max(scores, axis=1, keepdims=True))
            prob = (power * (1.0 / jnp.sum(power, axis=1, keepdims=True))).astype(BF16)
            prob_ref[0, 2 * pair + side] = prob
            outs.append(dot(prob, values))
        mixed = jnp.where(inside, jnp.where(low, outs[0], outs[1]), 0.0)
        mixed_ref[0, :, pair * LANES : (pair + 1) * LANES] = mixed.astype(BF16)


def spec_image(shape):
    count = len(shape)
    return pl.BlockSpec((1,) + shape[1:], lambda i: (i,) + (0,) * (count - 1))


def spec_whole(shape):
    count = len(shape)
    return pl.BlockSpec(shape, lambda i: (0,) * count)


SMEM = pl.BlockSpec(memory_space=pltpu.SMEM)


def params():
    return pltpu.CompilerParams(vmem_limit_bytes=VMEM_BYTES)


def cost(flops, data):
    return pl.CostEstimate(flops=int(flops), bytes_accessed=int(data), transcendentals=0)


def attend(first, places, order, source, w, columns):
    images, tall, features = source.shape
    width, start = columns
    heads = width // 3 // 64
    shapes = [
        ((images, tall, width), BF16),
        ((images, heads, tall, tall), BF16),
        ((images, tall, width // 3), BF16),
    ]
    specs = [spec_image(s) for s, _ in shapes]
    if first:
        small = (w.shape[1] - features // w.shape[0], features)
        specs = [spec_image(source.shape), spec_whole(small)] + specs
        shapes = [((images, tall, features), BF16), (small, F32)] + shapes
    return pl.pallas_call(
        functools.partial(attend_body, first, places),
        grid=(images,),
        in_specs=[
            SMEM,
            spec_image(source.shape),
            pl.BlockSpec(w.shape[:2] + (width,), lambda i: (0, 0, start)),
        ],
        out_specs=specs,
        out_shape=[jax.ShapeDtypeStruct(s, t) for s, t in shapes],
        scratch_shapes=[pltpu.VMEM((features, width), BF16)],
        compiler_params=params(),
        cost_estimate=cost(2 * images * tall * features * width * 3, 8e6),
        name="attend",
    )(order, source, w)


def spread_router(experts, order_ref, small_ref, router):
    rows = small_ref.shape[0]
    slot, row = iota((LANES, rows), 0), iota((LANES, rows), 1)
    chip = order_ref[order_ref.shape[0] - 1]
    fits = (row == (slot ^ chip) + 2) & (slot < experts)
    router[...] = dot(jnp.where(fits, 1.0, 0.0).astype(BF16), small_ref[...].astype(BF16)).astype(BF16)


def softmaxes(logits, places, experts):
    rows = iota(logits.shape, 0) < places
    lanes = iota(logits.shape, 1) < experts
    tall = jnp.where(rows, logits, LOW)
    tall = jnp.exp(tall - jnp.max(tall, axis=0, keepdims=True))
    dispatch = tall / jnp.sum(tall, axis=0, keepdims=True)
    wide = jnp.where(lanes, logits, LOW)
    wide = jnp.exp(wide - jnp.max(wide, axis=1, keepdims=True))
    combine = wide / jnp.sum(wide, axis=1, keepdims=True)
    return dispatch, combine


def route_body(
    places, experts, order_ref, token_ref, cot_ref, m0, m1, w_ref, small_ref,
    resid_ref, logit_ref, packed_ref, weight, router,
):
    @pl.when(pl.program_id(0) == 0)
    def _():
        place_rows(order_ref, w_ref, weight)
        spread_router(experts, order_ref, small_ref, router)

    resid = token_ref[0].astype(F32)
    part = m0.shape[-1]
    resid = resid + dot(m0[0], weight[:part, :]) + dot(m1[0], weight[part:, :])
    resid_ref[0] = resid
    normed, _ = normalize(resid)
    act = (normed * small_ref[1:2, :]).astype(BF16)
    logits = dot(act, router[...], NT)
    logit_ref[0] = logits
    dispatch, combine = softmaxes(logits, places, experts)
    features = act.shape[1]
    rows = packed_ref.shape[1]
    packed_ref[0, :, :features] = dot(dispatch.astype(BF16), act, TN)[:rows].astype(BF16)
    packed_ref[0, :, features:] = dot(combine.astype(BF16), cot_ref[0], TN)[:rows].astype(BF16)


def w_out_spec(w):
    features = w.shape[2] // 3
    return pl.BlockSpec(w.shape[:2] + (features,), lambda i: (0, 0, 2))


def route(places, experts, slot_rows, order, tokens, cot, mixed, w, small):
    images, tall, features = tokens.shape
    shapes = [
        ((images, tall, features), F32),
        ((images, tall, LANES), F32),
        ((images, slot_rows, 2 * features), BF16),
    ]
    return pl.pallas_call(
        functools.partial(route_body, places, experts),
        grid=(images,),
        in_specs=[SMEM, spec_image(tokens.shape), spec_image(cot.shape)]
        + [spec_image(m.shape) for m in mixed]
        + [w_out_spec(w), spec_whole(small.shape)],
        out_specs=[spec_image(s) for s, _ in shapes],
        out_shape=[jax.ShapeDtypeStruct(s, t) for s, t in shapes],
        scratch_shapes=[pltpu.VMEM((features, features), BF16), pltpu.VMEM((LANES, features), BF16)],
        compiler_params=params(),
        cost_estimate=cost(4 * images * tall * features * features, 8e6),
        name="route",
    )(order, tokens, cot, *mixed, w, small)


def gelu_parts(values):
    scale, cubic = 0.7978845608028654, 0.044715
    square = values * values
    bent = jnp.tanh(scale * values * (1.0 + cubic * square))
    half = 0.5 * (1.0 + bent)
    slope = half + 0.5 * values * (1.0 - bent * bent) * scale * (1.0 + 3.0 * cubic * square)
    return values * half, slope


def expert_body(rows_ref, in_ref, out_ref, back_ref):
    features = in_ref.shape[0]
    rows, arriving = rows_ref[:, :features], rows_ref[:, features:]
    total = jnp.zeros((rows.shape[0], features), F32)
    grad_total = total
    step = 512
    for start in range(0, in_ref.shape[1], step):
        w_in = in_ref[:, start : start + step]
        w_out = out_ref[start : start + step, :]
        hidden, slope = gelu_parts(dot(rows, w_in))
        grad_pre = (dot(arriving, w_out, NT) * slope).astype(BF16)
        total = total + dot(hidden.astype(BF16), w_out)
        grad_total = grad_total + dot(grad_pre, w_in, NT)
    back_ref[:, :features] = total.astype(BF16)
    back_ref[:, features:] = grad_total.astype(BF16)


def expert(rows, piece_in, piece_out):
    return pl.pallas_call(
        expert_body,
        grid=(1,),
        in_specs=[spec_whole(rows.shape), spec_whole(piece_in.shape), spec_whole(piece_out.shape)],
        out_specs=spec_whole(rows.shape),
        out_shape=jax.ShapeDtypeStruct(rows.shape, BF16),
        compiler_params=params(),
        cost_estimate=cost(8 * 256 * piece_in.size, 5e6),
        name="expert",
    )(rows, piece_in, piece_out)


def expert_grad_body(rows_ref, in_ref, out_ref, grad_in_ref, grad_out_ref):
    features = in_ref.shape[0]
    rows, arriving = rows_ref[:, :features], rows_ref[:, features:]
    hidden, slope = gelu_parts(dot(rows, in_ref[...]))
    grad_pre = (dot(arriving, out_ref[...], NT) * slope).astype(BF16)
    grad_in_ref[...] = dot(rows, grad_pre, TN)
    grad_out_ref[...] = dot(hidden.astype(BF16), arriving, TN)


def expert_grad(rows, piece_in, piece_out):
    features, hidden = piece_in.shape
    step = 512
    wide = pl.BlockSpec((features, step), lambda i: (0, i))
    high = pl.BlockSpec((step, features), lambda i: (i, 0))
    return pl.pallas_call(
        expert_grad_body,
        grid=(hidden // step,),
        in_specs=[spec_whole(rows.shape), wide, high],
        out_specs=[wide, high],
        out_shape=[
            jax.ShapeDtypeStruct(piece_in.shape, F32),
            jax.ShapeDtypeStruct(piece_out.shape, F32),
        ],
        compiler_params=params(),
        cost_estimate=cost(8 * rows.shape[0] * piece_in.size, 14e6),
        name="expert_grad",
    )(rows, piece_in, piece_out)


def back_body(
    places, experts, order_ref, resid_ref, logit_ref, cot_ref, m0, m1, summed_ref, w_ref, small_ref,
    output_ref, att_ref, grad_mixed_ref, grad_w_ref, grad_side_ref, weight, router_rows, slots, total, side, gain_sum,
):
    step = pl.program_id(0)
    features = small_ref.shape[1]

    @pl.when(step == 0)
    def _():
        place_rows(order_ref, w_ref, weight)
        spread_router(experts, order_ref, small_ref, router_rows)
        slots[...] = jnp.zeros_like(slots)
        total[...] = jnp.zeros_like(total)
        side[...] = jnp.zeros_like(side)
        gain_sum[...] = jnp.zeros_like(gain_sum)

    rows = summed_ref.shape[1]
    slots[:rows, :] = summed_ref[0]
    expert_sum, grad_slots = slots[:, :features], slots[:, features:]
    resid = resid_ref[0]
    cot = cot_ref[0]
    gain = small_ref[1:2, :]
    dispatch, combine = softmaxes(logit_ref[0], places, experts)
    output = resid + dot(combine.astype(BF16), expert_sum)
    output_ref[0] = output[:places].astype(BF16)
    normed, factor = normalize(resid)
    act = (normed * gain).astype(BF16)
    grad_comb = dot(cot, expert_sum, NT)
    grad_disp = dot(act, grad_slots, NT)
    grad_logits = combine * (grad_comb - jnp.sum(grad_comb * combine, axis=1, keepdims=True))
    grad_logits = grad_logits + dispatch * (
        grad_disp - jnp.sum(grad_disp * dispatch, axis=0, keepdims=True)
    )
    grad_logits = grad_logits.astype(BF16)
    grad_act = dot(dispatch.astype(BF16), grad_slots) + dot(grad_logits, router_rows[...])
    side[...] += dot(act, grad_logits, TN)
    gain_sum[...] += jnp.sum(grad_act * normed, axis=0, keepdims=True)
    att = (cot.astype(F32) + norm_back(grad_act * gain, normed, factor)).astype(BF16)
    att_ref[0] = att
    grad_mixed_ref[0] = dot(att, weight[...], NT).astype(BF16)
    part = m0.shape[-1]
    total[:part, :] += dot(m0[0], att, TN)
    total[part:, :] += dot(m1[0], att, TN)

    @pl.when(step == pl.num_programs(0) - 1)
    def _():
        turned = jnp.broadcast_to(gain_sum[...], (LANES, features)).T
        lane = iota((features, LANES), 1)
        slot = iota((LANES, LANES), 0)
        slot = jnp.where(slot < experts, slot ^ order_ref[order_ref.shape[0] - 1], slot)
        swapped = jnp.where(slot == iota((LANES, LANES), 1), 1.0, 0.0).astype(BF16)
        side[...] = jnp.where(lane == experts, turned, dot(side[...].astype(BF16), swapped))
        grad_w_ref[...] = total[...].astype(BF16)
        grad_side_ref[...] = side[...].astype(BF16)


def back(places, experts, order, resid, logits, cot, mixed, summed, w, small):
    images, tall, features = resid.shape
    shapes = [
        ((images, places, features), BF16),
        ((images, tall, features), BF16),
        ((images, tall, features), BF16),
    ]
    grads = [(features, features), (features, LANES)]
    return pl.pallas_call(
        functools.partial(back_body, places, experts),
        grid=(images,),
        in_specs=[SMEM, spec_image(resid.shape), spec_image(logits.shape), spec_image(cot.shape)]
        + [spec_image(m.shape) for m in mixed]
        + [spec_image(summed.shape)]
        + [w_out_spec(w), spec_whole(small.shape)],
        out_specs=[spec_image(s) for s, _ in shapes] + [spec_whole(s) for s in grads],
        out_shape=[jax.ShapeDtypeStruct(s, t) for s, t in shapes]
        + [jax.ShapeDtypeStruct(s, BF16) for s in grads],
        scratch_shapes=[
            pltpu.VMEM((features, features), BF16),
            pltpu.VMEM((LANES, features), BF16),
            pltpu.VMEM((LANES, 2 * features), BF16),
            pltpu.VMEM((features, features), F32),
            pltpu.VMEM((features, LANES), F32),
            pltpu.VMEM((1, features), F32),
        ],
        compiler_params=params(),
        cost_estimate=cost(8 * images * tall * features * features, 16e6),
        name="back",
    )(order, resid, logits, cot, *mixed, summed, w, small)


def attend_back_body(extra, offset, order_ref, joint_ref, prob_ref, grad_ref, mixed_ref, act_ref, *refs):
    more, (out_ref, keep_ref, give_ref, total) = refs[:extra], refs[extra:]
    step = pl.program_id(0)

    @pl.when(step == 0)
    def _():
        total[...] = jnp.zeros_like(total)

    tall, width = joint_ref.shape[1:]
    third = width // 3
    low = iota((tall, LANES), 1) < LANES // 2
    for pair in range(third // LANES):
        query, keys, values = (
            joint_ref[0, :, part * third + pair * LANES : part * third + (pair + 1) * LANES]
            for part in range(3)
        )
        grad = grad_ref[0, :, offset + pair * LANES : offset + (pair + 1) * LANES]
        product = grad.astype(F32) * mixed_ref[0, :, pair * LANES : (pair + 1) * LANES].astype(F32)
        grads = []
        for side in range(2):
            mine = low if side == 0 else ~low
            prob = prob_ref[0, 2 * pair + side]
            inner = jnp.sum(jnp.where(mine, product, 0.0), axis=1, keepdims=True)
            grad_prob = dot(jnp.where(mine, grad, 0), values, NT)
            grad_scores = (prob.astype(F32) * (grad_prob - inner) * 0.125).astype(BF16)
            grads.append(
                (dot(grad_scores, keys), dot(grad_scores, query, TN), dot(prob, grad, TN))
            )
        for part in range(3):
            joined = jnp.where(low, grads[0][part], grads[1][part]).astype(BF16)
            out_ref[0, :, part * third + pair * LANES : part * third + (pair + 1) * LANES] = joined
    total[...] += dot(act_ref[0], out_ref[0], TN)

    @pl.when(step == pl.num_programs(0) - 1)
    def _():
        store_blocks(order_ref, total, keep_ref, give_ref, slice(0, width))
        place = width
        for source in more:
            end = place + source.shape[1]
            store_blocks(order_ref, source, keep_ref, give_ref, slice(place, end))
            place = end


def attend_back(blocks, offset, order, joint, prob, grad_mixed, mixed, act, more=()):
    images, tall, width = joint.shape
    features = act.shape[-1]
    third = width // 3
    columns = width + sum(m.shape[1] for m in more)
    half = (blocks // 2, features // blocks, columns)
    return pl.pallas_call(
        functools.partial(attend_back_body, len(more), offset),
        grid=(images,),
        in_specs=[
            SMEM,
            spec_image(joint.shape),
            spec_image(prob.shape),
            spec_image(grad_mixed.shape),
            spec_image(mixed.shape),
            spec_image(act.shape),
        ]
        + [spec_whole(m.shape) for m in more],
        out_specs=[spec_image(joint.shape), spec_whole(half), spec_whole(half)],
        out_shape=[
            jax.ShapeDtypeStruct(joint.shape, BF16),
            jax.ShapeDtypeStruct(half, BF16),
            jax.ShapeDtypeStruct(half, BF16),
        ],
        scratch_shapes=[pltpu.VMEM((features, width), F32)],
        compiler_params=params(),
        cost_estimate=cost(2 * images * tall * features * width * 5, 16e6),
        name="attend_back",
    )(order, joint, prob, grad_mixed, mixed, act, *more)


def finish_body(places, order_ref, token_ref, att_ref, j0, j1, w0, w1, small_ref, out_ref, s0, s1):
    @pl.when(pl.program_id(0) == 0)
    def _():
        for source, target in ((w0, s0), (w1, s1)):
            place_rows(order_ref, source, target)

    grad_act = dot(j0[0], s0[...], NT) + dot(j1[0], s1[...], NT)
    normed, factor = normalize(token_ref[0].astype(F32))
    result = att_ref[0].astype(F32) + norm_back(grad_act * small_ref[0:1, :], normed, factor)
    out_ref[0] = result[:places].astype(BF16)


def finish(places, order, tokens, att, joints, weights, small):
    images, tall, features = tokens.shape
    shape = (images, places, features)
    return pl.pallas_call(
        functools.partial(finish_body, places),
        grid=(images,),
        in_specs=[SMEM, spec_image(tokens.shape), spec_image(att.shape)]
        + [spec_image(j.shape) for j in joints]
        + [
            pl.BlockSpec(w.shape[:2] + (j.shape[2],), lambda i: (0, 0, 0))
            for w, j in zip(weights, joints)
        ]
        + [spec_whole(small.shape)],
        out_specs=spec_image(shape),
        out_shape=jax.ShapeDtypeStruct(shape, BF16),
        scratch_shapes=[pltpu.VMEM((features, j.shape[-1]), BF16) for j in joints],
        compiler_params=params(),
        cost_estimate=cost(6 * images * tall * features * features, 12e6),
        name="finish",
    )(order, tokens, att, *joints, *weights, small)


def per_device(
    tokens, cotangent, heads_in, heads_out, slot_router, first_gain, second_gain, expert_in, expert_out
):
    images, places, features = tokens.shape
    experts = slot_router.shape[1]
    group = lax.axis_size("grp")
    reps = lax.axis_size("rep")
    me = lax.axis_index("grp")
    own_rows = heads_in.shape[0]
    chip = me // 2
    direct = group == 8
    blocks = 8
    ways = jnp.arange(blocks, dtype=jnp.int32)
    if direct:
        order = jnp.concatenate([ways ^ me, (ways % 4 * 2 + ways // 4) ^ me, chip[None]])
    else:
        order = jnp.concatenate([ways, ways, chip[None]])
    tall = -(-places // 16) * 16
    slot_rows = -(-experts // 16) * 16
    part = features // 3
    wide = 3 * part

    thirds = [heads_in[:, k * features : (k + 1) * features] for k in range(3)]
    head_part = jnp.concatenate([t[:, :part] for t in thirds], axis=1)
    tail_part = jnp.concatenate([t[:, part:] for t in thirds] + [heads_out], axis=1)
    small = jnp.concatenate([first_gain[None], second_gain[None], slot_router.T], axis=0)
    small_rows = -(-small.shape[0] // 16) * 16
    grow = ((0, 0), (0, tall - places), (0, 0))
    source = jnp.pad(tokens, grow)
    cot = jnp.pad(cotangent, grow)
    if direct:
        small = jnp.pad(small, ((0, small_rows - small.shape[0]), (0, wide - own_rows)))
        head_part = jnp.concatenate([head_part, small], axis=0)
        middle = head_part.shape[0] // 2
        half = own_rows // 2
        first = gather_stage(head_part[None, :middle], group, 2)
        second = gather_stage(head_part[None, middle:], group, 4)
        tail = after(tail_part, first, second)
        first = gather_stage(first, group, 4)
        second = gather_stage(second, group, 2)
        tail_first = gather_stage(tail[None, :half], group, 2)
        tail_second = gather_stage(tail[None, half:], group, 4)
        held = join_halves(first, second)
        w_head = jnp.stack([held, swap(held, "grp", group, 1)], axis=1)
        w_head = w_head.reshape(blocks, -1, wide)
        tail_first, tail_second, source, cot = after((tail_first, tail_second, source, cot), w_head)
        source = after(source, cot, tail_first, tail_second)
    else:
        w_head = lax.all_gather(head_part, "grp", axis=0, tiled=True).reshape(blocks, -1, wide)
        small = lax.all_gather(small, "grp", axis=1, tiled=True).reshape(-1, blocks, features // blocks)
        small = small.transpose(1, 0, 2)
        small = jnp.pad(
            small,
            ((0, 0), (0, small_rows - small.shape[1]), (0, wide - small.shape[2])),
        )
        w_head = jnp.concatenate([w_head, small], axis=1)
        w_tail = lax.all_gather(tail_part, "grp", axis=0, tiled=True).reshape(blocks, -1, 3 * features)

    act, small, joint_head, prob_head, mixed_head = attend(
        True, places, order, source, w_head, (wide, 0)
    )
    if direct:
        first = swap(tail_first, "grp", group, 4)
        second = swap(tail_second, "grp", group, 2)
        first, second = after((first, second), mixed_head)
        held = join_halves(
            jnp.concatenate([tail_first, first]), jnp.concatenate([tail_second, second])
        )
        w_tail = jnp.stack([held, swap(held, "grp", group, 1)], axis=1)
        w_tail = w_tail.reshape(blocks, -1, 3 * features)
    joint_tail, prob_tail, mixed_tail = attend(False, places, order, act, w_tail, (2 * wide, 0))
    mixes = [mixed_head, mixed_tail]
    resid, logits, packed = route(
        places, experts, slot_rows, order, source, cot, mixes, w_tail, small
    )

    leaving = packed[:, :experts].transpose(1, 0, 2)
    arrived = jnp.stack(
        [leaving[0]] + [swap(leaving[k], "grp", group, 2 * k) for k in range(1, experts)]
    )
    arrived = jnp.stack([arrived, swap(arrived, "grp", group, 1)])
    received = arrived.reshape(2 * experts * images, 2 * features)
    piece_in, piece_out = expert_in[0], expert_out[0]
    result = expert(received, piece_in, piece_out).reshape(2, experts, images, 2 * features)
    both = add_low(result[0], swap(result[1], "grp", group, 1))
    summed = jnp.stack(
        [both[0]] + [swap(both[k], "grp", group, 2 * k) for k in range(1, experts)], axis=1
    )
    summed = jnp.pad(summed, ((0, 0), (0, slot_rows - experts), (0, 0)))

    every = received
    every = jnp.concatenate([every, swap(after(every, summed), "rep", reps, 1)])
    output, att, grad_mixed, grad_out, grad_side = back(
        places, experts, order, resid, logits, cot, mixes, summed, w_tail, small
    )
    grad_mixed, every = lax.optimization_barrier((grad_mixed, every))
    far = swap(every, "rep", reps, 2)
    grad_joint_tail, keep_tail, give_tail = attend_back(
        blocks, part, order, joint_tail, prob_tail, grad_mixed, mixed_tail, act,
        (grad_out, grad_side),
    )
    if direct:
        own, others, sums = spread_sum(keep_tail, give_tail)
        grad_mixed = after(grad_mixed, *sums)
    grad_joint_head, keep_head, give_head = attend_back(
        blocks, 0, order, joint_head, prob_head, grad_mixed, mixed_head, act
    )
    every = jnp.concatenate([every, after(far, grad_joint_head)])
    if direct:
        own, others = after((own, others), grad_joint_head)
        tail_sum = add_low(own, *others)
        odd = lax.axis_index("rep") % 2 == 1
        upper, lower = tail_sum[:half], tail_sum[half:]
        mine = jnp.where(odd, lower, upper)
        other = swap(jnp.where(odd, upper, lower), "rep", reps, 1)
        own, others, sums = spread_sum(keep_head, give_head)
        att = after(att, mine, *sums)
        token_grad = finish(
            places, order, source, att, [grad_joint_head, grad_joint_tail], [w_head, w_tail], small
        )
        (own, others), other = after(((own, others), other), token_grad)
        tail_sum = add_low(mine, other)
        head_sum = add_low(own, *others)
        every, tail_sum, head_sum = after((every, tail_sum, head_sum), token_grad)
        tail_other = swap(tail_sum, "rep", reps, 2)
        head_other = swap(head_sum, "rep", reps, 1)
        expert_in_grad, expert_out_grad = expert_grad(every, piece_in, piece_out)
        tail_other, head_other = after((tail_other, head_other), expert_in_grad)
        tail_sum, head_sum = add_low(tail_sum, tail_other), add_low(head_sum, head_other)
        tail_other = swap(tail_sum, "rep", reps, 1)
        head_sum = head_sum.astype(F32) + swap(head_sum, "rep", reps, 3).astype(F32)
        tail_sum = jnp.concatenate(
            [jnp.where(odd, tail_other, tail_sum), jnp.where(odd, tail_sum, tail_other)]
        ).astype(F32)
    else:
        tail_sum = jnp.concatenate([keep_tail, give_tail]).reshape(features, -1)
        tail_sum = lax.psum_scatter(tail_sum, "grp", scatter_dimension=0, tiled=True)
        head_sum = jnp.concatenate([keep_head, give_head]).reshape(features, -1)
        head_sum = lax.psum_scatter(head_sum, "grp", scatter_dimension=0, tiled=True)
        token_grad = finish(
            places, order, source, att, [grad_joint_head, grad_joint_tail], [w_head, w_tail], small
        )
        expert_in_grad, expert_out_grad = expert_grad(every, piece_in, piece_out)
        tail_sum = lax.psum(tail_sum, "rep").astype(F32)
        head_sum = lax.psum(head_sum, "rep").astype(F32)

    pieces = []
    for k in range(3):
        pieces.append(head_sum[:, k * part : (k + 1) * part])
        pieces.append(tail_sum[:, 2 * k * part : 2 * (k + 1) * part])
    heads_in_sum = jnp.concatenate(pieces, axis=1)
    gain_one_grad = jnp.sum(heads_in_sum * heads_in.astype(F32), axis=1) / first_gain.astype(F32)
    rest = tail_sum[:, 2 * wide :]
    return (
        output,
        token_grad,
        heads_in_sum,
        rest[:, :features],
        rest[:, features : features + experts],
        gain_one_grad,
        rest[:, features + experts],
        expert_in_grad[None],
        expert_out_grad[None],
    )


def solution(mesh):
    token_spec = P(("rep", "grp"), None, None)
    matrix, vector, stack = P("grp", None), P("grp"), P("grp", None, None)
    return jax.shard_map(
        per_device,
        mesh=mesh,
        in_specs=(token_spec, token_spec, matrix, matrix, matrix, vector, vector, stack, stack),
        out_specs=(token_spec, token_spec, matrix, matrix, matrix, vector, vector, stack, stack),
        check_vma=False,
    )
```

```python
import functools

import jax
import jax.numpy as jnp
from jax import lax
from jax.experimental import pallas as pl
from jax.experimental.pallas import tpu as pltpu
from jax.sharding import PartitionSpec as P

HEADS = 12
LANES = 128
F32 = jnp.float32
BF16 = jnp.bfloat16
LOW = -1e30

NN = (((1,), (0,)), ((), ()))
NT = (((1,), (1,)), ((), ()))
TN = (((0,), (0,)), ((), ()))


def dot(left, right, form=NN):
    return lax.dot_general(left, right, form, preferred_element_type=F32)


def swap(values, axis, size, bit):
    return lax.ppermute(values, axis, [(place, place ^ bit) for place in range(size)])


def after(values, *others):
    return lax.optimization_barrier((values, others))[0]


def gather_first(own):
    return swap(own[0], "grp", 8, 2), swap(own[1], "grp", 8, 4)


def gather_second(joined):
    return swap(joined[0], "grp", 8, 4), swap(joined[1], "grp", 8, 2)


def gather_last(*stages):
    held = tuple(part for stage in stages for part in stage)
    return held + tuple(swap(part, "grp", 8, 1) for part in held)


def as_gathered(blocks, cut):
    held = []
    for k in range(2):
        own, x, y, far = blocks[k], blocks[k + 2], blocks[k + 4], blocks[k + 6]
        held += [own[:cut], own[cut:], x[:cut], y[cut:]]
        held += [jnp.concatenate([y[:cut], far[:cut]]), jnp.concatenate([x[cut:], far[cut:]])]
    return tuple(held)


def iota(shape, axis):
    return lax.broadcasted_iota(jnp.int32, shape, axis)


def normalize(values):
    center = values - jnp.mean(values, axis=-1, keepdims=True)
    factor = lax.rsqrt(jnp.mean(center * center, axis=-1, keepdims=True) + 1e-06)
    return center * factor, factor


def norm_back(scaled, normed, factor):
    inner = (
        scaled
        - jnp.mean(scaled, axis=-1, keepdims=True)
        - normed * jnp.mean(scaled * normed, axis=-1, keepdims=True)
    )
    return factor * inner


def pieces_of(rows, extra):
    half = rows // 2
    cut = extra + half
    for core in range(2):
        base = 6 * core
        yield base, extra, core, 0
        yield base + 1, 0, core, half
        yield base + 2, extra, core + 2, 0
        yield base + 3, 0, core + 4, half
        yield base + 4, extra, core + 4, 0
        yield base + 4, cut + extra, core + 6, 0
        yield base + 5, 0, core + 2, half
        yield base + 5, half, core + 6, half


def place_pieces(order_ref, pieces, rows, extra, target, columns):
    half = rows // 2
    for n, start, block, offset in pieces_of(rows, extra):
        place = pl.multiple_of(order_ref[block] * rows + offset, 16)
        target[pl.ds(place, half), :] = pieces[n][start : start + half, columns]


def store_blocks(order_ref, source, targets, columns):
    rows = source.shape[0] // 8
    n = 0
    for target in targets:
        for k in range(target.shape[0] // rows):
            start = pl.multiple_of(order_ref[8 + n] * rows, 32)
            target[k * rows : (k + 1) * rows, columns] = source[pl.ds(start, rows), :].astype(BF16)
            n += 1


def gather_small(order_ref, pieces, rows, extra, small_ref):
    total = jnp.zeros(small_ref.shape, F32)
    lane = iota((LANES, small_ref.shape[1]), 0)
    place = iota((LANES, small_ref.shape[1]), 1)
    cut = extra + rows // 2
    for core in range(2):
        for n, start, block in ((0, 0, 0), (2, 0, 2), (4, 0, 4), (4, cut, 6)):
            held = pieces[6 * core + n][start : start + extra, :LANES]
            fits = (place == order_ref[block + core] * rows + lane) & (lane < rows)
            total = total + dot(held, jnp.where(fits, 1.0, 0.0).astype(BF16))
    small_ref[...] = total


def rows_of(place, tall):
    return pl.ds(pl.multiple_of(place * tall, 16), tall)


VM = pl.BlockSpec(memory_space=pltpu.VMEM)
SM = pl.BlockSpec(memory_space=pltpu.SMEM)


def call(body, name, inputs, outputs, scratch, limit, flops, hbm=()):
    return pl.pallas_call(
        body,
        in_specs=[SM if x.dtype == jnp.int32 else VM for x in inputs],
        out_specs=[VM] * len(outputs),
        out_shape=[
            jax.ShapeDtypeStruct(shape, kind) if n in hbm else pltpu.VMEM(shape, kind)
            for n, (shape, kind) in enumerate(outputs)
        ],
        scratch_shapes=[pltpu.VMEM(shape, kind) for shape, kind in scratch],
        compiler_params=pltpu.CompilerParams(vmem_limit_bytes=limit * 1024 * 1024),
        cost_estimate=pl.CostEstimate(flops=int(flops), bytes_accessed=1000000, transcendentals=0),
        name=name,
    )(*inputs)


def prepare_body(in_ref, out_ref, router_ref, gains_ref, h0, h1, t0, t1):
    rows, features = out_ref.shape
    half = rows // 2
    experts = router_ref.shape[1]
    part = features // 3
    extra = h0.shape[0] - half
    gains = gains_ref[...].astype(F32)
    router = router_ref[...].astype(F32)
    router = jnp.concatenate([router, jnp.zeros((rows, LANES - experts), F32)], axis=1).T
    small = jnp.concatenate([gains, router[: extra - 2]], axis=0)
    small = jnp.concatenate([small, jnp.zeros((extra, LANES - rows), F32)], axis=1)
    h0[:extra, :] = jnp.zeros((extra, h0.shape[1]), BF16)
    h0[:extra, :LANES] = small.astype(BF16)
    for head, tail, start, here in ((h0, t0, extra, slice(0, half)), (h1, t1, 0, slice(half, rows))):
        for k in range(3):
            base = k * features
            head[start:, k * part : (k + 1) * part] = in_ref[here, base : base + part]
            tail[:, 2 * k * part : 2 * (k + 1) * part] = in_ref[here, base + part : base + features]
        tail[:, 2 * features :] = out_ref[here, :]


def prepare(heads_in, heads_out, router, gains):
    rows, features = heads_out.shape
    extra = -(-(router.shape[1] + 2) // 16) * 16
    return call(
        prepare_body,
        "prepare",
        (heads_in, heads_out, router, gains),
        [
            ((extra + rows // 2, features), BF16),
            ((rows // 2, features), BF16),
            ((rows // 2, 3 * features), BF16),
            ((rows // 2, 3 * features), BF16),
        ],
        [],
        4,
        1e6,
    )


def join_body(a0, a1, b0, b1, a_ref, b_ref):
    for first, second, target in ((a0, a1, a_ref), (b0, b1, b_ref)):
        target[: first.shape[0], :] = first[...]
        target[first.shape[0] :, :] = second[...]


def join(own, got):
    outputs = [((2 * x.shape[0], x.shape[1]), BF16) for x in own]
    return call(join_body, "join", (own[0], got[0], own[1], got[1]), outputs, [], 4, 1e6)


def attend_body(first, images, places, order_ref, source_ref, *refs):
    pieces, refs = refs[:12], refs[12:]
    features = source_ref.shape[1]
    rows = features // 8
    if first:
        act_ref, small_ref, weight, joint_ref, prob_ref, mixed_ref = refs
        extra = small_ref.shape[0]
    else:
        out_weight, weight, joint_ref, prob_ref, mixed_ref = refs
        act_ref = source_ref
        extra = 0
    tall = source_ref.shape[0] // images
    width = weight.shape[1]
    place_pieces(order_ref, pieces, rows, extra, weight, slice(0, width))
    if first:
        gather_small(order_ref, pieces, rows, extra, small_ref)

        @pl.loop(0, images)
        def _(i):
            here = rows_of(i, tall)
            normed, _ = normalize(source_ref[here, :].astype(F32))
            act_ref[here, :] = (normed * small_ref[0:1, :]).astype(BF16)
    else:
        place_pieces(order_ref, pieces, rows, 0, out_weight, slice(width, width + features))

    @pl.loop(0, images // 2)
    def _(i):
        here = rows_of(i, 2 * tall)
        joint_ref[here, :] = dot(act_ref[here, :], weight[...]).astype(BF16)

    third = width // 3
    heads = prob_ref.shape[0] // images
    low = iota((tall, LANES), 1) < LANES // 2
    inside = iota((tall, LANES), 0) < places
    seen = iota((tall, tall), 1) < places

    @pl.loop(0, images)
    def _(i):
        here = rows_of(i, tall)
        for pair in range(third // LANES):
            query, keys, values = (
                joint_ref[here, part * third + pair * LANES : part * third + (pair + 1) * LANES]
                for part in range(3)
            )
            query = query * 0.125
            outs = []
            for side in range(2):
                mine = low if side == 0 else ~low
                scores = dot(jnp.where(mine, query, 0), keys, NT)
                scores = jnp.where(seen, scores, LOW)
                power = jnp.exp(scores - jnp.max(scores, axis=1, keepdims=True))
                prob = (power * (1.0 / jnp.sum(power, axis=1, keepdims=True))).astype(BF16)
                prob_ref[i * heads + 2 * pair + side] = prob
                outs.append(dot(prob, values))
            mixed = jnp.where(inside, jnp.where(low, outs[0], outs[1]), 0.0)
            mixed_ref[here, pair * LANES : (pair + 1) * LANES] = mixed.astype(BF16)


def attend(first, images, places, order, source, pieces, width):
    total, features = source.shape
    tall = total // images
    heads = width // 3 // 64
    extra = pieces[0].shape[0] - features // 16
    outputs = [
        ((features, width), BF16),
        ((total, width), BF16),
        ((images * heads, tall, tall), BF16),
        ((total, width // 3), BF16),
    ]
    if first:
        outputs = [((total, features), BF16), ((extra, features), F32)] + outputs
    else:
        outputs = [((features, features), BF16)] + outputs
    return call(
        functools.partial(attend_body, first, images, places),
        "attend",
        (order, source, *pieces),
        outputs,
        [],
        12,
        2 * total * features * width * 2,
    )


def softmaxes(logits, places, experts):
    rows = iota(logits.shape, 0) < experts
    lanes = iota(logits.shape, 1) < places
    wide = jnp.where(lanes, logits, LOW)
    wide = jnp.exp(wide - jnp.max(wide, axis=1, keepdims=True))
    dispatch = wide / jnp.sum(wide, axis=1, keepdims=True)
    tall = jnp.where(rows, logits, LOW)
    tall = jnp.exp(tall - jnp.max(tall, axis=0, keepdims=True))
    combine = tall / jnp.sum(tall, axis=0, keepdims=True)
    return jnp.where(rows, dispatch, 0.0), combine


def slot_rows_of(experts, order_ref, small_ref, slots):
    rows = small_ref.shape[0]
    slot, row = iota((slots, rows), 0), iota((slots, rows), 1)
    chip = order_ref[order_ref.shape[0] - 1]
    fits = (row == (slot ^ chip) + 2) & (slot < experts)
    return dot(jnp.where(fits, 1.0, 0.0).astype(BF16), small_ref[...].astype(BF16)).astype(BF16)


def pick_rows(shape, wanted):
    row, column = iota(shape, 0), iota(shape, 1)
    return jnp.where(column == wanted(row), 1.0, 0.0).astype(BF16)


def route_body(
    images, places, experts, order_ref, token_ref, cot_ref, m0, m1, weight, small_ref,
    resid_ref, logit_ref, *refs,
):
    out_refs, packed_ref = refs[:-1], refs[-1]
    slots = logit_ref.shape[0] // images
    router = slot_rows_of(experts, order_ref, small_ref, slots)
    tall = token_ref.shape[0] // images
    features = token_ref.shape[1]

    @pl.loop(0, images // 2)
    def _(i):
        here = rows_of(i, 2 * tall)
        mixed = jnp.concatenate([m0[here, :], m1[here, :]], axis=1)
        resid_ref[here, :] = token_ref[here, :].astype(F32) + dot(mixed, weight[...])

    @pl.loop(0, images)
    def _(i):
        here = rows_of(i, tall)
        normed, _ = normalize(resid_ref[here, :])
        act = (normed * small_ref[1:2, :]).astype(BF16)
        logits = dot(router, act, NT)
        group = rows_of(i, slots)
        logit_ref[group, :] = logits
        dispatch, combine = softmaxes(logits, places, experts)
        packed_ref[group, :features] = dot(dispatch.astype(BF16), act).astype(BF16)
        packed_ref[group, features:] = dot(combine.astype(BF16), cot_ref[here, :]).astype(BF16)

    high = out_refs[0].shape[0]
    pick = pick_rows(
        (experts * high, images * slots),
        lambda n: jnp.where(n % high < images, n % high * slots + n // high, -1),
    )
    packed = dot(pick, packed_ref[...]).astype(BF16)
    for k, out_ref in enumerate(out_refs):
        out_ref[...] = packed[k * high : (k + 1) * high, :]


def route(images, places, experts, slots, order, tokens, cot, mixed, w, small):
    total, features = tokens.shape
    high = -(-images // 8) * 8
    return call(
        functools.partial(route_body, images, places, experts),
        "route",
        (order, tokens, cot, *mixed, w, small),
        [((total, features), F32), ((images * slots, total // images), F32)]
        + [((high, 2 * features), BF16)] * experts,
        [((images * slots, 2 * features), BF16)],
        10,
        4 * total * features * features,
    )


def gelu_parts(values):
    scale, cubic = 0.7978845608028654, 0.044715
    square = values * values
    bent = jnp.tanh(scale * values * (1.0 + cubic * square))
    half = 0.5 * (1.0 + bent)
    slope = half + 0.5 * values * (1.0 - bent * bent) * scale * (1.0 + 3.0 * cubic * square)
    return values * half, slope


def expert_body(count, images, in_ref, out_ref, *refs):
    sources, (packed_ref, keep_ref, give_ref, rows_ref, back_ref) = refs[:count], refs[count:]
    features = in_ref.shape[0]
    high = sources[0].shape[0]
    for k, source in enumerate(sources):
        rows_ref[k * high : (k + 1) * high, :] = source[...]
    rows, arriving = rows_ref[:, :features], rows_ref[:, features:]
    total = jnp.zeros((rows.shape[0], features), F32)
    grad_total = total
    step = 512
    for start in range(0, in_ref.shape[1], step):
        w_in = in_ref[:, start : start + step]
        w_out = out_ref[start : start + step, :]
        hidden, slope = gelu_parts(dot(rows, w_in))
        grad_pre = (dot(arriving, w_out, NT) * slope).astype(BF16)
        total = total + dot(hidden.astype(BF16), w_out)
        grad_total = grad_total + dot(grad_pre, w_in, NT)
    back_ref[:, :features] = total.astype(BF16)
    back_ref[:, features:] = grad_total.astype(BF16)
    half = keep_ref.shape[0]
    keep_ref[...] = back_ref[:half, :]
    give_ref[...] = back_ref[half:, :]
    pick = pick_rows(
        (packed_ref.shape[0], rows_ref.shape[0]), lambda n: n // images * high + n % images
    )
    packed_ref[...] = dot(pick, rows_ref[...]).astype(BF16)


def expert(images, piece_in, piece_out, sources):
    high, wide = sources[0].shape
    rows = high * len(sources)
    return call(
        functools.partial(expert_body, len(sources), images),
        "expert",
        (piece_in, piece_out, *sources),
        [
            ((images * len(sources), wide), BF16),
            ((rows // 2, wide), BF16),
            ((rows // 2, wide), BF16),
        ],
        [((rows, wide), BF16)] * 2,
        8,
        1e9,
    )


def pair_sum_body(parts, keep_ref, *refs):
    got_refs, out_refs = refs[:parts], refs[parts:]
    rows = out_refs[0].shape[0]
    each = len(out_refs) // parts
    for k, out_ref in enumerate(out_refs):
        kept = keep_ref[k * rows : (k + 1) * rows, :].astype(F32)
        got = got_refs[k // each][k % each * rows : (k % each + 1) * rows, :].astype(F32)
        out_ref[...] = (kept + got).astype(BF16)


def pair_sum(keep, got, count):
    shape = (keep.shape[0] // count, keep.shape[1])
    body = functools.partial(pair_sum_body, len(got))
    return call(body, "pair_sum", (keep, *got), [(shape, BF16)] * count, [], 4, 1e6)


def total_body(*refs):
    refs[-1][...] = sum(ref[...].astype(F32) for ref in refs[:-1]).astype(BF16)


def total_sum(*terms):
    return call(total_body, "total_sum", terms, [(terms[0].shape, BF16)], [], 4, 1e6)[0]


def split_sum_body(order_ref, *refs):
    terms, (mine_ref, give_ref, scratch) = refs[:-3], refs[-3:]
    scratch[...] = sum(ref[...].astype(F32) for ref in terms)
    half = mine_ref.shape[0]
    odd = order_ref[order_ref.shape[0] - 2]
    mine = pl.multiple_of(odd * half, 16)
    other = pl.multiple_of((1 - odd) * half, 16)
    mine_ref[...] = scratch[pl.ds(mine, half), :].astype(BF16)
    give_ref[...] = scratch[pl.ds(other, half), :].astype(BF16)


def split_sum(order, *terms):
    rows, wide = terms[0].shape
    shape = (rows // 2, wide)
    return call(
        split_sum_body, "split_sum", (order, *terms), [(shape, BF16)] * 2, [((rows, wide), F32)], 8, 1e6
    )


def shares_body(
    experts, order_ref, head_ref, head_other, tail_ref, tail_other, w_ref, gain_ref,
    in_ref, out_ref, router_ref, gain_one_ref, gain_two_ref, tail,
):
    rows, features = out_ref.shape
    half = rows // 2
    odd = order_ref[order_ref.shape[0] - 2]
    tail[pl.ds(pl.multiple_of(odd * half, 16), half), :] = tail_ref[...].astype(F32)
    tail[pl.ds(pl.multiple_of((1 - odd) * half, 16), half), :] = tail_other[...].astype(F32)
    part = features // 3
    for k in range(3):
        here = slice(k * part, (k + 1) * part)
        in_ref[:, k * features : k * features + part] = (
            head_ref[:, here].astype(F32) + head_other[:, here].astype(F32)
        )
        in_ref[:, k * features + part : (k + 1) * features] = tail[:, 2 * k * part : 2 * (k + 1) * part]
    out_ref[...] = tail[:, 2 * features : 3 * features]
    rest = tail[:, 3 * features :]
    router_ref[...] = rest[:, :experts]
    gain_two_ref[...] = rest.T[experts : experts + 1, :]
    gain_one = jnp.sum(in_ref[...] * w_ref[...].astype(F32), axis=1, keepdims=True)
    gain_one = jnp.broadcast_to(gain_one, (rows, LANES)).T[:1, :]
    gain_one_ref[...] = gain_one / gain_ref[...].astype(F32)


def shares(experts, order, head, head_other, tail, tail_other, w, gain):
    rows, features = head.shape
    return call(
        functools.partial(shares_body, experts),
        "shares",
        (order, head, head_other, tail, tail_other, w, gain),
        [
            (w.shape, F32),
            ((rows, features), F32),
            ((rows, experts), F32),
            ((1, rows), F32),
            ((1, rows), F32),
        ],
        [((rows, tail.shape[1]), F32)],
        8,
        1e6,
        hbm=range(5),
    )


def expert_grad_body(count, *refs):
    sources, (in_ref, out_ref, grad_in_ref, grad_out_ref) = refs[:count], refs[count:]
    features = in_ref.shape[0]
    every = jnp.concatenate([source[...] for source in sources], axis=0)
    rows, arriving = every[:, :features], every[:, features:]
    hidden, slope = gelu_parts(dot(rows, in_ref[...]))
    grad_pre = (dot(arriving, out_ref[...], NT) * slope).astype(BF16)
    grad_in_ref[...] = dot(rows, grad_pre, TN)
    grad_out_ref[...] = dot(hidden.astype(BF16), arriving, TN)


def expert_grad(sources, piece_in, piece_out):
    features, hidden = piece_in.shape
    step = 256
    wide = pl.BlockSpec((features, step), lambda i: (0, i))
    high = pl.BlockSpec((step, features), lambda i: (i, 0))
    return pl.pallas_call(
        functools.partial(expert_grad_body, len(sources)),
        grid=(hidden // step,),
        in_specs=[pl.BlockSpec(x.shape, lambda i: (0, 0)) for x in sources] + [wide, high],
        out_specs=[wide, high],
        out_shape=[
            jax.ShapeDtypeStruct(piece_in.shape, F32),
            jax.ShapeDtypeStruct(piece_out.shape, F32),
        ],
        compiler_params=pltpu.CompilerParams(vmem_limit_bytes=16 * 1024 * 1024),
        cost_estimate=pl.CostEstimate(
            flops=1600 * piece_in.size, bytes_accessed=14000000, transcendentals=0
        ),
        name="expert_grad",
    )(*sources, piece_in, piece_out)


def back_body(
    images, places, experts, order_ref, resid_ref, logit_ref, cot_ref, m0, m1, weight, small_ref, *refs
):
    sources, refs = refs[:experts], refs[experts:]
    output_ref, att_ref, grad_mixed_ref, grad_w_ref, grad_side_ref, summed_ref = refs
    slots = logit_ref.shape[0] // images
    router = slot_rows_of(experts, order_ref, small_ref, slots)
    total, features = resid_ref.shape
    tall = total // images
    gain = small_ref[1:2, :]
    high = sources[0].shape[0]
    pick = pick_rows(
        (images * slots, experts * high),
        lambda n: jnp.where(n % slots < experts, n % slots * high + n // slots, -1),
    )
    arrived = jnp.concatenate([source[...] for source in sources], axis=0)
    summed_ref[...] = dot(pick, arrived).astype(BF16)

    def image(i, carry):
        side, gain_sum = carry
        here = rows_of(i, tall)
        group = rows_of(i, slots)
        expert_sum, grad_slots = summed_ref[group, :features], summed_ref[group, features:]
        resid = resid_ref[here, :]
        cot = cot_ref[here, :]
        dispatch, combine = softmaxes(logit_ref[group, :], places, experts)
        output = resid + dot(combine.astype(BF16), expert_sum, TN)
        output_ref[i] = output[:places].astype(BF16)
        normed, factor = normalize(resid)
        act = (normed * gain).astype(BF16)
        grad_comb = dot(expert_sum, cot, NT)
        grad_disp = dot(grad_slots, act, NT)
        grad_logits = combine * (grad_comb - jnp.sum(grad_comb * combine, axis=0, keepdims=True))
        grad_logits = grad_logits + dispatch * (
            grad_disp - jnp.sum(grad_disp * dispatch, axis=1, keepdims=True)
        )
        grad_logits = grad_logits.astype(BF16)
        grad_act = dot(
            jnp.concatenate([dispatch.astype(BF16), grad_logits], axis=0),
            jnp.concatenate([grad_slots, router], axis=0),
            TN,
        )
        att = cot.astype(F32) + norm_back(grad_act * gain, normed, factor)
        att_ref[here, :] = att.astype(BF16)
        return (
            side + dot(grad_logits, act),
            gain_sum + jnp.sum(grad_act * normed, axis=0, keepdims=True),
        )

    side, gain_sum = lax.fori_loop(
        0, images, image, (jnp.zeros((slots, features), F32), jnp.zeros((1, features), F32))
    )

    @pl.loop(0, images // 2)
    def _(i):
        here = rows_of(i, 2 * tall)
        grad_mixed_ref[here, :] = dot(att_ref[here, :], weight[...], NT).astype(BF16)

    part = m0.shape[1]
    grad_w_ref[:part, :] = dot(m0[...], att_ref[...], TN).astype(BF16)
    grad_w_ref[part:, :] = dot(m1[...], att_ref[...], TN).astype(BF16)
    slot = iota((LANES, slots), 0) ^ order_ref[order_ref.shape[0] - 1]
    slot = jnp.where(iota((LANES, slots), 0) < experts, slot, -1)
    fits = jnp.where(slot == iota((LANES, slots), 1), 1.0, 0.0).astype(BF16)
    side = dot(fits, side.astype(BF16))
    side = jnp.where(iota(side.shape, 0) == experts, gain_sum, side)
    grad_side_ref[...] = side.T.astype(BF16)


def back(images, places, experts, order, resid, logits, cot, mixed, w, small, sources):
    total, features = resid.shape
    return call(
        functools.partial(back_body, images, places, experts),
        "back",
        (order, resid, logits, cot, *mixed, w, small, *sources),
        [
            ((images, places, features), BF16),
            ((total, features), BF16),
            ((total, features), BF16),
            ((features, features), BF16),
            ((features, LANES), BF16),
        ],
        [((logits.shape[0], 2 * features), BF16)],
        14,
        8 * total * features * features,
        hbm=(0,),
    )


def attend_back_body(images, extra, offset, order_ref, joint_ref, prob_ref, grad_ref, mixed_ref, act_ref, *refs):
    more, (out_ref, *targets, total) = refs[:extra], refs[extra:]
    width = joint_ref.shape[1]
    tall = joint_ref.shape[0] // images
    third = width // 3
    heads = prob_ref.shape[0] // images
    low = iota((tall, LANES), 1) < LANES // 2

    @pl.loop(0, images)
    def _(i):
        here = rows_of(i, tall)
        for pair in range(third // LANES):
            query, keys, values = (
                joint_ref[here, part * third + pair * LANES : part * third + (pair + 1) * LANES]
                for part in range(3)
            )
            grad = grad_ref[here, offset + pair * LANES : offset + (pair + 1) * LANES]
            product = grad.astype(F32) * mixed_ref[
                here, pair * LANES : (pair + 1) * LANES
            ].astype(F32)
            grads = []
            for side in range(2):
                mine = low if side == 0 else ~low
                prob = prob_ref[i * heads + 2 * pair + side]
                inner = jnp.sum(jnp.where(mine, product, 0.0), axis=1, keepdims=True)
                grad_prob = dot(jnp.where(mine, grad, 0), values, NT)
                grad_scores = (prob.astype(F32) * (grad_prob - inner) * 0.125).astype(BF16)
                grads.append(
                    (dot(grad_scores, keys), dot(grad_scores, query, TN), dot(prob, grad, TN))
                )
            for part in range(3):
                joined = jnp.where(low, grads[0][part], grads[1][part]).astype(BF16)
                out_ref[
                    here, part * third + pair * LANES : part * third + (pair + 1) * LANES
                ] = joined

    step = third
    for start in range(0, width, step):
        total[:, start : start + step] = dot(
            act_ref[...], out_ref[:, start : start + step], TN
        ).astype(BF16)
    store_blocks(order_ref, total, targets, slice(0, width))
    place = width
    for source in more:
        end = place + source.shape[1]
        store_blocks(order_ref, source, targets, slice(place, end))
        place = end


def attend_back(images, offset, order, joint, prob, grad_mixed, mixed, act, splits, more=()):
    total, width = joint.shape
    features = act.shape[1]
    columns = width + sum(m.shape[1] for m in more)
    parts = [((features // n, columns), BF16) for n in splits]
    return call(
        functools.partial(attend_back_body, images, len(more), offset),
        "attend_back",
        (order, joint, prob, grad_mixed, mixed, act, *more),
        [(joint.shape, BF16)] + parts,
        [((features, width), BF16)],
        16,
        2 * total * features * width * 4,
    )


def finish_body(images, places, token_ref, att_ref, j0, j1, s0, s1, small_ref, out_ref):
    total, features = token_ref.shape
    tall = total // images

    @pl.loop(0, images // 2)
    def _(i):
        here = rows_of(i, 2 * tall)
        grad_act = dot(j0[here, :], s0[...], NT) + dot(j1[here, :], s1[...], NT)
        normed, factor = normalize(token_ref[here, :].astype(F32))
        result = att_ref[here, :].astype(F32)
        result = result + norm_back(grad_act * small_ref[0:1, :], normed, factor)
        result = result.astype(BF16)
        out_ref[2 * i] = result[:places]
        out_ref[2 * i + 1] = result[tall : tall + places]


def finish(images, places, tokens, att, joints, weights, small):
    total, features = tokens.shape
    return call(
        functools.partial(finish_body, images, places),
        "finish",
        (tokens, att, *joints, *weights, small),
        [((images, places, features), BF16)],
        [],
        12,
        6 * total * features * features,
        hbm=(0,),
    )[0]


def per_device(
    tokens, cotangent, heads_in, heads_out, slot_router, first_gain, second_gain, expert_in, expert_out
):
    images, places, features = tokens.shape
    experts = slot_router.shape[1]
    group = lax.axis_size("grp")
    reps = lax.axis_size("rep")
    me = lax.axis_index("grp")
    own_rows = heads_in.shape[0]
    chip = me // 2
    odd = lax.axis_index("rep") % 2
    direct = group == 8
    ways = jnp.arange(8, dtype=jnp.int32)
    if direct:
        order = jnp.concatenate([ways ^ me, (ways % 4 * 2 + ways // 4) ^ me, odd[None], chip[None]])
    else:
        order = jnp.concatenate([ways, ways, odd[None], chip[None]])
    tall = -(-places // 16) * 16
    slot_rows = -(-experts // 16) * 16
    part = features // 3
    wide = 3 * part

    grow = ((0, 0), (0, tall - places), (0, 0))
    source = jnp.pad(tokens, grow).reshape(images * tall, features)
    cot = jnp.pad(cotangent, grow).reshape(images * tall, features)
    gains = jnp.stack([first_gain, second_gain])
    if direct:
        h0, h1, t0, t1 = prepare(heads_in, heads_out, slot_router, gains)
        head_first = gather_first((h0, h1))
        head_first = after(head_first, source, cot)
        (t0, t1), head_first = lax.optimization_barrier(((t0, t1), head_first))
        head_second = gather_second(join((h0, h1), head_first))
        tail_first = gather_first((t0, t1))
        head = gather_last((h0, h1), head_first, head_second)
        tail_first = after(tail_first, *head)
        tail_join = join((t0, t1), tail_first)
        source = after(source, *tail_join)
    else:
        thirds = [heads_in[:, k * features : (k + 1) * features] for k in range(3)]
        head_part = jnp.concatenate([t[:, :part] for t in thirds], axis=1)
        tail_part = jnp.concatenate([t[:, part:] for t in thirds] + [heads_out], axis=1)
        small = jnp.concatenate([gains, slot_router.T], axis=0)
        extra = -(-small.shape[0] // 16) * 16
        head_part = lax.all_gather(head_part, "grp", axis=0, tiled=True).reshape(8, -1, wide)
        small = lax.all_gather(small, "grp", axis=1, tiled=True).reshape(-1, 8, features // 8)
        small = small.transpose(1, 0, 2)
        small = jnp.pad(small, ((0, 0), (0, extra - small.shape[1]), (0, wide - small.shape[2])))
        head = as_gathered(jnp.concatenate([small, head_part], axis=1), extra + features // 16)
        tail_part = lax.all_gather(tail_part, "grp", axis=0, tiled=True)
        tail = as_gathered(tail_part.reshape(8, -1, 3 * features), features // 16)

    act, small, w_head, joint_head, prob_head, mixed_head = attend(
        True, images, places, order, source, head, wide
    )
    if direct:
        tail_second = after(gather_second(tail_join), mixed_head)
        tail = gather_last((t0, t1), tail_first, tail_second)
    w_out, w_tail, joint_tail, prob_tail, mixed_tail = attend(
        False, images, places, order, act, tail, 2 * wide
    )
    mixes = [mixed_head, mixed_tail]
    resid, logits, *leaving = route(
        images, places, experts, slot_rows, order, source, cot, mixes, w_out, small
    )

    arrived = [leaving[0]] + [swap(leaving[k], "grp", group, 2 * k) for k in range(1, experts)]
    arrived = arrived + [swap(part, "grp", group, 1) for part in arrived]
    piece_in, piece_out = expert_in[0], expert_out[0]
    received, kept, given = expert(images, piece_in, piece_out, arrived)
    both = pair_sum(kept, [swap(given, "grp", group, 1)], experts)
    summed = [both[0]] + [swap(both[k], "grp", group, 2 * k) for k in range(1, experts)]
    received = after(received, *summed)
    far = [swap(received, "rep", reps, k) for k in range(1, reps)]
    output, att, grad_mixed, grad_out, grad_side = back(
        images, places, experts, order, resid, logits, cot, mixes, w_out, small, summed
    )
    grad_mixed, far = lax.optimization_barrier((grad_mixed, far))
    grad_joint_tail, keep_tail, give_tail = attend_back(
        images, part, order, joint_tail, prob_tail, grad_mixed, mixed_tail, act, (2, 2), (grad_out, grad_side)
    )
    if direct:
        sums = pair_sum(keep_tail, [swap(give_tail, "grp", group, 1)], 4)
        others = [swap(sums[k], "grp", group, 2 * k) for k in range(1, 4)]
        grad_mixed = after(grad_mixed, *sums)
    grad_joint_head, keep_head, *give_head = attend_back(
        images, 0, order, joint_head, prob_head, grad_mixed, mixed_head, act, (2, 4, 4)
    )
    joints, weights = [grad_joint_head, grad_joint_tail], [w_head, w_tail]
    every = [received] + far
    if direct:
        got = [swap(part, "grp", group, 1) for part in give_head]
        own, others = after((sums[0], others), got)
        mine, give = split_sum(order, own, *others)
        other = swap(give, "rep", reps, 1)
        sums = pair_sum(keep_head, got, 4)
        others = [swap(sums[k], "grp", group, 2 * k) for k in range(1, 4)]
        att = after(att, mine, *sums)
        token_grad = finish(images, places, source, att, joints, weights, small)
        own, others, other = after((sums[0], others, other), token_grad)
        tail_sum = total_sum(mine, other)
        head_sum = total_sum(own, *others)
        every, tail_sum, head_sum = after((every, tail_sum, head_sum), token_grad)
        tail_other = swap(tail_sum, "rep", reps, 2)
        head_other = swap(head_sum, "rep", reps, 1)
        expert_in_grad, expert_out_grad = expert_grad(every, piece_in, piece_out)
        tail_other, head_other = after((tail_other, head_other), expert_in_grad)
        tail_sum, head_sum = total_sum(tail_sum, tail_other), total_sum(head_sum, head_other)
        tail_other = swap(tail_sum, "rep", reps, 1)
        head_other = swap(head_sum, "rep", reps, 3)
        heads_in_grad, heads_out_grad, router_grad, gain_one_grad, gain_two_grad = shares(
            experts, order, head_sum, head_other, tail_sum, tail_other, heads_in, first_gain[None]
        )
        gain_one_grad, gain_two_grad = gain_one_grad[0], gain_two_grad[0]
    else:
        token_grad = finish(images, places, source, att, joints, weights, small)
        expert_in_grad, expert_out_grad = expert_grad(every, piece_in, piece_out)
        tail_sum = jnp.concatenate([keep_tail, give_tail])
        tail_sum = lax.psum_scatter(tail_sum, "grp", scatter_dimension=0, tiled=True)
        head_sum = jnp.concatenate([keep_head, *give_head])
        head_sum = lax.psum_scatter(head_sum, "grp", scatter_dimension=0, tiled=True)
        tail_sum = lax.psum(tail_sum, "rep").astype(F32)
        head_sum = lax.psum(head_sum, "rep").astype(F32)
        columns = []
        for k in range(3):
            columns.append(head_sum[:, k * part : (k + 1) * part])
            columns.append(tail_sum[:, 2 * k * part : 2 * (k + 1) * part])
        heads_in_grad = jnp.concatenate(columns, axis=1)
        gain_one_grad = jnp.sum(heads_in_grad * heads_in.astype(F32), axis=1)
        gain_one_grad = gain_one_grad / first_gain.astype(F32)
        heads_out_grad, rest = tail_sum[:, 2 * wide : 3 * wide], tail_sum[:, 3 * wide :]
        router_grad, gain_two_grad = rest[:, :experts], rest[:, experts]
    return (
        output,
        token_grad,
        heads_in_grad,
        heads_out_grad,
        router_grad,
        gain_one_grad,
        gain_two_grad,
        expert_in_grad[None],
        expert_out_grad[None],
    )


def solution(mesh):
    token_spec = P(("rep", "grp"), None, None)
    matrix, vector, stack = P("grp", None), P("grp"), P("grp", None, None)
    return jax.shard_map(
        per_device,
        mesh=mesh,
        in_specs=(token_spec, token_spec, matrix, matrix, matrix, vector, vector, stack, stack),
        out_specs=(token_spec, token_spec, matrix, matrix, matrix, vector, vector, stack, stack),
        check_vma=False,
    )
```

```python
import functools

import jax
import jax.numpy as jnp
from jax import lax
from jax.experimental import pallas as pl
from jax.experimental.pallas import tpu as pltpu
from jax.sharding import PartitionSpec as P

HEADS = 12
LANES = 128
F32 = jnp.float32
BF16 = jnp.bfloat16
LOW = -1e30

NN = (((1,), (0,)), ((), ()))
NT = (((1,), (1,)), ((), ()))
TN = (((0,), (0,)), ((), ()))


def dot(left, right, form=NN):
    return lax.dot_general(left, right, form, preferred_element_type=F32)


def swap(values, axis, size, bit):
    return lax.ppermute(values, axis, [(place, place ^ bit) for place in range(size)])


def after(values, *others):
    return lax.optimization_barrier((values, others))[0]


def gather_first(own):
    return swap(own[0], "grp", 8, 2), swap(own[1], "grp", 8, 4)


def gather_second(joined):
    return swap(joined[0], "grp", 8, 4), swap(joined[1], "grp", 8, 2)


def gather_last(*stages):
    held = tuple(part for stage in stages for part in stage)
    return held + tuple(swap(part, "grp", 8, 1) for part in held)


def as_gathered(blocks, cut):
    held = []
    for k in range(2):
        own, x, y, far = blocks[k], blocks[k + 2], blocks[k + 4], blocks[k + 6]
        held += [own[:cut], own[cut:], x[:cut], y[cut:]]
        held += [jnp.concatenate([y[:cut], far[:cut]]), jnp.concatenate([x[cut:], far[cut:]])]
    return tuple(held)


def iota(shape, axis):
    return lax.broadcasted_iota(jnp.int32, shape, axis)


def normalize(values):
    center = values - jnp.mean(values, axis=-1, keepdims=True)
    factor = lax.rsqrt(jnp.mean(center * center, axis=-1, keepdims=True) + 1e-06)
    return center * factor, factor


def norm_back(scaled, normed, factor):
    inner = (
        scaled
        - jnp.mean(scaled, axis=-1, keepdims=True)
        - normed * jnp.mean(scaled * normed, axis=-1, keepdims=True)
    )
    return factor * inner


def pieces_of(rows, extra):
    half = rows // 2
    cut = extra + half
    for core in range(2):
        base = 6 * core
        yield base, extra, core, 0
        yield base + 1, 0, core, half
        yield base + 2, extra, core + 2, 0
        yield base + 3, 0, core + 4, half
        yield base + 4, extra, core + 4, 0
        yield base + 4, cut + extra, core + 6, 0
        yield base + 5, 0, core + 2, half
        yield base + 5, half, core + 6, half


def place_pieces(order_ref, pieces, rows, extra, target, columns):
    half = rows // 2
    for n, start, block, offset in pieces_of(rows, extra):
        place = pl.multiple_of(order_ref[block] * rows + offset, 16)
        target[pl.ds(place, half), :] = pieces[n][start : start + half, columns]


def store_blocks(order_ref, source, targets, columns):
    rows = source.shape[0] // 8
    n = 0
    for target in targets:
        for k in range(target.shape[0] // rows):
            start = pl.multiple_of(order_ref[8 + n] * rows, 32)
            target[k * rows : (k + 1) * rows, columns] = source[pl.ds(start, rows), :].astype(BF16)
            n += 1


def gather_small(order_ref, pieces, rows, extra, small_ref):
    total = jnp.zeros(small_ref.shape, F32)
    lane = iota((LANES, small_ref.shape[1]), 0)
    place = iota((LANES, small_ref.shape[1]), 1)
    cut = extra + rows // 2
    for core in range(2):
        for n, start, block in ((0, 0, 0), (2, 0, 2), (4, 0, 4), (4, cut, 6)):
            held = pieces[6 * core + n][start : start + extra, :LANES]
            fits = (place == order_ref[block + core] * rows + lane) & (lane < rows)
            total = total + dot(held, jnp.where(fits, 1.0, 0.0).astype(BF16))
    small_ref[...] = total


def rows_of(place, tall):
    return pl.ds(pl.multiple_of(place * tall, 16), tall)


VM = pl.BlockSpec(memory_space=pltpu.VMEM)
SM = pl.BlockSpec(memory_space=pltpu.SMEM)


def call(body, name, inputs, outputs, scratch, limit, flops, hbm=()):
    return pl.pallas_call(
        body,
        in_specs=[SM if x.dtype == jnp.int32 else VM for x in inputs],
        out_specs=[VM] * len(outputs),
        out_shape=[
            jax.ShapeDtypeStruct(shape, kind) if n in hbm else pltpu.VMEM(shape, kind)
            for n, (shape, kind) in enumerate(outputs)
        ],
        scratch_shapes=[pltpu.VMEM(shape, kind) for shape, kind in scratch],
        compiler_params=pltpu.CompilerParams(vmem_limit_bytes=limit * 1024 * 1024),
        cost_estimate=pl.CostEstimate(flops=int(flops), bytes_accessed=1000000, transcendentals=0),
        name=name,
    )(*inputs)


def prepare_body(in_ref, out_ref, router_ref, gains_ref, h0, h1, t0, t1):
    rows, features = out_ref.shape
    half = rows // 2
    experts = router_ref.shape[1]
    part = features // 3
    extra = h0.shape[0] - half
    gains = gains_ref[...].astype(F32)
    router = router_ref[...].astype(F32)
    router = jnp.concatenate([router, jnp.zeros((rows, LANES - experts), F32)], axis=1).T
    small = jnp.concatenate([gains, router[: extra - 2]], axis=0)
    small = jnp.concatenate([small, jnp.zeros((extra, LANES - rows), F32)], axis=1)
    h0[:extra, :] = jnp.zeros((extra, h0.shape[1]), BF16)
    h0[:extra, :LANES] = small.astype(BF16)
    for head, tail, start, here in ((h0, t0, extra, slice(0, half)), (h1, t1, 0, slice(half, rows))):
        for k in range(3):
            base = k * features
            head[start:, k * part : (k + 1) * part] = in_ref[here, base : base + part]
            tail[:, 2 * k * part : 2 * (k + 1) * part] = in_ref[here, base + part : base + features]
        tail[:, 2 * features :] = out_ref[here, :]


def prepare(heads_in, heads_out, router, gains):
    rows, features = heads_out.shape
    extra = -(-(router.shape[1] + 2) // 16) * 16
    return call(
        prepare_body,
        "prepare",
        (heads_in, heads_out, router, gains),
        [
            ((extra + rows // 2, features), BF16),
            ((rows // 2, features), BF16),
            ((rows // 2, 3 * features), BF16),
            ((rows // 2, 3 * features), BF16),
        ],
        [],
        4,
        1e6,
    )


def join_body(a0, a1, b0, b1, a_ref, b_ref):
    for first, second, target in ((a0, a1, a_ref), (b0, b1, b_ref)):
        target[: first.shape[0], :] = first[...]
        target[first.shape[0] :, :] = second[...]


def join(own, got):
    outputs = [((2 * x.shape[0], x.shape[1]), BF16) for x in own]
    return call(join_body, "join", (own[0], got[0], own[1], got[1]), outputs, [], 4, 1e6)


def attend_body(first, images, places, order_ref, source_ref, *refs):
    pieces, refs = refs[:12], refs[12:]
    features = source_ref.shape[1]
    rows = features // 8
    if first:
        act_ref, small_ref, weight, joint_ref, prob_ref, mixed_ref = refs
        extra = small_ref.shape[0]
    else:
        out_weight, weight, joint_ref, prob_ref, mixed_ref = refs
        act_ref = source_ref
        extra = 0
    tall = source_ref.shape[0] // images
    width = weight.shape[1]
    place_pieces(order_ref, pieces, rows, extra, weight, slice(0, width))
    if first:
        gather_small(order_ref, pieces, rows, extra, small_ref)

        for i in range(images):
            here = rows_of(i, tall)
            normed, _ = normalize(source_ref[here, :].astype(F32))
            act_ref[here, :] = (normed * small_ref[0:1, :]).astype(BF16)
    else:
        place_pieces(order_ref, pieces, rows, 0, out_weight, slice(width, width + features))

    for i in range(images // 2):
        here = rows_of(i, 2 * tall)
        joint_ref[here, :] = dot(act_ref[here, :], weight[...]).astype(BF16)

    third = width // 3
    heads = prob_ref.shape[0] // images
    low = iota((tall, LANES), 1) < LANES // 2
    inside = iota((tall, LANES), 0) < places
    seen = iota((tall, tall), 1) < places

    for i in range(images):
        here = slice(i * tall, (i + 1) * tall)
        for pair in range(third // LANES):
            query, keys, values = (
                joint_ref[here, part * third + pair * LANES : part * third + (pair + 1) * LANES]
                for part in range(3)
            )
            query = query * 0.125
            values_ones = jnp.concatenate([values, jnp.ones_like(values)], axis=1)
            outs = []
            for side in range(2):
                mine = low if side == 0 else ~low
                scores = dot(jnp.where(mine, query, 0), keys, NT)
                scores = jnp.where(seen, scores, LOW)
                power = jnp.exp(scores - jnp.max(scores, axis=1, keepdims=True)).astype(BF16)
                got = dot(power, values_ones)
                shrink = 1.0 / got[:, LANES:]
                outs.append(got[:, :LANES] * shrink)
                shrink = jnp.concatenate([shrink, shrink[:, : tall - LANES]], axis=1)
                prob_ref[i * heads + 2 * pair + side] = (power.astype(F32) * shrink).astype(BF16)
            mixed = jnp.where(inside, jnp.where(low, outs[0], outs[1]), 0.0)
            mixed_ref[here, pair * LANES : (pair + 1) * LANES] = mixed.astype(BF16)


def attend(first, images, places, order, source, pieces, width):
    total, features = source.shape
    tall = total // images
    heads = width // 3 // 64
    extra = pieces[0].shape[0] - features // 16
    outputs = [
        ((features, width), BF16),
        ((total, width), BF16),
        ((images * heads, tall, tall), BF16),
        ((total, width // 3), BF16),
    ]
    if first:
        outputs = [((total, features), BF16), ((extra, features), F32)] + outputs
    else:
        outputs = [((features, features), BF16)] + outputs
    return call(
        functools.partial(attend_body, first, images, places),
        "attend",
        (order, source, *pieces),
        outputs,
        [],
        12,
        2 * total * features * width * 2,
    )


def softmaxes(logits, places, experts):
    rows = iota(logits.shape, 0) < experts
    lanes = iota(logits.shape, 1) < places
    wide = jnp.where(lanes, logits, LOW)
    wide = jnp.exp(wide - jnp.max(wide, axis=1, keepdims=True))
    dispatch = wide / jnp.sum(wide, axis=1, keepdims=True)
    tall = jnp.where(rows, logits, LOW)
    tall = jnp.exp(tall - jnp.max(tall, axis=0, keepdims=True))
    combine = tall / jnp.sum(tall, axis=0, keepdims=True)
    return jnp.where(rows, dispatch, 0.0), combine


def slot_rows_of(experts, order_ref, small_ref, slots):
    rows = small_ref.shape[0]
    slot, row = iota((slots, rows), 0), iota((slots, rows), 1)
    chip = order_ref[order_ref.shape[0] - 1]
    fits = (row == (slot ^ chip) + 2) & (slot < experts)
    return dot(jnp.where(fits, 1.0, 0.0).astype(BF16), small_ref[...].astype(BF16)).astype(BF16)


def pick_rows(shape, wanted):
    row, column = iota(shape, 0), iota(shape, 1)
    return jnp.where(column == wanted(row), 1.0, 0.0).astype(BF16)


def route_body(
    images, places, experts, order_ref, token_ref, cot_ref, m0, m1, weight, small_ref,
    resid_ref, logit_ref, *refs,
):
    out_refs, packed_ref = refs[:-1], refs[-1]
    slots = logit_ref.shape[0] // images
    router = slot_rows_of(experts, order_ref, small_ref, slots)
    tall = token_ref.shape[0] // images
    features = token_ref.shape[1]

    for i in range(images // 2):
        here = rows_of(i, 2 * tall)
        mixed = jnp.concatenate([m0[here, :], m1[here, :]], axis=1)
        resid_ref[here, :] = token_ref[here, :].astype(F32) + dot(mixed, weight[...])

    for i in range(images):
        here = rows_of(i, tall)
        normed, _ = normalize(resid_ref[here, :])
        act = (normed * small_ref[1:2, :]).astype(BF16)
        logits = dot(router, act, NT)
        group = rows_of(i, slots)
        logit_ref[group, :] = logits
        dispatch, combine = softmaxes(logits, places, experts)
        packed_ref[group, :features] = dot(dispatch.astype(BF16), act).astype(BF16)
        packed_ref[group, features:] = dot(combine.astype(BF16), cot_ref[here, :]).astype(BF16)

    high = out_refs[0].shape[0]
    pick = pick_rows(
        (experts * high, images * slots),
        lambda n: jnp.where(n % high < images, n % high * slots + n // high, -1),
    )
    packed = dot(pick, packed_ref[...]).astype(BF16)
    for k, out_ref in enumerate(out_refs):
        out_ref[...] = packed[k * high : (k + 1) * high, :]


def route(images, places, experts, slots, order, tokens, cot, mixed, w, small):
    total, features = tokens.shape
    high = -(-images // 8) * 8
    return call(
        functools.partial(route_body, images, places, experts),
        "route",
        (order, tokens, cot, *mixed, w, small),
        [((total, features), F32), ((images * slots, total // images), F32)]
        + [((high, 2 * features), BF16)] * experts,
        [((images * slots, 2 * features), BF16)],
        10,
        4 * total * features * features,
    )


def gelu_parts(values):
    scale, cubic = 0.7978845608028654, 0.044715
    square = values * values
    bent = jnp.tanh(scale * values * (1.0 + cubic * square))
    half = 0.5 * (1.0 + bent)
    slope = half + 0.5 * values * (1.0 - bent * bent) * scale * (1.0 + 3.0 * cubic * square)
    return values * half, slope


def expert_body(count, images, in_ref, out_ref, *refs):
    sources, (packed_ref, keep_ref, give_ref, rows_ref, back_ref) = refs[:count], refs[count:]
    features = in_ref.shape[0]
    high = sources[0].shape[0]
    for k, source in enumerate(sources):
        rows_ref[k * high : (k + 1) * high, :] = source[...]
    rows, arriving = rows_ref[:, :features], rows_ref[:, features:]
    total = jnp.zeros((rows.shape[0], features), F32)
    grad_total = total
    step = 512
    for start in range(0, in_ref.shape[1], step):
        w_in = in_ref[:, start : start + step]
        w_out = out_ref[start : start + step, :]
        hidden, slope = gelu_parts(dot(rows, w_in))
        grad_pre = (dot(arriving, w_out, NT) * slope).astype(BF16)
        total = total + dot(hidden.astype(BF16), w_out)
        grad_total = grad_total + dot(grad_pre, w_in, NT)
    back_ref[:, :features] = total.astype(BF16)
    back_ref[:, features:] = grad_total.astype(BF16)
    half = keep_ref.shape[0]
    keep_ref[...] = back_ref[:half, :]
    give_ref[...] = back_ref[half:, :]
    pick = pick_rows(
        (packed_ref.shape[0], rows_ref.shape[0]), lambda n: n // images * high + n % images
    )
    packed_ref[...] = dot(pick, rows_ref[...]).astype(BF16)


def expert(images, piece_in, piece_out, sources):
    high, wide = sources[0].shape
    rows = high * len(sources)
    return call(
        functools.partial(expert_body, len(sources), images),
        "expert",
        (piece_in, piece_out, *sources),
        [
            ((images * len(sources), wide), BF16),
            ((rows // 2, wide), BF16),
            ((rows // 2, wide), BF16),
        ],
        [((rows, wide), BF16)] * 2,
        8,
        1e9,
    )


def pair_sum_body(parts, keep_ref, *refs):
    got_refs, out_refs = refs[:parts], refs[parts:]
    rows = out_refs[0].shape[0]
    each = len(out_refs) // parts
    for k, out_ref in enumerate(out_refs):
        kept = keep_ref[k * rows : (k + 1) * rows, :].astype(F32)
        got = got_refs[k // each][k % each * rows : (k % each + 1) * rows, :].astype(F32)
        out_ref[...] = (kept + got).astype(BF16)


def pair_sum(keep, got, count):
    shape = (keep.shape[0] // count, keep.shape[1])
    body = functools.partial(pair_sum_body, len(got))
    return call(body, "pair_sum", (keep, *got), [(shape, BF16)] * count, [], 4, 1e6)


def total_body(*refs):
    refs[-1][...] = sum(ref[...].astype(F32) for ref in refs[:-1]).astype(BF16)


def total_sum(*terms):
    return call(total_body, "total_sum", terms, [(terms[0].shape, BF16)], [], 4, 1e6)[0]


def split_sum_body(order_ref, *refs):
    terms, (mine_ref, give_ref, scratch) = refs[:-3], refs[-3:]
    scratch[...] = sum(ref[...].astype(F32) for ref in terms)
    half = mine_ref.shape[0]
    odd = order_ref[order_ref.shape[0] - 2]
    mine = pl.multiple_of(odd * half, 16)
    other = pl.multiple_of((1 - odd) * half, 16)
    mine_ref[...] = scratch[pl.ds(mine, half), :].astype(BF16)
    give_ref[...] = scratch[pl.ds(other, half), :].astype(BF16)


def split_sum(order, *terms):
    rows, wide = terms[0].shape
    shape = (rows // 2, wide)
    return call(
        split_sum_body, "split_sum", (order, *terms), [(shape, BF16)] * 2, [((rows, wide), F32)], 8, 1e6
    )


def shares_body(
    experts, order_ref, head_ref, head_other, tail_ref, tail_other, w_ref, gain_ref,
    in_ref, out_ref, router_ref, gain_one_ref, gain_two_ref, tail,
):
    rows, features = out_ref.shape
    half = rows // 2
    odd = order_ref[order_ref.shape[0] - 2]
    tail[pl.ds(pl.multiple_of(odd * half, 16), half), :] = tail_ref[...].astype(F32)
    tail[pl.ds(pl.multiple_of((1 - odd) * half, 16), half), :] = tail_other[...].astype(F32)
    part = features // 3
    for k in range(3):
        here = slice(k * part, (k + 1) * part)
        in_ref[:, k * features : k * features + part] = (
            head_ref[:, here].astype(F32) + head_other[:, here].astype(F32)
        )
        in_ref[:, k * features + part : (k + 1) * features] = tail[:, 2 * k * part : 2 * (k + 1) * part]
    out_ref[...] = tail[:, 2 * features : 3 * features]
    rest = tail[:, 3 * features :]
    router_ref[...] = rest[:, :experts]
    gain_two_ref[...] = rest.T[experts : experts + 1, :]
    gain_one = jnp.sum(in_ref[...] * w_ref[...].astype(F32), axis=1, keepdims=True)
    gain_one = jnp.broadcast_to(gain_one, (rows, LANES)).T[:1, :]
    gain_one_ref[...] = gain_one / gain_ref[...].astype(F32)


def shares(experts, order, head, head_other, tail, tail_other, w, gain):
    rows, features = head.shape
    return call(
        functools.partial(shares_body, experts),
        "shares",
        (order, head, head_other, tail, tail_other, w, gain),
        [
            (w.shape, F32),
            ((rows, features), F32),
            ((rows, experts), F32),
            ((1, rows), F32),
            ((1, rows), F32),
        ],
        [((rows, tail.shape[1]), F32)],
        8,
        1e6,
        hbm=range(5),
    )


def expert_grad_body(count, *refs):
    sources, (in_ref, out_ref, grad_in_ref, grad_out_ref) = refs[:count], refs[count:]
    features = in_ref.shape[0]
    every = jnp.concatenate([source[...] for source in sources], axis=0)
    rows, arriving = every[:, :features], every[:, features:]
    hidden, slope = gelu_parts(dot(rows, in_ref[...]))
    grad_pre = (dot(arriving, out_ref[...], NT) * slope).astype(BF16)
    grad_in_ref[...] = dot(rows, grad_pre, TN)
    grad_out_ref[...] = dot(hidden.astype(BF16), arriving, TN)


def expert_grad(sources, piece_in, piece_out):
    features, hidden = piece_in.shape
    step = 256
    wide = pl.BlockSpec((features, step), lambda i: (0, i))
    high = pl.BlockSpec((step, features), lambda i: (i, 0))
    return pl.pallas_call(
        functools.partial(expert_grad_body, len(sources)),
        grid=(hidden // step,),
        in_specs=[pl.BlockSpec(x.shape, lambda i: (0, 0)) for x in sources] + [wide, high],
        out_specs=[wide, high],
        out_shape=[
            jax.ShapeDtypeStruct(piece_in.shape, F32),
            jax.ShapeDtypeStruct(piece_out.shape, F32),
        ],
        compiler_params=pltpu.CompilerParams(vmem_limit_bytes=16 * 1024 * 1024),
        cost_estimate=pl.CostEstimate(
            flops=1600 * piece_in.size, bytes_accessed=14000000, transcendentals=0
        ),
        name="expert_grad",
    )(*sources, piece_in, piece_out)


def back_body(
    images, places, experts, order_ref, resid_ref, logit_ref, cot_ref, m0, m1, weight, small_ref, *refs
):
    sources, refs = refs[:experts], refs[experts:]
    output_ref, att_ref, grad_mixed_ref, grad_w_ref, grad_side_ref, summed_ref = refs
    slots = logit_ref.shape[0] // images
    router = slot_rows_of(experts, order_ref, small_ref, slots)
    total, features = resid_ref.shape
    tall = total // images
    gain = small_ref[1:2, :]
    high = sources[0].shape[0]
    pick = pick_rows(
        (images * slots, experts * high),
        lambda n: jnp.where(n % slots < experts, n % slots * high + n // slots, -1),
    )
    arrived = jnp.concatenate([source[...] for source in sources], axis=0)
    summed_ref[...] = dot(pick, arrived).astype(BF16)

    def image(i, carry):
        side, gain_sum = carry
        here = rows_of(i, tall)
        group = rows_of(i, slots)
        expert_sum, grad_slots = summed_ref[group, :features], summed_ref[group, features:]
        resid = resid_ref[here, :]
        cot = cot_ref[here, :]
        dispatch, combine = softmaxes(logit_ref[group, :], places, experts)
        output = resid + dot(combine.astype(BF16), expert_sum, TN)
        output_ref[i] = output[:places].astype(BF16)
        normed, factor = normalize(resid)
        act = (normed * gain).astype(BF16)
        grad_comb = dot(expert_sum, cot, NT)
        grad_disp = dot(grad_slots, act, NT)
        grad_logits = combine * (grad_comb - jnp.sum(grad_comb * combine, axis=0, keepdims=True))
        grad_logits = grad_logits + dispatch * (
            grad_disp - jnp.sum(grad_disp * dispatch, axis=1, keepdims=True)
        )
        grad_logits = grad_logits.astype(BF16)
        grad_act = dot(
            jnp.concatenate([dispatch.astype(BF16), grad_logits], axis=0),
            jnp.concatenate([grad_slots, router], axis=0),
            TN,
        )
        att = cot.astype(F32) + norm_back(grad_act * gain, normed, factor)
        att_ref[here, :] = att.astype(BF16)
        return (
            side + dot(grad_logits, act),
            gain_sum + jnp.sum(grad_act * normed, axis=0, keepdims=True),
        )

    carry = (jnp.zeros((slots, features), F32), jnp.zeros((1, features), F32))
    for i in range(images):
        carry = image(i, carry)
    side, gain_sum = carry

    for i in range(images // 2):
        here = rows_of(i, 2 * tall)
        grad_mixed_ref[here, :] = dot(att_ref[here, :], weight[...], NT).astype(BF16)

    part = m0.shape[1]
    grad_w_ref[:part, :] = dot(m0[...], att_ref[...], TN).astype(BF16)
    grad_w_ref[part:, :] = dot(m1[...], att_ref[...], TN).astype(BF16)
    slot = iota((LANES, slots), 0) ^ order_ref[order_ref.shape[0] - 1]
    slot = jnp.where(iota((LANES, slots), 0) < experts, slot, -1)
    fits = jnp.where(slot == iota((LANES, slots), 1), 1.0, 0.0).astype(BF16)
    side = dot(fits, side.astype(BF16))
    side = jnp.where(iota(side.shape, 0) == experts, gain_sum, side)
    grad_side_ref[...] = side.T.astype(BF16)


def back(images, places, experts, order, resid, logits, cot, mixed, w, small, sources):
    total, features = resid.shape
    return call(
        functools.partial(back_body, images, places, experts),
        "back",
        (order, resid, logits, cot, *mixed, w, small, *sources),
        [
            ((images, places, features), BF16),
            ((total, features), BF16),
            ((total, features), BF16),
            ((features, features), BF16),
            ((features, LANES), BF16),
        ],
        [((logits.shape[0], 2 * features), BF16)],
        14,
        8 * total * features * features,
        hbm=(0,),
    )


def attend_back_body(images, extra, offset, order_ref, joint_ref, prob_ref, grad_ref, mixed_ref, act_ref, *refs):
    more, (out_ref, *targets, total) = refs[:extra], refs[extra:]
    width = joint_ref.shape[1]
    tall = joint_ref.shape[0] // images
    third = width // 3
    heads = prob_ref.shape[0] // images
    low = iota((tall, LANES), 1) < LANES // 2

    for i in range(images):
        here = slice(i * tall, (i + 1) * tall)
        for pair in range(third // LANES):
            query, keys, values = (
                joint_ref[here, part * third + pair * LANES : part * third + (pair + 1) * LANES]
                for part in range(3)
            )
            grad = grad_ref[here, offset + pair * LANES : offset + (pair + 1) * LANES]
            product = grad.astype(F32) * mixed_ref[
                here, pair * LANES : (pair + 1) * LANES
            ].astype(F32)
            query_high, grad_high = query.T, grad.T
            grad_query, grad_keys, grad_values = [], [], []
            for side in range(2):
                mine = low if side == 0 else ~low
                rows = slice(side * LANES // 2, (side + 1) * LANES // 2)
                prob = prob_ref[i * heads + 2 * pair + side]
                inner = jnp.sum(jnp.where(mine, product, 0.0), axis=1, keepdims=True)
                grad_prob = dot(jnp.where(mine, grad, 0), values, NT)
                grad_scores = (prob.astype(F32) * (grad_prob - inner)).astype(BF16)
                grad_query.append(dot(grad_scores, keys))
                grad_keys.append(dot(query_high[rows], grad_scores))
                grad_values.append(dot(grad_high[rows], prob))
            joined = (
                (jnp.where(low, *grad_query) * 0.125).astype(BF16),
                (jnp.concatenate(grad_keys, axis=0) * 0.125).astype(BF16).T,
                jnp.concatenate(grad_values, axis=0).astype(BF16).T,
            )
            for part in range(3):
                out_ref[
                    here, part * third + pair * LANES : part * third + (pair + 1) * LANES
                ] = joined[part]

    step = third
    for start in range(0, width, step):
        total[:, start : start + step] = dot(
            act_ref[...], out_ref[:, start : start + step], TN
        ).astype(BF16)
    store_blocks(order_ref, total, targets, slice(0, width))
    place = width
    for source in more:
        end = place + source.shape[1]
        store_blocks(order_ref, source, targets, slice(place, end))
        place = end


def attend_back(images, offset, order, joint, prob, grad_mixed, mixed, act, splits, more=()):
    total, width = joint.shape
    features = act.shape[1]
    columns = width + sum(m.shape[1] for m in more)
    parts = [((features // n, columns), BF16) for n in splits]
    return call(
        functools.partial(attend_back_body, images, len(more), offset),
        "attend_back",
        (order, joint, prob, grad_mixed, mixed, act, *more),
        [(joint.shape, BF16)] + parts,
        [((features, width), BF16)],
        16,
        2 * total * features * width * 4,
    )


def finish_body(images, places, token_ref, att_ref, j0, j1, s0, s1, small_ref, out_ref):
    total, features = token_ref.shape
    tall = total // images

    for i in range(images // 2):
        here = rows_of(i, 2 * tall)
        grad_act = dot(j0[here, :], s0[...], NT) + dot(j1[here, :], s1[...], NT)
        normed, factor = normalize(token_ref[here, :].astype(F32))
        result = att_ref[here, :].astype(F32)
        result = result + norm_back(grad_act * small_ref[0:1, :], normed, factor)
        result = result.astype(BF16)
        out_ref[2 * i] = result[:places]
        out_ref[2 * i + 1] = result[tall : tall + places]


def finish(images, places, tokens, att, joints, weights, small):
    total, features = tokens.shape
    return call(
        functools.partial(finish_body, images, places),
        "finish",
        (tokens, att, *joints, *weights, small),
        [((images, places, features), BF16)],
        [],
        12,
        6 * total * features * features,
        hbm=(0,),
    )[0]


def per_device(
    tokens, cotangent, heads_in, heads_out, slot_router, first_gain, second_gain, expert_in, expert_out
):
    images, places, features = tokens.shape
    experts = slot_router.shape[1]
    group = lax.axis_size("grp")
    reps = lax.axis_size("rep")
    me = lax.axis_index("grp")
    own_rows = heads_in.shape[0]
    chip = me // 2
    odd = lax.axis_index("rep") % 2
    direct = group == 8
    ways = jnp.arange(8, dtype=jnp.int32)
    if direct:
        order = jnp.concatenate([ways ^ me, (ways % 4 * 2 + ways // 4) ^ me, odd[None], chip[None]])
    else:
        order = jnp.concatenate([ways, ways, odd[None], chip[None]])
    tall = -(-places // 16) * 16
    slot_rows = -(-experts // 16) * 16
    part = features // 3
    wide = 3 * part

    grow = ((0, 0), (0, tall - places), (0, 0))
    source = jnp.pad(tokens, grow).reshape(images * tall, features)
    cot = jnp.pad(cotangent, grow).reshape(images * tall, features)
    gains = jnp.stack([first_gain, second_gain])
    if direct:
        h0, h1, t0, t1 = prepare(heads_in, heads_out, slot_router, gains)
        head_first = gather_first((h0, h1))
        head_first = after(head_first, source, cot)
        (t0, t1), head_first = lax.optimization_barrier(((t0, t1), head_first))
        head_second = gather_second(join((h0, h1), head_first))
        tail_first = gather_first((t0, t1))
        head = gather_last((h0, h1), head_first, head_second)
        tail_first = after(tail_first, *head)
        tail_join = join((t0, t1), tail_first)
        source = after(source, *tail_join)
    else:
        thirds = [heads_in[:, k * features : (k + 1) * features] for k in range(3)]
        head_part = jnp.concatenate([t[:, :part] for t in thirds], axis=1)
        tail_part = jnp.concatenate([t[:, part:] for t in thirds] + [heads_out], axis=1)
        small = jnp.concatenate([gains, slot_router.T], axis=0)
        extra = -(-small.shape[0] // 16) * 16
        head_part = lax.all_gather(head_part, "grp", axis=0, tiled=True).reshape(8, -1, wide)
        small = lax.all_gather(small, "grp", axis=1, tiled=True).reshape(-1, 8, features // 8)
        small = small.transpose(1, 0, 2)
        small = jnp.pad(small, ((0, 0), (0, extra - small.shape[1]), (0, wide - small.shape[2])))
        head = as_gathered(jnp.concatenate([small, head_part], axis=1), extra + features // 16)
        tail_part = lax.all_gather(tail_part, "grp", axis=0, tiled=True)
        tail = as_gathered(tail_part.reshape(8, -1, 3 * features), features // 16)

    act, small, w_head, joint_head, prob_head, mixed_head = attend(
        True, images, places, order, source, head, wide
    )
    if direct:
        tail_second = after(gather_second(tail_join), mixed_head)
        tail = gather_last((t0, t1), tail_first, tail_second)
    w_out, w_tail, joint_tail, prob_tail, mixed_tail = attend(
        False, images, places, order, act, tail, 2 * wide
    )
    mixes = [mixed_head, mixed_tail]
    resid, logits, *leaving = route(
        images, places, experts, slot_rows, order, source, cot, mixes, w_out, small
    )

    arrived = [leaving[0]] + [swap(leaving[k], "grp", group, 2 * k) for k in range(1, experts)]
    arrived = arrived + [swap(part, "grp", group, 1) for part in arrived]
    piece_in, piece_out = expert_in[0], expert_out[0]
    received, kept, given = expert(images, piece_in, piece_out, arrived)
    both = pair_sum(kept, [swap(given, "grp", group, 1)], experts)
    summed = [both[0]] + [swap(both[k], "grp", group, 2 * k) for k in range(1, experts)]
    received = after(received, *summed)
    far = [swap(received, "rep", reps, k) for k in range(1, reps)]
    output, att, grad_mixed, grad_out, grad_side = back(
        images, places, experts, order, resid, logits, cot, mixes, w_out, small, summed
    )
    grad_mixed, far = lax.optimization_barrier((grad_mixed, far))
    grad_joint_tail, keep_tail, give_tail = attend_back(
        images, part, order, joint_tail, prob_tail, grad_mixed, mixed_tail, act, (2, 2), (grad_out, grad_side)
    )
    if direct:
        sums = pair_sum(keep_tail, [swap(give_tail, "grp", group, 1)], 4)
        others = [swap(sums[k], "grp", group, 2 * k) for k in range(1, 4)]
        grad_mixed = after(grad_mixed, *sums)
    grad_joint_head, keep_head, *give_head = attend_back(
        images, 0, order, joint_head, prob_head, grad_mixed, mixed_head, act, (2, 4, 4)
    )
    joints, weights = [grad_joint_head, grad_joint_tail], [w_head, w_tail]
    every = [received] + far
    if direct:
        got = [swap(part, "grp", group, 1) for part in give_head]
        own, others = after((sums[0], others), got)
        mine, give = split_sum(order, own, *others)
        other = swap(give, "rep", reps, 1)
        sums = pair_sum(keep_head, got, 4)
        others = [swap(sums[k], "grp", group, 2 * k) for k in range(1, 4)]
        att = after(att, mine, *sums)
        token_grad = finish(images, places, source, att, joints, weights, small)
        own, others, other = after((sums[0], others, other), token_grad)
        tail_sum = total_sum(mine, other)
        head_sum = total_sum(own, *others)
        every, tail_sum, head_sum = after((every, tail_sum, head_sum), token_grad)
        tail_other = swap(tail_sum, "rep", reps, 2)
        head_other = swap(head_sum, "rep", reps, 1)
        expert_in_grad, expert_out_grad = expert_grad(every, piece_in, piece_out)
        tail_other, head_other = after((tail_other, head_other), expert_in_grad)
        tail_sum, head_sum = total_sum(tail_sum, tail_other), total_sum(head_sum, head_other)
        tail_other = swap(tail_sum, "rep", reps, 1)
        head_other = swap(head_sum, "rep", reps, 3)
        heads_in_grad, heads_out_grad, router_grad, gain_one_grad, gain_two_grad = shares(
            experts, order, head_sum, head_other, tail_sum, tail_other, heads_in, first_gain[None]
        )
        gain_one_grad, gain_two_grad = gain_one_grad[0], gain_two_grad[0]
    else:
        token_grad = finish(images, places, source, att, joints, weights, small)
        expert_in_grad, expert_out_grad = expert_grad(every, piece_in, piece_out)
        tail_sum = jnp.concatenate([keep_tail, give_tail])
        tail_sum = lax.psum_scatter(tail_sum, "grp", scatter_dimension=0, tiled=True)
        head_sum = jnp.concatenate([keep_head, *give_head])
        head_sum = lax.psum_scatter(head_sum, "grp", scatter_dimension=0, tiled=True)
        tail_sum = lax.psum(tail_sum, "rep").astype(F32)
        head_sum = lax.psum(head_sum, "rep").astype(F32)
        columns = []
        for k in range(3):
            columns.append(head_sum[:, k * part : (k + 1) * part])
            columns.append(tail_sum[:, 2 * k * part : 2 * (k + 1) * part])
        heads_in_grad = jnp.concatenate(columns, axis=1)
        gain_one_grad = jnp.sum(heads_in_grad * heads_in.astype(F32), axis=1)
        gain_one_grad = gain_one_grad / first_gain.astype(F32)
        heads_out_grad, rest = tail_sum[:, 2 * wide : 3 * wide], tail_sum[:, 3 * wide :]
        router_grad, gain_two_grad = rest[:, :experts], rest[:, experts]
    return (
        output,
        token_grad,
        heads_in_grad,
        heads_out_grad,
        router_grad,
        gain_one_grad,
        gain_two_grad,
        expert_in_grad[None],
        expert_out_grad[None],
    )


def solution(mesh):
    token_spec = P(("rep", "grp"), None, None)
    matrix, vector, stack = P("grp", None), P("grp"), P("grp", None, None)
    return jax.shard_map(
        per_device,
        mesh=mesh,
        in_specs=(token_spec, token_spec, matrix, matrix, matrix, vector, vector, stack, stack),
        out_specs=(token_spec, token_spec, matrix, matrix, matrix, vector, vector, stack, stack),
        check_vma=False,
    )
```

```python
import functools

import jax
import jax.numpy as jnp
from jax import lax
from jax.experimental import pallas as pl
from jax.experimental.pallas import tpu as pltpu
from jax.sharding import PartitionSpec as P

HEADS = 12
LANES = 128
F32 = jnp.float32
BF16 = jnp.bfloat16
LOW = -1e30

NN = (((1,), (0,)), ((), ()))
NT = (((1,), (1,)), ((), ()))
TN = (((0,), (0,)), ((), ()))


def dot(left, right, form=NN):
    return lax.dot_general(left, right, form, preferred_element_type=F32)


def swap(values, axis, size, bit):
    return lax.ppermute(values, axis, [(place, place ^ bit) for place in range(size)])


def after(values, *others):
    return lax.optimization_barrier((values, others))[0]


def gather_first(own):
    return swap(own[0], "grp", 8, 2), swap(own[1], "grp", 8, 4)


def gather_second(joined):
    return swap(joined[0], "grp", 8, 4), swap(joined[1], "grp", 8, 2)


def gather_last(*stages):
    held = tuple(part for stage in stages for part in stage)
    return held + tuple(swap(part, "grp", 8, 1) for part in held)


def as_gathered(blocks, cut):
    held = []
    for k in range(2):
        own, x, y, far = blocks[k], blocks[k + 2], blocks[k + 4], blocks[k + 6]
        held += [own[:cut], own[cut:], x[:cut], y[cut:]]
        held += [jnp.concatenate([y[:cut], far[:cut]]), jnp.concatenate([x[cut:], far[cut:]])]
    return tuple(held)


def iota(shape, axis):
    return lax.broadcasted_iota(jnp.int32, shape, axis)


def normalize(values):
    center = values - jnp.mean(values, axis=-1, keepdims=True)
    factor = lax.rsqrt(jnp.mean(center * center, axis=-1, keepdims=True) + 1e-06)
    return center * factor, factor


def norm_back(scaled, normed, factor):
    inner = (
        scaled
        - jnp.mean(scaled, axis=-1, keepdims=True)
        - normed * jnp.mean(scaled * normed, axis=-1, keepdims=True)
    )
    return factor * inner


def pieces_of(rows, extra):
    half = rows // 2
    cut = extra + half
    for core in range(2):
        base = 6 * core
        yield base, extra, core, 0
        yield base + 1, 0, core, half
        yield base + 2, extra, core + 2, 0
        yield base + 3, 0, core + 4, half
        yield base + 4, extra, core + 4, 0
        yield base + 4, cut + extra, core + 6, 0
        yield base + 5, 0, core + 2, half
        yield base + 5, half, core + 6, half


def place_pieces(order_ref, pieces, rows, extra, target, columns):
    half = rows // 2
    for n, start, block, offset in pieces_of(rows, extra):
        place = pl.multiple_of(order_ref[block] * rows + offset, 16)
        target[pl.ds(place, half), :] = pieces[n][start : start + half, columns]


def store_blocks(order_ref, source, targets, columns):
    rows = source.shape[0] // 8
    n = 0
    for target in targets:
        for k in range(target.shape[0] // rows):
            start = pl.multiple_of(order_ref[8 + n] * rows, 32)
            target[k * rows : (k + 1) * rows, columns] = source[pl.ds(start, rows), :].astype(BF16)
            n += 1


def gather_small(order_ref, pieces, rows, extra, small_ref):
    total = jnp.zeros(small_ref.shape, F32)
    lane = iota((LANES, small_ref.shape[1]), 0)
    place = iota((LANES, small_ref.shape[1]), 1)
    cut = extra + rows // 2
    for core in range(2):
        for n, start, block in ((0, 0, 0), (2, 0, 2), (4, 0, 4), (4, cut, 6)):
            held = pieces[6 * core + n][start : start + extra, :LANES]
            fits = (place == order_ref[block + core] * rows + lane) & (lane < rows)
            total = total + dot(held, jnp.where(fits, 1.0, 0.0).astype(BF16))
    small_ref[...] = total


def rows_of(place, tall):
    return pl.ds(pl.multiple_of(place * tall, 16), tall)


def each_image(images, together, body):
    if images % together:
        together = 1
    if together == images:
        for i in range(images):
            body(i)
        return

    @pl.loop(0, images // together)
    def _(step):
        for k in range(together):
            body(step * together + k)


VM = pl.BlockSpec(memory_space=pltpu.VMEM)
SM = pl.BlockSpec(memory_space=pltpu.SMEM)


def call(body, name, inputs, outputs, scratch, limit, flops, hbm=()):
    return pl.pallas_call(
        body,
        in_specs=[SM if x.dtype == jnp.int32 else VM for x in inputs],
        out_specs=[VM] * len(outputs),
        out_shape=[
            jax.ShapeDtypeStruct(shape, kind) if n in hbm else pltpu.VMEM(shape, kind)
            for n, (shape, kind) in enumerate(outputs)
        ],
        scratch_shapes=[pltpu.VMEM(shape, kind) for shape, kind in scratch],
        compiler_params=pltpu.CompilerParams(vmem_limit_bytes=min(limit, 10) * 1024 * 1024),
        cost_estimate=pl.CostEstimate(flops=int(flops), bytes_accessed=1000000, transcendentals=0),
        name=name,
    )(*inputs)


def prepare_body(in_ref, out_ref, router_ref, one_ref, two_ref, h0, h1, t0, t1):
    rows, features = out_ref.shape
    half = rows // 2
    part = features // 3
    extra = h0.shape[0] - half
    small = [ref[...].astype(F32) for ref in (one_ref, two_ref, router_ref)]
    small.append(jnp.zeros((extra - 2 - router_ref.shape[0], rows), F32))
    small = jnp.concatenate(small, axis=0)
    small = jnp.concatenate([small, jnp.zeros((extra, LANES - rows), F32)], axis=1)
    h0[:extra, :] = jnp.zeros((extra, h0.shape[1]), BF16)
    h0[:extra, :LANES] = small.astype(BF16)
    for head, tail, start, here in ((h0, t0, extra, slice(0, half)), (h1, t1, 0, slice(half, rows))):
        for k in range(3):
            base = k * features
            head[start:, k * part : (k + 1) * part] = in_ref[here, base : base + part]
            tail[:, 2 * k * part : 2 * (k + 1) * part] = in_ref[here, base + part : base + features]
        tail[:, 2 * features :] = out_ref[here, :]


def prepare(heads_in, heads_out, router, one, two):
    rows, features = heads_out.shape
    extra = -(-(router.shape[0] + 2) // 16) * 16
    inputs = (heads_in, heads_out, router, one, two)
    outputs = [
        (extra + rows // 2, features),
        (rows // 2, features),
        (rows // 2, 3 * features),
        (rows // 2, 3 * features),
    ]
    return pl.pallas_call(
        prepare_body,
        grid=(1,),
        in_specs=[pl.BlockSpec(x.shape, lambda i: (0, 0)) for x in inputs],
        out_specs=[VM] * len(outputs),
        out_shape=[pltpu.VMEM(shape, BF16) for shape in outputs],
        compiler_params=pltpu.CompilerParams(vmem_limit_bytes=4 * 1024 * 1024),
        name="prepare",
    )(*inputs)


def join_body(a0, a1, b0, b1, a_ref, b_ref):
    for first, second, target in ((a0, a1, a_ref), (b0, b1, b_ref)):
        target[: first.shape[0], :] = first[...]
        target[first.shape[0] :, :] = second[...]


def join(own, got):
    outputs = [((2 * x.shape[0], x.shape[1]), BF16) for x in own]
    return call(join_body, "join", (own[0], got[0], own[1], got[1]), outputs, [], 4, 1e6)


def attend_body(first, images, places, order_ref, source_ref, *refs):
    pieces, refs = refs[:12], refs[12:]
    features = source_ref.shape[1]
    rows = features // 8
    if first:
        act_ref, small_ref, weight, joint_ref, prob_ref, mixed_ref = refs
        extra = small_ref.shape[0]
    else:
        out_weight, weight, joint_ref, prob_ref, mixed_ref = refs
        act_ref = source_ref
        extra = 0
    tall = source_ref.shape[0] // images
    width = weight.shape[1]
    place_pieces(order_ref, pieces, rows, extra, weight, slice(0, width))
    if first:
        gather_small(order_ref, pieces, rows, extra, small_ref)

        for i in range(images):
            here = rows_of(i, tall)
            normed, _ = normalize(source_ref[here, :].astype(F32))
            act_ref[here, :] = (normed * small_ref[0:1, :]).astype(BF16)
    else:
        place_pieces(order_ref, pieces, rows, 0, out_weight, slice(width, width + features))

    for i in range(images // 2):
        here = rows_of(i, 2 * tall)
        joint_ref[here, :] = dot(act_ref[here, :], weight[...]).astype(BF16)

    third = width // 3
    heads = prob_ref.shape[0] // images
    low = iota((tall, LANES), 1) < LANES // 2
    inside = iota((tall, LANES), 0) < places
    seen = iota((tall, tall), 1) < places

    def attend_image(i):
        here = rows_of(i, tall)
        for pair in range(third // LANES):
            query, keys, values = (
                joint_ref[here, part * third + pair * LANES : part * third + (pair + 1) * LANES]
                for part in range(3)
            )
            query = query * 0.125
            values_ones = jnp.concatenate([values, jnp.ones_like(values)], axis=1)
            outs = []
            for side in range(2):
                mine = low if side == 0 else ~low
                scores = dot(jnp.where(mine, query, 0), keys, NT)
                scores = jnp.where(seen, scores, LOW)
                power = jnp.exp(scores - jnp.max(scores, axis=1, keepdims=True)).astype(BF16)
                got = dot(power, values_ones)
                shrink = 1.0 / got[:, LANES:]
                outs.append(got[:, :LANES] * shrink)
                shrink = jnp.concatenate([shrink, shrink[:, : tall - LANES]], axis=1)
                prob_ref[i * heads + 2 * pair + side] = (power.astype(F32) * shrink).astype(BF16)
            mixed = jnp.where(inside, jnp.where(low, outs[0], outs[1]), 0.0)
            mixed_ref[here, pair * LANES : (pair + 1) * LANES] = mixed.astype(BF16)

    each_image(images, 2, attend_image)


def attend(first, images, places, order, source, pieces, width):
    total, features = source.shape
    tall = total // images
    heads = width // 3 // 64
    extra = pieces[0].shape[0] - features // 16
    outputs = [
        ((features, width), BF16),
        ((total, width), BF16),
        ((images * heads, tall, tall), BF16),
        ((total, width // 3), BF16),
    ]
    if first:
        outputs = [((total, features), BF16), ((extra, features), F32)] + outputs
    else:
        outputs = [((features, features), BF16)] + outputs
    return call(
        functools.partial(attend_body, first, images, places),
        "attend",
        (order, source, *pieces),
        outputs,
        [],
        12,
        2 * total * features * width * 2,
    )


def softmaxes(logits, places, experts):
    rows = iota(logits.shape, 0) < experts
    lanes = iota(logits.shape, 1) < places
    wide = jnp.where(lanes, logits, LOW)
    wide = jnp.exp(wide - jnp.max(wide, axis=1, keepdims=True))
    dispatch = wide / jnp.sum(wide, axis=1, keepdims=True)
    tall = jnp.where(rows, logits, LOW)
    tall = jnp.exp(tall - jnp.max(tall, axis=0, keepdims=True))
    combine = tall / jnp.sum(tall, axis=0, keepdims=True)
    return jnp.where(rows, dispatch, 0.0), combine


def slot_rows_of(experts, order_ref, small_ref, slots):
    rows = small_ref.shape[0]
    slot, row = iota((slots, rows), 0), iota((slots, rows), 1)
    chip = order_ref[order_ref.shape[0] - 1]
    fits = (row == (slot ^ chip) + 2) & (slot < experts)
    return dot(jnp.where(fits, 1.0, 0.0).astype(BF16), small_ref[...].astype(BF16)).astype(BF16)


def pick_rows(shape, wanted):
    row, column = iota(shape, 0), iota(shape, 1)
    return jnp.where(column == wanted(row), 1.0, 0.0).astype(BF16)


def route_body(
    images, places, experts, order_ref, token_ref, cot_ref, m0, m1, weight, small_ref,
    resid_ref, logit_ref, *refs,
):
    out_refs, packed_ref = refs[:-1], refs[-1]
    slots = logit_ref.shape[0] // images
    router = slot_rows_of(experts, order_ref, small_ref, slots)
    tall = token_ref.shape[0] // images
    features = token_ref.shape[1]

    for i in range(images // 2):
        here = rows_of(i, 2 * tall)
        mixed = jnp.concatenate([m0[here, :], m1[here, :]], axis=1)
        resid_ref[here, :] = token_ref[here, :].astype(F32) + dot(mixed, weight[...])

    def route_image(i):
        here = rows_of(i, tall)
        normed, _ = normalize(resid_ref[here, :])
        act = (normed * small_ref[1:2, :]).astype(BF16)
        logits = dot(router, act, NT)
        group = rows_of(i, slots)
        logit_ref[group, :] = logits
        dispatch, combine = softmaxes(logits, places, experts)
        packed_ref[group, :features] = dot(dispatch.astype(BF16), act).astype(BF16)
        packed_ref[group, features:] = dot(combine.astype(BF16), cot_ref[here, :]).astype(BF16)

    each_image(images, 3, route_image)

    high = out_refs[0].shape[0]
    pick = pick_rows(
        (experts * high, images * slots),
        lambda n: jnp.where(n % high < images, n % high * slots + n // high, -1),
    )
    packed = dot(pick, packed_ref[...]).astype(BF16)
    for k, out_ref in enumerate(out_refs):
        out_ref[...] = packed[k * high : (k + 1) * high, :]


def route(images, places, experts, slots, order, tokens, cot, mixed, w, small):
    total, features = tokens.shape
    high = -(-images // 8) * 8
    return call(
        functools.partial(route_body, images, places, experts),
        "route",
        (order, tokens, cot, *mixed, w, small),
        [((total, features), F32), ((images * slots, total // images), F32)]
        + [((high, 2 * features), BF16)] * experts,
        [((images * slots, 2 * features), BF16)],
        10,
        4 * total * features * features,
    )


def gelu_parts(values):
    scale, cubic = 0.7978845608028654, 0.044715
    square = values * values
    bent = jnp.tanh(scale * values * (1.0 + cubic * square))
    half = 0.5 * (1.0 + bent)
    slope = half + 0.5 * values * (1.0 - bent * bent) * scale * (1.0 + 3.0 * cubic * square)
    return values * half, slope


def expert_body(count, images, in_ref, out_ref, *refs):
    sources, (packed_ref, keep_ref, give_ref, rows_ref, back_ref) = refs[:count], refs[count:]
    features = in_ref.shape[0]
    high = sources[0].shape[0]
    for k, source in enumerate(sources):
        rows_ref[k * high : (k + 1) * high, :] = source[...]
    rows, arriving = rows_ref[:, :features], rows_ref[:, features:]
    total = jnp.zeros((rows.shape[0], features), F32)
    grad_total = total
    step = 512
    for start in range(0, in_ref.shape[1], step):
        w_in = in_ref[:, start : start + step]
        w_out = out_ref[start : start + step, :]
        hidden, slope = gelu_parts(dot(rows, w_in))
        grad_pre = (dot(arriving, w_out, NT) * slope).astype(BF16)
        total = total + dot(hidden.astype(BF16), w_out)
        grad_total = grad_total + dot(grad_pre, w_in, NT)
    back_ref[:, :features] = total.astype(BF16)
    back_ref[:, features:] = grad_total.astype(BF16)
    half = keep_ref.shape[0]
    keep_ref[...] = back_ref[:half, :]
    give_ref[...] = back_ref[half:, :]
    pick = pick_rows(
        (packed_ref.shape[0], rows_ref.shape[0]), lambda n: n // images * high + n % images
    )
    packed_ref[...] = dot(pick, rows_ref[...]).astype(BF16)


def expert(images, piece_in, piece_out, sources):
    high, wide = sources[0].shape
    rows = high * len(sources)
    return call(
        functools.partial(expert_body, len(sources), images),
        "expert",
        (piece_in, piece_out, *sources),
        [
            ((images * len(sources), wide), BF16),
            ((rows // 2, wide), BF16),
            ((rows // 2, wide), BF16),
        ],
        [((rows, wide), BF16)] * 2,
        8,
        1e9,
    )


def pair_sum_body(parts, keep_ref, *refs):
    got_refs, out_refs = refs[:parts], refs[parts:]
    rows = out_refs[0].shape[0]
    each = len(out_refs) // parts
    for k, out_ref in enumerate(out_refs):
        kept = keep_ref[k * rows : (k + 1) * rows, :].astype(F32)
        got = got_refs[k // each][k % each * rows : (k % each + 1) * rows, :].astype(F32)
        out_ref[...] = (kept + got).astype(BF16)


def pair_sum(keep, got, count):
    shape = (keep.shape[0] // count, keep.shape[1])
    body = functools.partial(pair_sum_body, len(got))
    return call(body, "pair_sum", (keep, *got), [(shape, BF16)] * count, [], 4, 1e6)


def total_body(*refs):
    refs[-1][...] = sum(ref[...].astype(F32) for ref in refs[:-1]).astype(BF16)


def total_sum(*terms):
    return call(total_body, "total_sum", terms, [(terms[0].shape, BF16)], [], 4, 1e6)[0]


def split_sum_body(order_ref, *refs):
    terms, (mine_ref, give_ref, scratch) = refs[:-3], refs[-3:]
    scratch[...] = sum(ref[...].astype(F32) for ref in terms)
    half = mine_ref.shape[0]
    odd = order_ref[order_ref.shape[0] - 2]
    mine = pl.multiple_of(odd * half, 16)
    other = pl.multiple_of((1 - odd) * half, 16)
    mine_ref[...] = scratch[pl.ds(mine, half), :].astype(BF16)
    give_ref[...] = scratch[pl.ds(other, half), :].astype(BF16)


def split_sum(order, *terms):
    rows, wide = terms[0].shape
    shape = (rows // 2, wide)
    return call(
        split_sum_body, "split_sum", (order, *terms), [(shape, BF16)] * 2, [((rows, wide), F32)], 8, 1e6
    )


def shares_body(
    experts, order_ref, head_ref, head_other, tail_ref, tail_other, w_ref, gain_ref,
    in_ref, out_ref, router_ref, gain_one_ref, gain_two_ref, tail,
):
    rows, features = out_ref.shape
    half = rows // 2
    odd = order_ref[order_ref.shape[0] - 2]
    tail[pl.ds(pl.multiple_of(odd * half, 16), half), :] = tail_ref[...].astype(F32)
    tail[pl.ds(pl.multiple_of((1 - odd) * half, 16), half), :] = tail_other[...].astype(F32)
    part = features // 3
    for k in range(3):
        here = slice(k * part, (k + 1) * part)
        in_ref[:, k * features : k * features + part] = (
            head_ref[:, here].astype(F32) + head_other[:, here].astype(F32)
        )
        in_ref[:, k * features + part : (k + 1) * features] = tail[:, 2 * k * part : 2 * (k + 1) * part]
    out_ref[...] = tail[:, 2 * features : 3 * features]
    rest = tail[:, 3 * features :]
    rest = rest.T
    router_ref[...] = rest[:experts, :]
    gain_two_ref[...] = rest[experts : experts + 1, :]
    gain_one = jnp.sum(in_ref[...] * w_ref[...].astype(F32), axis=1, keepdims=True)
    gain_one = jnp.broadcast_to(gain_one, (rows, LANES)).T[:1, :]
    gain_one_ref[...] = gain_one / gain_ref[...].astype(F32)


def shares(experts, order, head, head_other, tail, tail_other, w, gain):
    rows, features = head.shape
    return call(
        functools.partial(shares_body, experts),
        "shares",
        (order, head, head_other, tail, tail_other, w, gain),
        [
            (w.shape, F32),
            ((rows, features), F32),
            ((experts, rows), F32),
            ((1, rows), F32),
            ((1, rows), F32),
        ],
        [((rows, tail.shape[1]), F32)],
        8,
        1e6,
        hbm=range(5),
    )


def expert_grad_body(count, *refs):
    sources, (in_ref, out_ref, grad_in_ref, grad_out_ref) = refs[:count], refs[count:]
    features = in_ref.shape[0]
    every = jnp.concatenate([source[...] for source in sources], axis=0)
    rows, arriving = every[:, :features], every[:, features:]
    hidden, slope = gelu_parts(dot(rows, in_ref[...]))
    grad_pre = (dot(arriving, out_ref[...], NT) * slope).astype(BF16)
    grad_in_ref[...] = dot(rows, grad_pre, TN)
    grad_out_ref[...] = dot(hidden.astype(BF16), arriving, TN)


def expert_grad(sources, piece_in, piece_out):
    features, hidden = piece_in.shape
    step = 256
    wide = pl.BlockSpec((features, step), lambda i: (0, i))
    high = pl.BlockSpec((step, features), lambda i: (i, 0))
    return pl.pallas_call(
        functools.partial(expert_grad_body, len(sources)),
        grid=(hidden // step,),
        in_specs=[pl.BlockSpec(x.shape, lambda i: (0, 0)) for x in sources] + [wide, high],
        out_specs=[wide, high],
        out_shape=[
            jax.ShapeDtypeStruct(piece_in.shape, F32),
            jax.ShapeDtypeStruct(piece_out.shape, F32),
        ],
        compiler_params=pltpu.CompilerParams(vmem_limit_bytes=16 * 1024 * 1024),
        cost_estimate=pl.CostEstimate(
            flops=1600 * piece_in.size, bytes_accessed=14000000, transcendentals=0
        ),
        name="expert_grad",
    )(*sources, piece_in, piece_out)


def back_body(
    images, places, experts, order_ref, resid_ref, logit_ref, cot_ref, m0, m1, weight, small_ref, *refs
):
    sources, refs = refs[:experts], refs[experts:]
    output_ref, att_ref, grad_mixed_ref, grad_w_ref, grad_side_ref, summed_ref = refs
    slots = logit_ref.shape[0] // images
    router = slot_rows_of(experts, order_ref, small_ref, slots)
    total, features = resid_ref.shape
    tall = total // images
    gain = small_ref[1:2, :]
    high = sources[0].shape[0]
    pick = pick_rows(
        (images * slots, experts * high),
        lambda n: jnp.where(n % slots < experts, n % slots * high + n // slots, -1),
    )
    arrived = jnp.concatenate([source[...] for source in sources], axis=0)
    summed_ref[...] = dot(pick, arrived).astype(BF16)

    def image(i, carry):
        side, gain_sum = carry
        here = rows_of(i, tall)
        group = rows_of(i, slots)
        expert_sum, grad_slots = summed_ref[group, :features], summed_ref[group, features:]
        resid = resid_ref[here, :]
        cot = cot_ref[here, :]
        dispatch, combine = softmaxes(logit_ref[group, :], places, experts)
        output = resid + dot(combine.astype(BF16), expert_sum, TN)
        output_ref[i] = output[:places].astype(BF16)
        normed, factor = normalize(resid)
        act = (normed * gain).astype(BF16)
        grad_comb = dot(expert_sum, cot, NT)
        grad_disp = dot(grad_slots, act, NT)
        grad_logits = combine * (grad_comb - jnp.sum(grad_comb * combine, axis=0, keepdims=True))
        grad_logits = grad_logits + dispatch * (
            grad_disp - jnp.sum(grad_disp * dispatch, axis=1, keepdims=True)
        )
        grad_logits = grad_logits.astype(BF16)
        grad_act = dot(
            jnp.concatenate([dispatch.astype(BF16), grad_logits], axis=0),
            jnp.concatenate([grad_slots, router], axis=0),
            TN,
        )
        att = cot.astype(F32) + norm_back(grad_act * gain, normed, factor)
        att_ref[here, :] = att.astype(BF16)
        return (
            side + dot(grad_logits, act),
            gain_sum + jnp.sum(grad_act * normed, axis=0, keepdims=True),
        )

    together = 3 if images % 3 == 0 else 1

    def some(step, carry):
        for k in range(together):
            carry = image(step * together + k, carry)
        return carry

    carry = (jnp.zeros((slots, features), F32), jnp.zeros((1, features), F32))
    side, gain_sum = lax.fori_loop(0, images // together, some, carry)

    for i in range(images // 2):
        here = rows_of(i, 2 * tall)
        grad_mixed_ref[here, :] = dot(att_ref[here, :], weight[...], NT).astype(BF16)

    part = m0.shape[1]
    grad_w_ref[:part, :] = dot(m0[...], att_ref[...], TN).astype(BF16)
    grad_w_ref[part:, :] = dot(m1[...], att_ref[...], TN).astype(BF16)
    slot = iota((LANES, slots), 0) ^ order_ref[order_ref.shape[0] - 1]
    slot = jnp.where(iota((LANES, slots), 0) < experts, slot, -1)
    fits = jnp.where(slot == iota((LANES, slots), 1), 1.0, 0.0).astype(BF16)
    side = dot(fits, side.astype(BF16))
    side = jnp.where(iota(side.shape, 0) == experts, gain_sum, side)
    grad_side_ref[...] = side.T.astype(BF16)


def back(images, places, experts, order, resid, logits, cot, mixed, w, small, sources):
    total, features = resid.shape
    return call(
        functools.partial(back_body, images, places, experts),
        "back",
        (order, resid, logits, cot, *mixed, w, small, *sources),
        [
            ((images, places, features), BF16),
            ((total, features), BF16),
            ((total, features), BF16),
            ((features, features), BF16),
            ((features, LANES), BF16),
        ],
        [((logits.shape[0], 2 * features), BF16)],
        14,
        8 * total * features * features,
        hbm=(0,),
    )


def attend_back_body(images, extra, offset, order_ref, joint_ref, prob_ref, grad_ref, mixed_ref, act_ref, *refs):
    more, (out_ref, *targets, total) = refs[:extra], refs[extra:]
    width = joint_ref.shape[1]
    tall = joint_ref.shape[0] // images
    third = width // 3
    heads = prob_ref.shape[0] // images
    low = iota((tall, LANES), 1) < LANES // 2

    def back_image(i):
        here = rows_of(i, tall)
        for pair in range(third // LANES):
            query, keys, values = (
                joint_ref[here, part * third + pair * LANES : part * third + (pair + 1) * LANES]
                for part in range(3)
            )
            grad = grad_ref[here, offset + pair * LANES : offset + (pair + 1) * LANES]
            product = grad.astype(F32) * mixed_ref[
                here, pair * LANES : (pair + 1) * LANES
            ].astype(F32)
            query_high, grad_high = query.T, grad.T
            grad_query, grad_keys, grad_values = [], [], []
            for side in range(2):
                mine = low if side == 0 else ~low
                rows = slice(side * LANES // 2, (side + 1) * LANES // 2)
                prob = prob_ref[i * heads + 2 * pair + side]
                inner = jnp.sum(jnp.where(mine, product, 0.0), axis=1, keepdims=True)
                grad_prob = dot(jnp.where(mine, grad, 0), values, NT)
                grad_scores = (prob.astype(F32) * (grad_prob - inner)).astype(BF16)
                grad_query.append(dot(grad_scores, keys))
                grad_keys.append(dot(query_high[rows], grad_scores))
                grad_values.append(dot(grad_high[rows], prob))
            joined = (
                (jnp.where(low, *grad_query) * 0.125).astype(BF16),
                (jnp.concatenate(grad_keys, axis=0) * 0.125).astype(BF16).T,
                jnp.concatenate(grad_values, axis=0).astype(BF16).T,
            )
            for part in range(3):
                out_ref[
                    here, part * third + pair * LANES : part * third + (pair + 1) * LANES
                ] = joined[part]

    each_image(images, 2, back_image)

    step = third
    for start in range(0, width, step):
        total[:, start : start + step] = dot(
            act_ref[...], out_ref[:, start : start + step], TN
        ).astype(BF16)
    store_blocks(order_ref, total, targets, slice(0, width))
    place = width
    for source in more:
        end = place + source.shape[1]
        store_blocks(order_ref, source, targets, slice(place, end))
        place = end


def attend_back(images, offset, order, joint, prob, grad_mixed, mixed, act, splits, more=()):
    total, width = joint.shape
    features = act.shape[1]
    columns = width + sum(m.shape[1] for m in more)
    parts = [((features // n, columns), BF16) for n in splits]
    return call(
        functools.partial(attend_back_body, images, len(more), offset),
        "attend_back",
        (order, joint, prob, grad_mixed, mixed, act, *more),
        [(joint.shape, BF16)] + parts,
        [((features, width), BF16)],
        16,
        2 * total * features * width * 4,
    )


def finish_body(images, places, token_ref, att_ref, j0, j1, s0, s1, small_ref, out_ref):
    total, features = token_ref.shape
    tall = total // images

    @pl.loop(0, images // 2)
    def _(i):
        here = rows_of(i, 2 * tall)
        grad_act = dot(j0[here, :], s0[...], NT) + dot(j1[here, :], s1[...], NT)
        normed, factor = normalize(token_ref[here, :].astype(F32))
        result = att_ref[here, :].astype(F32)
        result = result + norm_back(grad_act * small_ref[0:1, :], normed, factor)
        result = result.astype(BF16)
        out_ref[2 * i] = result[:places]
        out_ref[2 * i + 1] = result[tall : tall + places]


def finish(images, places, tokens, att, joints, weights, small):
    total, features = tokens.shape
    return call(
        functools.partial(finish_body, images, places),
        "finish",
        (tokens, att, *joints, *weights, small),
        [((images, places, features), BF16)],
        [],
        12,
        6 * total * features * features,
        hbm=(0,),
    )[0]


def per_device(
    tokens, cotangent, heads_in, heads_out, slot_router, first_gain, second_gain, expert_in, expert_out
):
    images, places, features = tokens.shape
    experts = slot_router.shape[1]
    group = lax.axis_size("grp")
    reps = lax.axis_size("rep")
    me = lax.axis_index("grp")
    own_rows = heads_in.shape[0]
    chip = me // 2
    odd = lax.axis_index("rep") % 2
    direct = group == 8
    ways = jnp.arange(8, dtype=jnp.int32)
    if direct:
        order = jnp.concatenate([ways ^ me, (ways % 4 * 2 + ways // 4) ^ me, odd[None], chip[None]])
    else:
        order = jnp.concatenate([ways, ways, odd[None], chip[None]])
    tall = -(-places // 16) * 16
    slot_rows = -(-experts // 16) * 16
    part = features // 3
    wide = 3 * part

    grow = ((0, 0), (0, tall - places), (0, 0))
    source = jnp.pad(tokens, grow).reshape(images * tall, features)
    cot = jnp.pad(cotangent, grow).reshape(images * tall, features)
    if direct:
        rows_in, order = lax.optimization_barrier((heads_in, order))
        h0, h1, t0, t1 = prepare(
            rows_in, heads_out, slot_router.T, first_gain[None], second_gain[None]
        )
        head_first = gather_first((h0, h1))
        head_first = after(head_first, source, cot)
        (t0, t1), head_first = lax.optimization_barrier(((t0, t1), head_first))
        head_second = gather_second(join((h0, h1), head_first))
        tail_first = gather_first((t0, t1))
        head = gather_last((h0, h1), head_first, head_second)
        tail_first = after(tail_first, *head)
        tail_join = join((t0, t1), tail_first)
        source = after(source, *tail_join)
    else:
        thirds = [heads_in[:, k * features : (k + 1) * features] for k in range(3)]
        head_part = jnp.concatenate([t[:, :part] for t in thirds], axis=1)
        tail_part = jnp.concatenate([t[:, part:] for t in thirds] + [heads_out], axis=1)
        small = jnp.concatenate([first_gain[None], second_gain[None], slot_router.T], axis=0)
        extra = -(-small.shape[0] // 16) * 16
        head_part = lax.all_gather(head_part, "grp", axis=0, tiled=True).reshape(8, -1, wide)
        small = lax.all_gather(small, "grp", axis=1, tiled=True).reshape(-1, 8, features // 8)
        small = small.transpose(1, 0, 2)
        small = jnp.pad(small, ((0, 0), (0, extra - small.shape[1]), (0, wide - small.shape[2])))
        head = as_gathered(jnp.concatenate([small, head_part], axis=1), extra + features // 16)
        tail_part = lax.all_gather(tail_part, "grp", axis=0, tiled=True)
        tail = as_gathered(tail_part.reshape(8, -1, 3 * features), features // 16)

    act, small, w_head, joint_head, prob_head, mixed_head = attend(
        True, images, places, order, source, head, wide
    )
    if direct:
        tail_second = after(gather_second(tail_join), mixed_head)
        tail = gather_last((t0, t1), tail_first, tail_second)
    w_out, w_tail, joint_tail, prob_tail, mixed_tail = attend(
        False, images, places, order, act, tail, 2 * wide
    )
    mixes = [mixed_head, mixed_tail]
    resid, logits, *leaving = route(
        images, places, experts, slot_rows, order, source, cot, mixes, w_out, small
    )

    arrived = [leaving[0]] + [swap(leaving[k], "grp", group, 2 * k) for k in range(1, experts)]
    arrived = arrived + [swap(part, "grp", group, 1) for part in arrived]
    piece_in, piece_out = expert_in[0], expert_out[0]
    received, kept, given = expert(images, piece_in, piece_out, arrived)
    both = pair_sum(kept, [swap(given, "grp", group, 1)], experts)
    summed = [both[0]] + [swap(both[k], "grp", group, 2 * k) for k in range(1, experts)]
    received = after(received, *summed)
    far = [swap(received, "rep", reps, k) for k in range(1, reps)]
    output, att, grad_mixed, grad_out, grad_side = back(
        images, places, experts, order, resid, logits, cot, mixes, w_out, small, summed
    )
    grad_mixed, far = lax.optimization_barrier((grad_mixed, far))
    grad_joint_tail, keep_tail, give_tail = attend_back(
        images, part, order, joint_tail, prob_tail, grad_mixed, mixed_tail, act, (2, 2), (grad_out, grad_side)
    )
    if direct:
        sums = pair_sum(keep_tail, [swap(give_tail, "grp", group, 1)], 4)
        others = [swap(sums[k], "grp", group, 2 * k) for k in range(1, 4)]
        grad_mixed = after(grad_mixed, *sums)
    grad_joint_head, keep_head, *give_head = attend_back(
        images, 0, order, joint_head, prob_head, grad_mixed, mixed_head, act, (2, 4, 4)
    )
    joints, weights = [grad_joint_head, grad_joint_tail], [w_head, w_tail]
    every = [received] + far
    if direct:
        got = [swap(part, "grp", group, 1) for part in give_head]
        own, others = after((sums[0], others), got)
        mine, give = split_sum(order, own, *others)
        other = swap(give, "rep", reps, 1)
        sums = pair_sum(keep_head, got, 4)
        others = [swap(sums[k], "grp", group, 2 * k) for k in range(1, 4)]
        att = after(att, mine, *sums)
        token_grad = finish(images, places, source, att, joints, weights, small)
        own, others, other = after((sums[0], others, other), token_grad)
        tail_sum = total_sum(mine, other)
        head_sum = total_sum(own, *others)
        every, tail_sum, head_sum = after((every, tail_sum, head_sum), token_grad)
        tail_other = swap(tail_sum, "rep", reps, 2)
        head_other = swap(head_sum, "rep", reps, 1)
        expert_in_grad, expert_out_grad = expert_grad(every, piece_in, piece_out)
        tail_other, head_other = after((tail_other, head_other), expert_in_grad)
        tail_sum, head_sum = total_sum(tail_sum, tail_other), total_sum(head_sum, head_other)
        tail_other = swap(tail_sum, "rep", reps, 1)
        head_other = swap(head_sum, "rep", reps, 3)
        heads_in_grad, heads_out_grad, router_grad, gain_one_grad, gain_two_grad = shares(
            experts, order, head_sum, head_other, tail_sum, tail_other, heads_in, first_gain[None]
        )
        gain_one_grad, gain_two_grad = gain_one_grad[0], gain_two_grad[0]
        router_grad = router_grad.T
    else:
        token_grad = finish(images, places, source, att, joints, weights, small)
        expert_in_grad, expert_out_grad = expert_grad(every, piece_in, piece_out)
        tail_sum = jnp.concatenate([keep_tail, give_tail])
        tail_sum = lax.psum_scatter(tail_sum, "grp", scatter_dimension=0, tiled=True)
        head_sum = jnp.concatenate([keep_head, *give_head])
        head_sum = lax.psum_scatter(head_sum, "grp", scatter_dimension=0, tiled=True)
        tail_sum = lax.psum(tail_sum, "rep").astype(F32)
        head_sum = lax.psum(head_sum, "rep").astype(F32)
        columns = []
        for k in range(3):
            columns.append(head_sum[:, k * part : (k + 1) * part])
            columns.append(tail_sum[:, 2 * k * part : 2 * (k + 1) * part])
        heads_in_grad = jnp.concatenate(columns, axis=1)
        gain_one_grad = jnp.sum(heads_in_grad * heads_in.astype(F32), axis=1)
        gain_one_grad = gain_one_grad / first_gain.astype(F32)
        heads_out_grad, rest = tail_sum[:, 2 * wide : 3 * wide], tail_sum[:, 3 * wide :]
        router_grad, gain_two_grad = rest[:, :experts], rest[:, experts]
    return (
        output,
        token_grad,
        heads_in_grad,
        heads_out_grad,
        router_grad,
        gain_one_grad,
        gain_two_grad,
        expert_in_grad[None],
        expert_out_grad[None],
    )


def solution(mesh):
    token_spec = P(("rep", "grp"), None, None)
    matrix, vector, stack = P("grp", None), P("grp"), P("grp", None, None)
    return jax.shard_map(
        per_device,
        mesh=mesh,
        in_specs=(token_spec, token_spec, matrix, matrix, matrix, vector, vector, stack, stack),
        out_specs=(token_spec, token_spec, matrix, matrix, matrix, vector, vector, stack, stack),
        check_vma=False,
    )
```

```python
import functools

import jax
import jax.numpy as jnp
from jax import lax
from jax.experimental import pallas as pl
from jax.experimental.pallas import tpu as pltpu
from jax.sharding import PartitionSpec as P

HEADS = 12
LANES = 128
F32 = jnp.float32
BF16 = jnp.bfloat16
LOW = -1e30

NN = (((1,), (0,)), ((), ()))
NT = (((1,), (1,)), ((), ()))
TN = (((0,), (0,)), ((), ()))


def dot(left, right, form=NN):
    return lax.dot_general(left, right, form, preferred_element_type=F32)


def swap(values, axis, size, bit):
    return lax.ppermute(values, axis, [(place, place ^ bit) for place in range(size)])


def after(values, *others):
    return lax.optimization_barrier((values, others))[0]


def gather_first(own):
    return swap(own[0], "grp", 8, 2), swap(own[1], "grp", 8, 4)


def gather_second(joined):
    return swap(joined[0], "grp", 8, 4), swap(joined[1], "grp", 8, 2)


def gather_last(*stages):
    held = tuple(part for stage in stages for part in stage)
    return held + tuple(swap(part, "grp", 8, 1) for part in held)


def as_gathered(blocks, cut):
    held = []
    for k in range(2):
        own, x, y, far = blocks[k], blocks[k + 2], blocks[k + 4], blocks[k + 6]
        held += [own[:cut], own[cut:], x[:cut], y[cut:]]
        held += [jnp.concatenate([y[:cut], far[:cut]]), jnp.concatenate([x[cut:], far[cut:]])]
    return tuple(held)


def iota(shape, axis):
    return lax.broadcasted_iota(jnp.int32, shape, axis)


def normalize(values):
    center = values - jnp.mean(values, axis=-1, keepdims=True)
    factor = lax.rsqrt(jnp.mean(center * center, axis=-1, keepdims=True) + 1e-06)
    return center * factor, factor


def norm_back(scaled, normed, factor):
    inner = (
        scaled
        - jnp.mean(scaled, axis=-1, keepdims=True)
        - normed * jnp.mean(scaled * normed, axis=-1, keepdims=True)
    )
    return factor * inner


def first_part(features):
    return features // 3


def pieces_of(rows, extra):
    half = rows // 2
    cut = extra + half
    for core in range(2):
        base = 6 * core
        yield base, extra, core, 0
        yield base + 1, 0, core, half
        yield base + 2, extra, core + 2, 0
        yield base + 3, 0, core + 4, half
        yield base + 4, extra, core + 4, 0
        yield base + 4, cut + extra, core + 6, 0
        yield base + 5, 0, core + 2, half
        yield base + 5, half, core + 6, half


def place_pieces(order_ref, pieces, rows, extra, target, columns):
    half = rows // 2
    for n, start, block, offset in pieces_of(rows, extra):
        place = pl.multiple_of(order_ref[block] * rows + offset, 16)
        target[pl.ds(place, half), :] = pieces[n][start : start + half, columns]


def store_blocks(order_ref, source, targets, columns):
    rows = source.shape[0] // 8
    n = 0
    for target in targets:
        for k in range(target.shape[0] // rows):
            start = pl.multiple_of(order_ref[8 + n] * rows, 32)
            target[k * rows : (k + 1) * rows, columns] = source[pl.ds(start, rows), :].astype(BF16)
            n += 1


def gather_small(order_ref, pieces, rows, extra, small_ref):
    total = jnp.zeros(small_ref.shape, F32)
    lane = iota((LANES, small_ref.shape[1]), 0)
    place = iota((LANES, small_ref.shape[1]), 1)
    cut = extra + rows // 2
    for core in range(2):
        for n, start, block in ((0, 0, 0), (2, 0, 2), (4, 0, 4), (4, cut, 6)):
            held = pieces[6 * core + n][start : start + extra, :LANES]
            fits = (place == order_ref[block + core] * rows + lane) & (lane < rows)
            total = total + dot(held, jnp.where(fits, 1.0, 0.0).astype(BF16))
    small_ref[...] = total


def rows_of(place, tall):
    return pl.ds(pl.multiple_of(place * tall, 16), tall)


def each_image(images, together, body):
    if images % together:
        together = 1
    if together == images:
        for i in range(images):
            body(i)
        return

    @pl.loop(0, images // together)
    def _(step):
        for k in range(together):
            body(step * together + k)


VM = pl.BlockSpec(memory_space=pltpu.VMEM)
SM = pl.BlockSpec(memory_space=pltpu.SMEM)


def call(body, name, inputs, outputs, scratch, limit, flops, hbm=()):
    return pl.pallas_call(
        body,
        in_specs=[SM if x.dtype == jnp.int32 else VM for x in inputs],
        out_specs=[VM] * len(outputs),
        out_shape=[
            jax.ShapeDtypeStruct(shape, kind) if n in hbm else pltpu.VMEM(shape, kind)
            for n, (shape, kind) in enumerate(outputs)
        ],
        scratch_shapes=[pltpu.VMEM(shape, kind) for shape, kind in scratch],
        compiler_params=pltpu.CompilerParams(vmem_limit_bytes=min(limit, 10) * 1024 * 1024),
        cost_estimate=pl.CostEstimate(flops=int(flops), bytes_accessed=1000000, transcendentals=0),
        name=name,
    )(*inputs)


def prepare_body(in_hbm, out_hbm, small_ref, h0, h1, t0, t1, in_ref, out_ref, sems):
    rows, features = out_ref.shape
    half = rows // 2
    part = first_part(features)
    rest = features - part
    extra = h0.shape[0] - half
    h0[:extra, :] = jnp.zeros((extra, h0.shape[1]), BF16)
    h0[:extra, :LANES] = small_ref[...]
    copies = [
        pltpu.make_async_copy(source, target, sems.at[k])
        for k, (source, target) in enumerate(((in_hbm, in_ref), (out_hbm, out_ref)))
    ]
    for copy in copies:
        copy.start()
    for copy in copies:
        copy.wait()
    for head, tail, start, here in ((h0, t0, extra, slice(0, half)), (h1, t1, 0, slice(half, rows))):
        for k in range(3):
            base = k * features
            head[start:, k * part : (k + 1) * part] = in_ref[here, base : base + part]
            tail[:, k * rest : (k + 1) * rest] = in_ref[here, base + part : base + features]
        tail[:, 3 * rest :] = out_ref[here, :]


def prepare(heads_in, heads_out, small):
    rows, features = heads_out.shape
    part = first_part(features)
    head, tail = 3 * part, 4 * features - 3 * part
    outputs = [
        (small.shape[0] + rows // 2, head),
        (rows // 2, head),
        (rows // 2, tail),
        (rows // 2, tail),
    ]
    return pl.pallas_call(
        prepare_body,
        in_specs=[pl.BlockSpec(memory_space=pltpu.HBM)] * 2 + [VM],
        out_specs=[VM] * len(outputs),
        out_shape=[pltpu.VMEM(shape, BF16) for shape in outputs],
        scratch_shapes=[
            pltpu.VMEM(heads_in.shape, BF16),
            pltpu.VMEM(heads_out.shape, BF16),
            pltpu.SemaphoreType.DMA((2,)),
        ],
        compiler_params=pltpu.CompilerParams(vmem_limit_bytes=4 * 1024 * 1024),
        name="prepare",
    )(heads_in, heads_out, small)


def join_body(a0, a1, b0, b1, a_ref, b_ref):
    for first, second, target in ((a0, a1, a_ref), (b0, b1, b_ref)):
        target[: first.shape[0], :] = first[...]
        target[first.shape[0] :, :] = second[...]


def join(own, got):
    outputs = [((2 * x.shape[0], x.shape[1]), BF16) for x in own]
    return call(join_body, "join", (own[0], got[0], own[1], got[1]), outputs, [], 4, 1e6)


def attend_body(first, images, places, order_ref, source_ref, *refs):
    pieces, refs = refs[:12], refs[12:]
    features = source_ref.shape[1]
    rows = features // 8
    if first:
        act_ref, small_ref, weight, joint_ref, prob_ref, mixed_ref = refs
        extra = small_ref.shape[0]
    else:
        out_weight, weight, joint_ref, prob_ref, mixed_ref = refs
        act_ref = source_ref
        extra = 0
    tall = source_ref.shape[0] // images
    width = weight.shape[1]
    place_pieces(order_ref, pieces, rows, extra, weight, slice(0, width))
    if first:
        gather_small(order_ref, pieces, rows, extra, small_ref)

        for i in range(images):
            here = rows_of(i, tall)
            normed, _ = normalize(source_ref[here, :].astype(F32))
            act_ref[here, :] = (normed * small_ref[0:1, :]).astype(BF16)
    else:
        place_pieces(order_ref, pieces, rows, 0, out_weight, slice(width, width + features))

    for i in range(images // 2):
        here = rows_of(i, 2 * tall)
        joint_ref[here, :] = dot(act_ref[here, :], weight[...]).astype(BF16)

    third = width // 3
    heads = prob_ref.shape[0] // images
    low = iota((tall, LANES), 1) < LANES // 2
    inside = iota((tall, LANES), 0) < places
    seen = iota((tall, tall), 1) < places

    def attend_image(i):
        here = rows_of(i, tall)
        for pair in range(third // LANES):
            query, keys, values = (
                joint_ref[here, part * third + pair * LANES : part * third + (pair + 1) * LANES]
                for part in range(3)
            )
            query = query * 0.125
            values_ones = jnp.concatenate([values, jnp.ones_like(values)], axis=1)
            outs = []
            for side in range(2):
                mine = low if side == 0 else ~low
                scores = dot(jnp.where(mine, query, 0), keys, NT)
                scores = jnp.where(seen, scores, LOW)
                power = jnp.exp(scores - jnp.max(scores, axis=1, keepdims=True)).astype(BF16)
                got = dot(power, values_ones)
                shrink = 1.0 / got[:, LANES:]
                outs.append(got[:, :LANES] * shrink)
                shrink = jnp.concatenate([shrink, shrink[:, : tall - LANES]], axis=1)
                prob_ref[i * heads + 2 * pair + side] = (power.astype(F32) * shrink).astype(BF16)
            mixed = jnp.where(inside, jnp.where(low, outs[0], outs[1]), 0.0)
            mixed_ref[here, pair * LANES : (pair + 1) * LANES] = mixed.astype(BF16)

    each_image(images, 2, attend_image)


def attend(first, images, places, order, source, pieces, width):
    total, features = source.shape
    tall = total // images
    heads = width // 3 // 64
    extra = pieces[0].shape[0] - features // 16
    outputs = [
        ((features, width), BF16),
        ((total, width), BF16),
        ((images * heads, tall, tall), BF16),
        ((total, width // 3), BF16),
    ]
    if first:
        outputs = [((total, features), BF16), ((extra, features), F32)] + outputs
    else:
        outputs = [((features, features), BF16)] + outputs
    return call(
        functools.partial(attend_body, first, images, places),
        "attend",
        (order, source, *pieces),
        outputs,
        [],
        12,
        2 * total * features * width * 2,
    )


def softmaxes(logits, places, experts):
    rows = iota(logits.shape, 0) < experts
    lanes = iota(logits.shape, 1) < places
    wide = jnp.where(lanes, logits, LOW)
    wide = jnp.exp(wide - jnp.max(wide, axis=1, keepdims=True))
    dispatch = wide / jnp.sum(wide, axis=1, keepdims=True)
    tall = jnp.where(rows, logits, LOW)
    tall = jnp.exp(tall - jnp.max(tall, axis=0, keepdims=True))
    combine = tall / jnp.sum(tall, axis=0, keepdims=True)
    return jnp.where(rows, dispatch, 0.0), combine


def slot_rows_of(experts, order_ref, small_ref, slots):
    rows = small_ref.shape[0]
    slot, row = iota((slots, rows), 0), iota((slots, rows), 1)
    chip = order_ref[order_ref.shape[0] - 1]
    fits = (row == (slot ^ chip) + 2) & (slot < experts)
    return dot(jnp.where(fits, 1.0, 0.0).astype(BF16), small_ref[...].astype(BF16)).astype(BF16)


def pick_rows(shape, wanted):
    row, column = iota(shape, 0), iota(shape, 1)
    return jnp.where(column == wanted(row), 1.0, 0.0).astype(BF16)


def route_body(
    images, places, experts, order_ref, token_ref, cot_ref, m0, m1, weight, small_ref,
    resid_ref, logit_ref, *refs,
):
    out_refs, packed_ref = refs[:-1], refs[-1]
    slots = logit_ref.shape[0] // images
    router = slot_rows_of(experts, order_ref, small_ref, slots)
    tall = token_ref.shape[0] // images
    features = token_ref.shape[1]

    for i in range(images // 2):
        here = rows_of(i, 2 * tall)
        mixed = jnp.concatenate([m0[here, :], m1[here, :]], axis=1)
        resid_ref[here, :] = token_ref[here, :].astype(F32) + dot(mixed, weight[...])

    def route_image(i):
        here = rows_of(i, tall)
        normed, _ = normalize(resid_ref[here, :])
        act = (normed * small_ref[1:2, :]).astype(BF16)
        logits = dot(router, act, NT)
        group = rows_of(i, slots)
        logit_ref[group, :] = logits
        dispatch, combine = softmaxes(logits, places, experts)
        packed_ref[group, :features] = dot(dispatch.astype(BF16), act).astype(BF16)
        packed_ref[group, features:] = dot(combine.astype(BF16), cot_ref[here, :]).astype(BF16)

    each_image(images, 6, route_image)

    high = out_refs[0].shape[0]
    pick = pick_rows(
        (experts * high, images * slots),
        lambda n: jnp.where(n % high < images, n % high * slots + n // high, -1),
    )
    packed = dot(pick, packed_ref[...]).astype(BF16)
    for k, out_ref in enumerate(out_refs):
        out_ref[...] = packed[k * high : (k + 1) * high, :]


def route(images, places, experts, slots, order, tokens, cot, mixed, w, small):
    total, features = tokens.shape
    high = -(-images // 8) * 8
    return call(
        functools.partial(route_body, images, places, experts),
        "route",
        (order, tokens, cot, *mixed, w, small),
        [((total, features), F32), ((images * slots, total // images), F32)]
        + [((high, 2 * features), BF16)] * experts,
        [((images * slots, 2 * features), BF16)],
        10,
        4 * total * features * features,
    )


def gelu_parts(values):
    scale, cubic = 0.7978845608028654, 0.044715
    square = values * values
    bent = jnp.tanh(scale * values * (1.0 + cubic * square))
    half = 0.5 * (1.0 + bent)
    slope = half + 0.5 * values * (1.0 - bent * bent) * scale * (1.0 + 3.0 * cubic * square)
    return values * half, slope


def expert_body(count, images, in_ref, out_ref, *refs):
    sources, (packed_ref, keep_ref, give_ref, rows_ref, back_ref) = refs[:count], refs[count:]
    features = in_ref.shape[0]
    high = sources[0].shape[0]
    for k, source in enumerate(sources):
        rows_ref[k * high : (k + 1) * high, :] = source[...]
    rows, arriving = rows_ref[:, :features], rows_ref[:, features:]
    total = jnp.zeros((rows.shape[0], features), F32)
    grad_total = total
    step = 512
    for start in range(0, in_ref.shape[1], step):
        w_in = in_ref[:, start : start + step]
        w_out = out_ref[start : start + step, :]
        hidden, slope = gelu_parts(dot(rows, w_in))
        grad_pre = (dot(arriving, w_out, NT) * slope).astype(BF16)
        total = total + dot(hidden.astype(BF16), w_out)
        grad_total = grad_total + dot(grad_pre, w_in, NT)
    back_ref[:, :features] = total.astype(BF16)
    back_ref[:, features:] = grad_total.astype(BF16)
    half = keep_ref.shape[0]
    keep_ref[...] = back_ref[:half, :]
    give_ref[...] = back_ref[half:, :]
    pick = pick_rows(
        (packed_ref.shape[0], rows_ref.shape[0]), lambda n: n // images * high + n % images
    )
    packed_ref[...] = dot(pick, rows_ref[...]).astype(BF16)


def expert(images, piece_in, piece_out, sources):
    high, wide = sources[0].shape
    rows = high * len(sources)
    return call(
        functools.partial(expert_body, len(sources), images),
        "expert",
        (piece_in, piece_out, *sources),
        [
            ((images * len(sources), wide), BF16),
            ((rows // 2, wide), BF16),
            ((rows // 2, wide), BF16),
        ],
        [((rows, wide), BF16)] * 2,
        8,
        1e9,
    )


def pair_sum_body(parts, keep_ref, *refs):
    got_refs, out_refs = refs[:parts], refs[parts:]
    rows = out_refs[0].shape[0]
    each = len(out_refs) // parts
    for k, out_ref in enumerate(out_refs):
        kept = keep_ref[k * rows : (k + 1) * rows, :].astype(F32)
        got = got_refs[k // each][k % each * rows : (k % each + 1) * rows, :].astype(F32)
        out_ref[...] = (kept + got).astype(BF16)


def pair_sum(keep, got, count):
    shape = (keep.shape[0] // count, keep.shape[1])
    body = functools.partial(pair_sum_body, len(got))
    return call(body, "pair_sum", (keep, *got), [(shape, BF16)] * count, [], 4, 1e6)


def total_body(*refs):
    refs[-1][...] = sum(ref[...].astype(F32) for ref in refs[:-1]).astype(BF16)


def total_sum(*terms):
    return call(total_body, "total_sum", terms, [(terms[0].shape, BF16)], [], 4, 1e6)[0]


def split_sum_body(order_ref, *refs):
    terms, (mine_ref, give_ref, scratch) = refs[:-3], refs[-3:]
    scratch[...] = sum(ref[...].astype(F32) for ref in terms)
    half = mine_ref.shape[0]
    odd = order_ref[order_ref.shape[0] - 2]
    mine = pl.multiple_of(odd * half, 16)
    other = pl.multiple_of((1 - odd) * half, 16)
    mine_ref[...] = scratch[pl.ds(mine, half), :].astype(BF16)
    give_ref[...] = scratch[pl.ds(other, half), :].astype(BF16)


def split_sum(order, *terms):
    rows, wide = terms[0].shape
    shape = (rows // 2, wide)
    return call(
        split_sum_body, "split_sum", (order, *terms), [(shape, BF16)] * 2, [((rows, wide), F32)], 8, 1e6
    )


def shares_body(
    experts, order_ref, head_ref, head_other, tail_ref, tail_other, w_ref, gain_ref,
    in_ref, out_ref, router_ref, gain_one_ref, gain_two_ref, tail,
):
    rows, features = out_ref.shape
    half = rows // 2
    odd = order_ref[order_ref.shape[0] - 2]
    tail[pl.ds(pl.multiple_of(odd * half, 16), half), :] = tail_ref[...].astype(F32)
    tail[pl.ds(pl.multiple_of((1 - odd) * half, 16), half), :] = tail_other[...].astype(F32)
    part = first_part(features)
    left = features - part
    for k in range(3):
        here = slice(k * part, (k + 1) * part)
        in_ref[:, k * features : k * features + part] = (
            head_ref[:, here].astype(F32) + head_other[:, here].astype(F32)
        )
        in_ref[:, k * features + part : (k + 1) * features] = tail[:, k * left : (k + 1) * left]
    out_ref[...] = tail[:, 3 * left : 3 * left + features]
    rest = tail[:, 3 * left + features :]
    rest = rest.T
    router_ref[...] = rest[:experts, :]
    gain_two_ref[...] = rest[experts : experts + 1, :]
    gain_one = jnp.sum(in_ref[...] * w_ref[...].astype(F32), axis=1, keepdims=True)
    gain_one = jnp.broadcast_to(gain_one, (rows, LANES)).T[:1, :]
    gain_one_ref[...] = gain_one / gain_ref[...].astype(F32)


def shares(experts, order, head, head_other, tail, tail_other, w, gain):
    rows, features = w.shape[0], w.shape[1] // 3
    return call(
        functools.partial(shares_body, experts),
        "shares",
        (order, head, head_other, tail, tail_other, w, gain),
        [
            (w.shape, F32),
            ((rows, features), F32),
            ((experts, rows), F32),
            ((1, rows), F32),
            ((1, rows), F32),
        ],
        [((rows, tail.shape[1]), F32)],
        8,
        1e6,
        hbm=range(5),
    )


def expert_grad_body(count, *refs):
    sources, (in_ref, out_ref, grad_in_ref, grad_out_ref) = refs[:count], refs[count:]
    features = in_ref.shape[0]
    every = jnp.concatenate([source[...] for source in sources], axis=0)
    rows, arriving = every[:, :features], every[:, features:]
    hidden, slope = gelu_parts(dot(rows, in_ref[...]))
    grad_pre = (dot(arriving, out_ref[...], NT) * slope).astype(BF16)
    grad_in_ref[...] = dot(rows, grad_pre, TN)
    grad_out_ref[...] = dot(hidden.astype(BF16), arriving, TN)


def expert_grad(sources, piece_in, piece_out):
    features, hidden = piece_in.shape
    step = 256
    wide = pl.BlockSpec((features, step), lambda i: (0, i))
    high = pl.BlockSpec((step, features), lambda i: (i, 0))
    return pl.pallas_call(
        functools.partial(expert_grad_body, len(sources)),
        grid=(hidden // step,),
        in_specs=[pl.BlockSpec(x.shape, lambda i: (0, 0)) for x in sources] + [wide, high],
        out_specs=[wide, high],
        out_shape=[
            jax.ShapeDtypeStruct(piece_in.shape, F32),
            jax.ShapeDtypeStruct(piece_out.shape, F32),
        ],
        compiler_params=pltpu.CompilerParams(vmem_limit_bytes=16 * 1024 * 1024),
        cost_estimate=pl.CostEstimate(
            flops=1600 * piece_in.size, bytes_accessed=14000000, transcendentals=0
        ),
        name="expert_grad",
    )(*sources, piece_in, piece_out)


def back_body(
    images, places, experts, order_ref, resid_ref, logit_ref, cot_ref, m0, m1, weight, small_ref, *refs
):
    sources, refs = refs[:experts], refs[experts:]
    output_ref, att_ref, grad_mixed_ref, grad_w_ref, grad_side_ref, summed_ref = refs
    slots = logit_ref.shape[0] // images
    router = slot_rows_of(experts, order_ref, small_ref, slots)
    total, features = resid_ref.shape
    tall = total // images
    gain = small_ref[1:2, :]
    high = sources[0].shape[0]
    pick = pick_rows(
        (images * slots, experts * high),
        lambda n: jnp.where(n % slots < experts, n % slots * high + n // slots, -1),
    )
    arrived = jnp.concatenate([source[...] for source in sources], axis=0)
    summed_ref[...] = dot(pick, arrived).astype(BF16)

    def image(i, carry):
        side, gain_sum = carry
        here = rows_of(i, tall)
        group = rows_of(i, slots)
        expert_sum, grad_slots = summed_ref[group, :features], summed_ref[group, features:]
        resid = resid_ref[here, :]
        cot = cot_ref[here, :]
        dispatch, combine = softmaxes(logit_ref[group, :], places, experts)
        output = resid + dot(combine.astype(BF16), expert_sum, TN)
        output_ref[i] = output[:places].astype(BF16)
        normed, factor = normalize(resid)
        act = (normed * gain).astype(BF16)
        grad_comb = dot(expert_sum, cot, NT)
        grad_disp = dot(grad_slots, act, NT)
        grad_logits = combine * (grad_comb - jnp.sum(grad_comb * combine, axis=0, keepdims=True))
        grad_logits = grad_logits + dispatch * (
            grad_disp - jnp.sum(grad_disp * dispatch, axis=1, keepdims=True)
        )
        grad_logits = grad_logits.astype(BF16)
        grad_act = dot(
            jnp.concatenate([dispatch.astype(BF16), grad_logits], axis=0),
            jnp.concatenate([grad_slots, router], axis=0),
            TN,
        )
        att = cot.astype(F32) + norm_back(grad_act * gain, normed, factor)
        att_ref[here, :] = att.astype(BF16)
        return (
            side + dot(grad_logits, act),
            gain_sum + jnp.sum(grad_act * normed, axis=0, keepdims=True),
        )

    together = 3 if images % 3 == 0 else 1

    def some(step, carry):
        for k in range(together):
            carry = image(step * together + k, carry)
        return carry

    carry = (jnp.zeros((slots, features), F32), jnp.zeros((1, features), F32))
    side, gain_sum = lax.fori_loop(0, images // together, some, carry)

    for i in range(images // 2):
        here = rows_of(i, 2 * tall)
        grad_mixed_ref[here, :] = dot(att_ref[here, :], weight[...], NT).astype(BF16)

    part = m0.shape[1]
    grad_w_ref[:part, :] = dot(m0[...], att_ref[...], TN).astype(BF16)
    grad_w_ref[part:, :] = dot(m1[...], att_ref[...], TN).astype(BF16)
    slot = iota((LANES, slots), 0) ^ order_ref[order_ref.shape[0] - 1]
    slot = jnp.where(iota((LANES, slots), 0) < experts, slot, -1)
    fits = jnp.where(slot == iota((LANES, slots), 1), 1.0, 0.0).astype(BF16)
    side = dot(fits, side.astype(BF16))
    side = jnp.where(iota(side.shape, 0) == experts, gain_sum, side)
    grad_side_ref[...] = side.T.astype(BF16)


def back(images, places, experts, order, resid, logits, cot, mixed, w, small, sources):
    total, features = resid.shape
    return call(
        functools.partial(back_body, images, places, experts),
        "back",
        (order, resid, logits, cot, *mixed, w, small, *sources),
        [
            ((images, places, features), BF16),
            ((total, features), BF16),
            ((total, features), BF16),
            ((features, features), BF16),
            ((features, LANES), BF16),
        ],
        [((logits.shape[0], 2 * features), BF16)],
        14,
        8 * total * features * features,
        hbm=(0,),
    )


def attend_back_body(images, extra, offset, order_ref, joint_ref, prob_ref, grad_ref, mixed_ref, act_ref, *refs):
    more, (out_ref, *targets, total) = refs[:extra], refs[extra:]
    width = joint_ref.shape[1]
    tall = joint_ref.shape[0] // images
    third = width // 3
    heads = prob_ref.shape[0] // images
    low = iota((tall, LANES), 1) < LANES // 2

    def back_image(i):
        here = rows_of(i, tall)
        for pair in range(third // LANES):
            query, keys, values = (
                joint_ref[here, part * third + pair * LANES : part * third + (pair + 1) * LANES]
                for part in range(3)
            )
            grad = grad_ref[here, offset + pair * LANES : offset + (pair + 1) * LANES]
            product = grad.astype(F32) * mixed_ref[
                here, pair * LANES : (pair + 1) * LANES
            ].astype(F32)
            query_high, grad_high = query.T, grad.T
            grad_query, grad_keys, grad_values = [], [], []
            for side in range(2):
                mine = low if side == 0 else ~low
                rows = slice(side * LANES // 2, (side + 1) * LANES // 2)
                prob = prob_ref[i * heads + 2 * pair + side]
                inner = jnp.sum(jnp.where(mine, product, 0.0), axis=1, keepdims=True)
                grad_prob = dot(jnp.where(mine, grad, 0), values, NT)
                grad_scores = (prob.astype(F32) * (grad_prob - inner)).astype(BF16)
                grad_query.append(dot(grad_scores, keys))
                grad_keys.append(dot(query_high[rows], grad_scores))
                grad_values.append(dot(grad_high[rows], prob))
            joined = (
                (jnp.where(low, *grad_query) * 0.125).astype(BF16),
                (jnp.concatenate(grad_keys, axis=0) * 0.125).astype(BF16).T,
                jnp.concatenate(grad_values, axis=0).astype(BF16).T,
            )
            for part in range(3):
                out_ref[
                    here, part * third + pair * LANES : part * third + (pair + 1) * LANES
                ] = joined[part]

    each_image(images, 2, back_image)

    step = third
    for start in range(0, width, step):
        total[:, start : start + step] = dot(
            act_ref[...], out_ref[:, start : start + step], TN
        ).astype(BF16)
    store_blocks(order_ref, total, targets, slice(0, width))
    place = width
    for source in more:
        end = place + source.shape[1]
        store_blocks(order_ref, source, targets, slice(place, end))
        place = end


def attend_back(images, offset, order, joint, prob, grad_mixed, mixed, act, splits, more=()):
    total, width = joint.shape
    features = act.shape[1]
    columns = width + sum(m.shape[1] for m in more)
    parts = [((features // n, columns), BF16) for n in splits]
    return call(
        functools.partial(attend_back_body, images, len(more), offset),
        "attend_back",
        (order, joint, prob, grad_mixed, mixed, act, *more),
        [(joint.shape, BF16)] + parts,
        [((features, width), BF16)],
        16,
        2 * total * features * width * 4,
    )


def finish_body(images, places, token_ref, att_ref, j0, j1, s0, s1, small_ref, out_ref):
    total, features = token_ref.shape
    tall = total // images

    @pl.loop(0, images // 2)
    def _(i):
        here = rows_of(i, 2 * tall)
        grad_act = dot(j0[here, :], s0[...], NT) + dot(j1[here, :], s1[...], NT)
        normed, factor = normalize(token_ref[here, :].astype(F32))
        result = att_ref[here, :].astype(F32)
        result = result + norm_back(grad_act * small_ref[0:1, :], normed, factor)
        result = result.astype(BF16)
        out_ref[2 * i] = result[:places]
        out_ref[2 * i + 1] = result[tall : tall + places]


def finish(images, places, tokens, att, joints, weights, small):
    total, features = tokens.shape
    return call(
        functools.partial(finish_body, images, places),
        "finish",
        (tokens, att, *joints, *weights, small),
        [((images, places, features), BF16)],
        [],
        12,
        6 * total * features * features,
        hbm=(0,),
    )[0]


def per_device(
    tokens, cotangent, heads_in, heads_out, slot_router, first_gain, second_gain, expert_in, expert_out
):
    images, places, features = tokens.shape
    experts = slot_router.shape[1]
    group = lax.axis_size("grp")
    reps = lax.axis_size("rep")
    me = lax.axis_index("grp")
    own_rows = heads_in.shape[0]
    chip = me // 2
    odd = lax.axis_index("rep") % 2
    direct = group == 8
    ways = jnp.arange(8, dtype=jnp.int32)
    if direct:
        order = jnp.concatenate([ways ^ me, (ways % 4 * 2 + ways // 4) ^ me, odd[None], chip[None]])
    else:
        order = jnp.concatenate([ways, ways, odd[None], chip[None]])
    tall = -(-places // 16) * 16
    slot_rows = -(-experts // 16) * 16
    part = first_part(features)
    rest = features - part
    wide = 3 * part

    grow = ((0, 0), (0, tall - places), (0, 0))
    source = jnp.pad(tokens, grow).reshape(images * tall, features)
    cot = jnp.pad(cotangent, grow).reshape(images * tall, features)
    if direct:
        rows_in, order = lax.optimization_barrier((heads_in, order))
        small = jnp.concatenate([first_gain[None], second_gain[None], slot_router.T], axis=0)
        extra = -(-small.shape[0] // 16) * 16
        small = jnp.pad(small, ((0, extra - small.shape[0]), (0, LANES - own_rows)))
        h0, h1, t0, t1 = prepare(rows_in, heads_out, small)
        head_first = gather_first((h0, h1))
        head_first = after(head_first, source, cot)
        (t0, t1), head_first = lax.optimization_barrier(((t0, t1), head_first))
        head_second = gather_second(join((h0, h1), head_first))
        tail_first = gather_first((t0, t1))
        head = gather_last((h0, h1), head_first, head_second)
        tail_first = after(tail_first, *head)
        tail_join = join((t0, t1), tail_first)
        source = after(source, *tail_join)
    else:
        thirds = [heads_in[:, k * features : (k + 1) * features] for k in range(3)]
        head_part = jnp.concatenate([t[:, :part] for t in thirds], axis=1)
        tail_part = jnp.concatenate([t[:, part:] for t in thirds] + [heads_out], axis=1)
        small = jnp.concatenate([first_gain[None], second_gain[None], slot_router.T], axis=0)
        extra = -(-small.shape[0] // 16) * 16
        head_part = lax.all_gather(head_part, "grp", axis=0, tiled=True).reshape(8, -1, wide)
        small = lax.all_gather(small, "grp", axis=1, tiled=True).reshape(-1, 8, features // 8)
        small = small.transpose(1, 0, 2)
        small = jnp.pad(small, ((0, 0), (0, extra - small.shape[1]), (0, wide - small.shape[2])))
        head = as_gathered(jnp.concatenate([small, head_part], axis=1), extra + features // 16)
        tail_part = lax.all_gather(tail_part, "grp", axis=0, tiled=True)
        tail = as_gathered(tail_part.reshape(8, -1, 3 * rest + features), features // 16)

    act, small, w_head, joint_head, prob_head, mixed_head = attend(
        True, images, places, order, source, head, wide
    )
    if direct:
        tail_second = after(gather_second(tail_join), mixed_head)
        tail = gather_last((t0, t1), tail_first, tail_second)
    w_out, w_tail, joint_tail, prob_tail, mixed_tail = attend(
        False, images, places, order, act, tail, 3 * rest
    )
    mixes = [mixed_head, mixed_tail]
    resid, logits, *leaving = route(
        images, places, experts, slot_rows, order, source, cot, mixes, w_out, small
    )

    arrived = [leaving[0]] + [swap(leaving[k], "grp", group, 2 * k) for k in range(1, experts)]
    arrived = arrived + [swap(part, "grp", group, 1) for part in arrived]
    piece_in, piece_out = expert_in[0], expert_out[0]
    received, kept, given = expert(images, piece_in, piece_out, arrived)
    both = pair_sum(kept, [swap(given, "grp", group, 1)], experts)
    summed = [both[0]] + [swap(both[k], "grp", group, 2 * k) for k in range(1, experts)]
    received = after(received, *both)
    far = [swap(received, "rep", reps, k) for k in range(1, reps)]
    output, att, grad_mixed, grad_out, grad_side = back(
        images, places, experts, order, resid, logits, cot, mixes, w_out, small, summed
    )
    grad_mixed, far = lax.optimization_barrier((grad_mixed, far))
    grad_joint_tail, keep_tail, give_tail = attend_back(
        images, part, order, joint_tail, prob_tail, grad_mixed, mixed_tail, act, (2, 2), (grad_out, grad_side)
    )
    if direct:
        sums = pair_sum(keep_tail, [swap(give_tail, "grp", group, 1)], 4)
        others = [swap(sums[k], "grp", group, 2 * k) for k in range(1, 4)]
        grad_mixed = after(grad_mixed, *sums)
    grad_joint_head, keep_head, *give_head = attend_back(
        images, 0, order, joint_head, prob_head, grad_mixed, mixed_head, act, (2, 4, 4)
    )
    joints, weights = [grad_joint_head, grad_joint_tail], [w_head, w_tail]
    every = [received] + far
    if direct:
        got = [swap(part, "grp", group, 1) for part in give_head]
        own, others = after((sums[0], others), got)
        mine, give = split_sum(order, own, *others)
        other = swap(give, "rep", reps, 1)
        sums = pair_sum(keep_head, got, 4)
        others = [swap(sums[k], "grp", group, 2 * k) for k in range(1, 4)]
        att = after(att, mine, *sums)
        token_grad = finish(images, places, source, att, joints, weights, small)
        own, others, other = after((sums[0], others, other), token_grad)
        tail_sum = total_sum(mine, other)
        head_sum = total_sum(own, *others)
        every, tail_sum, head_sum = after((every, tail_sum, head_sum), token_grad)
        tail_other = swap(tail_sum, "rep", reps, 2)
        head_other = swap(head_sum, "rep", reps, 1)
        expert_in_grad, expert_out_grad = expert_grad(every, piece_in, piece_out)
        tail_other, head_other = after((tail_other, head_other), expert_in_grad)
        tail_sum, head_sum = total_sum(tail_sum, tail_other), total_sum(head_sum, head_other)
        tail_other = swap(tail_sum, "rep", reps, 1)
        head_other = swap(head_sum, "rep", reps, 3)
        heads_in_grad, heads_out_grad, router_grad, gain_one_grad, gain_two_grad = shares(
            experts, order, head_sum, head_other, tail_sum, tail_other, heads_in, first_gain[None]
        )
        gain_one_grad, gain_two_grad = gain_one_grad[0], gain_two_grad[0]
        router_grad = router_grad.T
    else:
        token_grad = finish(images, places, source, att, joints, weights, small)
        expert_in_grad, expert_out_grad = expert_grad(every, piece_in, piece_out)
        tail_sum = jnp.concatenate([keep_tail, give_tail])
        tail_sum = lax.psum_scatter(tail_sum, "grp", scatter_dimension=0, tiled=True)
        head_sum = jnp.concatenate([keep_head, *give_head])
        head_sum = lax.psum_scatter(head_sum, "grp", scatter_dimension=0, tiled=True)
        tail_sum = lax.psum(tail_sum, "rep").astype(F32)
        head_sum = lax.psum(head_sum, "rep").astype(F32)
        columns = []
        for k in range(3):
            columns.append(head_sum[:, k * part : (k + 1) * part])
            columns.append(tail_sum[:, k * rest : (k + 1) * rest])
        heads_in_grad = jnp.concatenate(columns, axis=1)
        gain_one_grad = jnp.sum(heads_in_grad * heads_in.astype(F32), axis=1)
        gain_one_grad = gain_one_grad / first_gain.astype(F32)
        tail_sum = tail_sum[:, 3 * rest :]
        heads_out_grad, tail_sum = tail_sum[:, :features], tail_sum[:, features:]
        router_grad, gain_two_grad = tail_sum[:, :experts], tail_sum[:, experts]
    return (
        output,
        token_grad,
        heads_in_grad,
        heads_out_grad,
        router_grad,
        gain_one_grad,
        gain_two_grad,
        expert_in_grad[None],
        expert_out_grad[None],
    )


def solution(mesh):
    token_spec = P(("rep", "grp"), None, None)
    matrix, vector, stack = P("grp", None), P("grp"), P("grp", None, None)
    return jax.shard_map(
        per_device,
        mesh=mesh,
        in_specs=(token_spec, token_spec, matrix, matrix, matrix, vector, vector, stack, stack),
        out_specs=(token_spec, token_spec, matrix, matrix, matrix, vector, vector, stack, stack),
        check_vma=False,
    )
```

```python
import functools

import jax
import jax.numpy as jnp
from jax import lax
from jax.experimental import pallas as pl
from jax.experimental.pallas import tpu as pltpu
from jax.sharding import PartitionSpec as P

HEADS = 12
LANES = 128
F32 = jnp.float32
BF16 = jnp.bfloat16
LOW = -1e30

NN = (((1,), (0,)), ((), ()))
NT = (((1,), (1,)), ((), ()))
TN = (((0,), (0,)), ((), ()))


def dot(left, right, form=NN):
    return lax.dot_general(left, right, form, preferred_element_type=F32)


def swap(values, axis, size, bit):
    return lax.ppermute(values, axis, [(place, place ^ bit) for place in range(size)])


def after(values, *others):
    return lax.optimization_barrier((values, others))[0]


def gather_first(own):
    return swap(own[0], "grp", 8, 2), swap(own[1], "grp", 8, 4)


def gather_second(joined):
    return swap(joined[0], "grp", 8, 4), swap(joined[1], "grp", 8, 2)


def gather_last(*stages):
    held = tuple(part for stage in stages for part in stage)
    return held + tuple(swap(part, "grp", 8, 1) for part in held)


def as_gathered(blocks, cut):
    held = []
    for k in range(2):
        own, x, y, far = blocks[k], blocks[k + 2], blocks[k + 4], blocks[k + 6]
        held += [own[:cut], own[cut:], x[:cut], y[cut:]]
        held += [jnp.concatenate([y[:cut], far[:cut]]), jnp.concatenate([x[cut:], far[cut:]])]
    return tuple(held)


def iota(shape, axis):
    return lax.broadcasted_iota(jnp.int32, shape, axis)


def normalize(values):
    center = values - jnp.mean(values, axis=-1, keepdims=True)
    factor = lax.rsqrt(jnp.mean(center * center, axis=-1, keepdims=True) + 1e-06)
    return center * factor, factor


def norm_back(scaled, normed, factor):
    inner = (
        scaled
        - jnp.mean(scaled, axis=-1, keepdims=True)
        - normed * jnp.mean(scaled * normed, axis=-1, keepdims=True)
    )
    return factor * inner


def first_part(features):
    return features // 3


def pieces_of(rows, extra):
    half = rows // 2
    cut = extra + half
    for core in range(2):
        base = 6 * core
        yield base, extra, core, 0
        yield base + 1, 0, core, half
        yield base + 2, extra, core + 2, 0
        yield base + 3, 0, core + 4, half
        yield base + 4, extra, core + 4, 0
        yield base + 4, cut + extra, core + 6, 0
        yield base + 5, 0, core + 2, half
        yield base + 5, half, core + 6, half


def place_pieces(order_ref, pieces, rows, extra, target, columns):
    half = rows // 2
    for n, start, block, offset in pieces_of(rows, extra):
        place = pl.multiple_of(order_ref[block] * rows + offset, 16)
        target[pl.ds(place, half), :] = pieces[n][start : start + half, columns]


def store_blocks(order_ref, source, targets, columns):
    rows = source.shape[0] // 8
    n = 0
    for target in targets:
        for k in range(target.shape[0] // rows):
            start = pl.multiple_of(order_ref[8 + n] * rows, 32)
            target[k * rows : (k + 1) * rows, columns] = source[pl.ds(start, rows), :].astype(BF16)
            n += 1


def gather_small(order_ref, pieces, rows, extra, small_ref):
    total = jnp.zeros(small_ref.shape, F32)
    lane = iota((LANES, small_ref.shape[1]), 0)
    place = iota((LANES, small_ref.shape[1]), 1)
    cut = extra + rows // 2
    for core in range(2):
        for n, start, block in ((0, 0, 0), (2, 0, 2), (4, 0, 4), (4, cut, 6)):
            held = pieces[6 * core + n][start : start + extra, :LANES]
            fits = (place == order_ref[block + core] * rows + lane) & (lane < rows)
            total = total + dot(held, jnp.where(fits, 1.0, 0.0).astype(BF16))
    small_ref[...] = total


def rows_of(place, tall):
    return pl.ds(pl.multiple_of(place * tall, 16), tall)


def each_image(images, together, body):
    if images % together:
        together = 1
    if together == images:
        for i in range(images):
            body(i)
        return

    @pl.loop(0, images // together)
    def _(step):
        for k in range(together):
            body(step * together + k)


VM = pl.BlockSpec(memory_space=pltpu.VMEM)
SM = pl.BlockSpec(memory_space=pltpu.SMEM)


def call(body, name, inputs, outputs, scratch, limit, flops, hbm=()):
    return pl.pallas_call(
        body,
        in_specs=[SM if x.dtype == jnp.int32 else VM for x in inputs],
        out_specs=[VM] * len(outputs),
        out_shape=[
            jax.ShapeDtypeStruct(shape, kind) if n in hbm else pltpu.VMEM(shape, kind)
            for n, (shape, kind) in enumerate(outputs)
        ],
        scratch_shapes=[pltpu.VMEM(shape, kind) for shape, kind in scratch],
        compiler_params=pltpu.CompilerParams(vmem_limit_bytes=(limit if limit == 13 else min(limit, 10)) * 1024 * 1024),
        cost_estimate=pl.CostEstimate(flops=int(flops), bytes_accessed=1000000, transcendentals=0),
        name=name,
    )(*inputs)


def prepare_body(in_hbm, out_hbm, small_ref, h0, h1, t0, t1, in_ref, out_ref, sems):
    rows, features = out_ref.shape
    half = rows // 2
    part = first_part(features)
    rest = features - part
    extra = h0.shape[0] - half
    h0[:extra, :] = jnp.zeros((extra, h0.shape[1]), BF16)
    h0[:extra, :LANES] = small_ref[...]
    copies = [
        pltpu.make_async_copy(source, target, sems.at[k])
        for k, (source, target) in enumerate(((in_hbm, in_ref), (out_hbm, out_ref)))
    ]
    for copy in copies:
        copy.start()
    for copy in copies:
        copy.wait()
    for head, tail, start, here in ((h0, t0, extra, slice(0, half)), (h1, t1, 0, slice(half, rows))):
        for k in range(3):
            base = k * features
            head[start:, k * part : (k + 1) * part] = in_ref[here, base : base + part]
            tail[:, k * rest : (k + 1) * rest] = in_ref[here, base + part : base + features]
        tail[:, 3 * rest :] = out_ref[here, :]


def prepare(heads_in, heads_out, small):
    rows, features = heads_out.shape
    part = first_part(features)
    head, tail = 3 * part, 4 * features - 3 * part
    outputs = [
        (small.shape[0] + rows // 2, head),
        (rows // 2, head),
        (rows // 2, tail),
        (rows // 2, tail),
    ]
    return pl.pallas_call(
        prepare_body,
        in_specs=[pl.BlockSpec(memory_space=pltpu.HBM)] * 2 + [VM],
        out_specs=[VM] * len(outputs),
        out_shape=[pltpu.VMEM(shape, BF16) for shape in outputs],
        scratch_shapes=[
            pltpu.VMEM(heads_in.shape, BF16),
            pltpu.VMEM(heads_out.shape, BF16),
            pltpu.SemaphoreType.DMA((2,)),
        ],
        compiler_params=pltpu.CompilerParams(vmem_limit_bytes=4 * 1024 * 1024),
        name="prepare",
    )(heads_in, heads_out, small)


def join_body(a0, a1, b0, b1, a_ref, b_ref):
    for first, second, target in ((a0, a1, a_ref), (b0, b1, b_ref)):
        target[: first.shape[0], :] = first[...]
        target[first.shape[0] :, :] = second[...]


def join(own, got):
    outputs = [((2 * x.shape[0], x.shape[1]), BF16) for x in own]
    return call(join_body, "join", (own[0], got[0], own[1], got[1]), outputs, [], 4, 1e6)


def attend_body(first, images, places, order_ref, source_ref, *refs):
    pieces, refs = refs[:12], refs[12:]
    features = source_ref.shape[1]
    rows = features // 8
    if first:
        act_ref, small_ref, weight, joint_ref, prob_ref, mixed_ref = refs
        extra = small_ref.shape[0]
    else:
        out_weight, weight, joint_ref, prob_ref, mixed_ref = refs
        act_ref = source_ref
        extra = 0
    tall = source_ref.shape[0] // images
    width = weight.shape[1]
    place_pieces(order_ref, pieces, rows, extra, weight, slice(0, width))
    if first:
        gather_small(order_ref, pieces, rows, extra, small_ref)

        for i in range(images):
            here = rows_of(i, tall)
            normed, _ = normalize(source_ref[here, :].astype(F32))
            act_ref[here, :] = (normed * small_ref[0:1, :]).astype(BF16)
    else:
        place_pieces(order_ref, pieces, rows, 0, out_weight, slice(width, width + features))

    for i in range(images // 2):
        here = rows_of(i, 2 * tall)
        joint_ref[here, :] = dot(act_ref[here, :], weight[...]).astype(BF16)

    third = width // 3
    heads = prob_ref.shape[0] // images
    low = iota((tall, LANES), 1) < LANES // 2
    inside = iota((tall, LANES), 0) < places
    seen = iota((tall, tall), 1) < places

    def attend_image(i):
        here = rows_of(i, tall)
        for pair in range(third // LANES):
            query, keys, values = (
                joint_ref[here, part * third + pair * LANES : part * third + (pair + 1) * LANES]
                for part in range(3)
            )
            query = query * 0.125
            values_ones = jnp.concatenate([values, jnp.ones_like(values)], axis=1)
            outs = []
            for side in range(2):
                mine = low if side == 0 else ~low
                scores = dot(jnp.where(mine, query, 0), keys, NT)
                scores = jnp.where(seen, scores, LOW)
                power = jnp.exp(scores - jnp.max(scores, axis=1, keepdims=True)).astype(BF16)
                got = dot(power, values_ones)
                shrink = 1.0 / got[:, LANES:]
                outs.append(got[:, :LANES] * shrink)
                shrink = jnp.concatenate([shrink, shrink[:, : tall - LANES]], axis=1)
                prob_ref[i * heads + 2 * pair + side] = (power.astype(F32) * shrink).astype(BF16)
            mixed = jnp.where(inside, jnp.where(low, outs[0], outs[1]), 0.0)
            mixed_ref[here, pair * LANES : (pair + 1) * LANES] = mixed.astype(BF16)

    each_image(images, 2, attend_image)


def attend(first, images, places, order, source, pieces, width):
    total, features = source.shape
    tall = total // images
    heads = width // 3 // 64
    extra = pieces[0].shape[0] - features // 16
    outputs = [
        ((features, width), BF16),
        ((total, width), BF16),
        ((images * heads, tall, tall), BF16),
        ((total, width // 3), BF16),
    ]
    if first:
        outputs = [((total, features), BF16), ((extra, features), F32)] + outputs
    else:
        outputs = [((features, features), BF16)] + outputs
    return call(
        functools.partial(attend_body, first, images, places),
        "attend",
        (order, source, *pieces),
        outputs,
        [],
        12,
        1 if first else 2 * total * features * width * 2,
    )


def softmaxes(logits, places, experts):
    rows = iota(logits.shape, 0) < experts
    lanes = iota(logits.shape, 1) < places
    wide = jnp.where(lanes, logits, LOW)
    wide = jnp.exp(wide - jnp.max(wide, axis=1, keepdims=True))
    dispatch = wide / jnp.sum(wide, axis=1, keepdims=True)
    tall = jnp.where(rows, logits, LOW)
    tall = jnp.exp(tall - jnp.max(tall, axis=0, keepdims=True))
    combine = tall / jnp.sum(tall, axis=0, keepdims=True)
    return jnp.where(rows, dispatch, 0.0), combine


def slot_rows_of(experts, order_ref, small_ref, slots):
    rows = small_ref.shape[0]
    slot, row = iota((slots, rows), 0), iota((slots, rows), 1)
    chip = order_ref[order_ref.shape[0] - 1]
    fits = (row == (slot ^ chip) + 2) & (slot < experts)
    return dot(jnp.where(fits, 1.0, 0.0).astype(BF16), small_ref[...].astype(BF16)).astype(BF16)


def pick_rows(shape, wanted):
    row, column = iota(shape, 0), iota(shape, 1)
    return jnp.where(column == wanted(row), 1.0, 0.0).astype(BF16)


def route_body(
    images, places, experts, order_ref, token_ref, cot_ref, m0, m1, weight, small_ref,
    resid_ref, logit_ref, *refs,
):
    out_refs, packed_ref = refs[:-1], refs[-1]
    slots = logit_ref.shape[0] // images
    router = slot_rows_of(experts, order_ref, small_ref, slots)
    tall = token_ref.shape[0] // images
    features = token_ref.shape[1]

    for i in range(images // 2):
        here = rows_of(i, 2 * tall)
        mixed = jnp.concatenate([m0[here, :], m1[here, :]], axis=1)
        resid_ref[here, :] = token_ref[here, :].astype(F32) + dot(mixed, weight[...])

    def route_image(i):
        here = rows_of(i, tall)
        normed, _ = normalize(resid_ref[here, :])
        act = (normed * small_ref[1:2, :]).astype(BF16)
        logits = dot(router, act, NT)
        group = rows_of(i, slots)
        logit_ref[group, :] = logits
        dispatch, combine = softmaxes(logits, places, experts)
        packed_ref[group, :features] = dot(dispatch.astype(BF16), act).astype(BF16)
        packed_ref[group, features:] = dot(combine.astype(BF16), cot_ref[here, :]).astype(BF16)

    each_image(images, 6, route_image)

    high = out_refs[0].shape[0]
    pick = pick_rows(
        (experts * high, images * slots),
        lambda n: jnp.where(n % high < images, n % high * slots + n // high, -1),
    )
    packed = dot(pick, packed_ref[...]).astype(BF16)
    for k, out_ref in enumerate(out_refs):
        out_ref[...] = packed[k * high : (k + 1) * high, :]


def route(images, places, experts, slots, order, tokens, cot, mixed, w, small):
    total, features = tokens.shape
    high = -(-images // 8) * 8
    return call(
        functools.partial(route_body, images, places, experts),
        "route",
        (order, tokens, cot, *mixed, w, small),
        [((total, features), F32), ((images * slots, total // images), F32)]
        + [((high, 2 * features), BF16)] * experts,
        [((images * slots, 2 * features), BF16)],
        10,
        4 * total * features * features,
    )


def gelu_parts(values):
    scale, cubic = 0.7978845608028654, 0.044715
    square = values * values
    bent = jnp.tanh(scale * values * (1.0 + cubic * square))
    half = 0.5 * (1.0 + bent)
    slope = half + 0.5 * values * (1.0 - bent * bent) * scale * (1.0 + 3.0 * cubic * square)
    return values * half, slope


def expert_body(count, images, in_ref, out_ref, *refs):
    sources, (packed_ref, keep_ref, give_ref, rows_ref, back_ref) = refs[:count], refs[count:]
    features = in_ref.shape[0]
    high = sources[0].shape[0]
    for k, source in enumerate(sources):
        rows_ref[k * high : (k + 1) * high, :] = source[...]
    rows, arriving = rows_ref[:, :features], rows_ref[:, features:]
    total = jnp.zeros((rows.shape[0], features), F32)
    grad_total = total
    step = 512
    for start in range(0, in_ref.shape[1], step):
        w_in = in_ref[:, start : start + step]
        w_out = out_ref[start : start + step, :]
        hidden, slope = gelu_parts(dot(rows, w_in))
        grad_pre = (dot(arriving, w_out, NT) * slope).astype(BF16)
        total = total + dot(hidden.astype(BF16), w_out)
        grad_total = grad_total + dot(grad_pre, w_in, NT)
    back_ref[:, :features] = total.astype(BF16)
    back_ref[:, features:] = grad_total.astype(BF16)
    half = keep_ref.shape[0]
    keep_ref[...] = back_ref[:half, :]
    give_ref[...] = back_ref[half:, :]
    pick = pick_rows(
        (packed_ref.shape[0], rows_ref.shape[0]), lambda n: n // images * high + n % images
    )
    packed_ref[...] = dot(pick, rows_ref[...]).astype(BF16)


def expert(images, piece_in, piece_out, sources):
    high, wide = sources[0].shape
    rows = high * len(sources)
    return call(
        functools.partial(expert_body, len(sources), images),
        "expert",
        (piece_in, piece_out, *sources),
        [
            ((images * len(sources), wide), BF16),
            ((rows // 2, wide), BF16),
            ((rows // 2, wide), BF16),
        ],
        [((rows, wide), BF16)] * 2,
        8,
        1e9,
    )


def pair_sum_body(parts, keep_ref, *refs):
    got_refs, out_refs = refs[:parts], refs[parts:]
    rows = out_refs[0].shape[0]
    each = len(out_refs) // parts
    for k, out_ref in enumerate(out_refs):
        kept = keep_ref[k * rows : (k + 1) * rows, :].astype(F32)
        got = got_refs[k // each][k % each * rows : (k % each + 1) * rows, :].astype(F32)
        out_ref[...] = (kept + got).astype(BF16)


def pair_sum(keep, got, count):
    shape = (keep.shape[0] // count, keep.shape[1])
    body = functools.partial(pair_sum_body, len(got))
    return call(body, "pair_sum", (keep, *got), [(shape, BF16)] * count, [], 4, 1e6)


def total_body(*refs):
    refs[-1][...] = sum(ref[...].astype(F32) for ref in refs[:-1]).astype(BF16)


def total_sum(*terms):
    return call(total_body, "total_sum", terms, [(terms[0].shape, BF16)], [], 4, 1e6)[0]


def split_sum_body(order_ref, *refs):
    terms, (mine_ref, give_ref, scratch) = refs[:-3], refs[-3:]
    scratch[...] = sum(ref[...].astype(F32) for ref in terms)
    half = mine_ref.shape[0]
    odd = order_ref[order_ref.shape[0] - 2]
    mine = pl.multiple_of(odd * half, 16)
    other = pl.multiple_of((1 - odd) * half, 16)
    mine_ref[...] = scratch[pl.ds(mine, half), :].astype(BF16)
    give_ref[...] = scratch[pl.ds(other, half), :].astype(BF16)


def split_sum(order, *terms):
    rows, wide = terms[0].shape
    shape = (rows // 2, wide)
    return call(
        split_sum_body, "split_sum", (order, *terms), [(shape, BF16)] * 2, [((rows, wide), F32)], 8, 1e6
    )


def shares_body(
    experts, order_ref, head_ref, head_other, tail_ref, tail_other, w_ref, gain_ref,
    in_ref, out_ref, router_ref, gain_one_ref, gain_two_ref, tail,
):
    rows, features = out_ref.shape
    half = rows // 2
    odd = order_ref[order_ref.shape[0] - 2]
    tail[pl.ds(pl.multiple_of(odd * half, 16), half), :] = tail_ref[...].astype(F32)
    tail[pl.ds(pl.multiple_of((1 - odd) * half, 16), half), :] = tail_other[...].astype(F32)
    part = first_part(features)
    left = features - part
    for k in range(3):
        here = slice(k * part, (k + 1) * part)
        in_ref[:, k * features : k * features + part] = (
            head_ref[:, here].astype(F32) + head_other[:, here].astype(F32)
        )
        in_ref[:, k * features + part : (k + 1) * features] = tail[:, k * left : (k + 1) * left]
    out_ref[...] = tail[:, 3 * left : 3 * left + features]
    rest = tail[:, 3 * left + features :]
    rest = rest.T
    router_ref[...] = rest[:experts, :]
    gain_two_ref[...] = rest[experts : experts + 1, :]
    gain_one = jnp.sum(in_ref[...] * w_ref[...].astype(F32), axis=1, keepdims=True)
    gain_one = jnp.broadcast_to(gain_one, (rows, LANES)).T[:1, :]
    gain_one_ref[...] = gain_one / gain_ref[...].astype(F32)


def shares(experts, order, head, head_other, tail, tail_other, w, gain):
    rows, features = w.shape[0], w.shape[1] // 3
    return call(
        functools.partial(shares_body, experts),
        "shares",
        (order, head, head_other, tail, tail_other, w, gain),
        [
            (w.shape, F32),
            ((rows, features), F32),
            ((experts, rows), F32),
            ((1, rows), F32),
            ((1, rows), F32),
        ],
        [((rows, tail.shape[1]), F32)],
        8,
        1e6,
        hbm=range(5),
    )


def expert_grad_body(count, *refs):
    sources, (in_ref, out_ref, grad_in_ref, grad_out_ref) = refs[:count], refs[count:]
    features = in_ref.shape[0]
    every = jnp.concatenate([source[...] for source in sources], axis=0)
    rows, arriving = every[:, :features], every[:, features:]
    hidden, slope = gelu_parts(dot(rows, in_ref[...]))
    grad_pre = (dot(arriving, out_ref[...], NT) * slope).astype(BF16)
    grad_in_ref[...] = dot(rows, grad_pre, TN)
    grad_out_ref[...] = dot(hidden.astype(BF16), arriving, TN)


def expert_grad(sources, piece_in, piece_out):
    features, hidden = piece_in.shape
    step = 256
    wide = pl.BlockSpec((features, step), lambda i: (0, i))
    high = pl.BlockSpec((step, features), lambda i: (i, 0))
    return pl.pallas_call(
        functools.partial(expert_grad_body, len(sources)),
        grid=(hidden // step,),
        in_specs=[pl.BlockSpec(x.shape, lambda i: (0, 0)) for x in sources] + [wide, high],
        out_specs=[wide, high],
        out_shape=[
            jax.ShapeDtypeStruct(piece_in.shape, F32),
            jax.ShapeDtypeStruct(piece_out.shape, F32),
        ],
        compiler_params=pltpu.CompilerParams(vmem_limit_bytes=16 * 1024 * 1024),
        cost_estimate=pl.CostEstimate(
            flops=1600 * piece_in.size, bytes_accessed=14000000, transcendentals=0
        ),
        name="expert_grad",
    )(*sources, piece_in, piece_out)


def back_body(
    images, places, experts, order_ref, resid_ref, logit_ref, cot_ref, m0, m1, weight, small_ref, *refs
):
    sources, refs = refs[:experts], refs[experts:]
    output_ref, att_ref, grad_mixed_ref, grad_w_ref, grad_side_ref, summed_ref = refs
    slots = logit_ref.shape[0] // images
    router = slot_rows_of(experts, order_ref, small_ref, slots)
    total, features = resid_ref.shape
    tall = total // images
    gain = small_ref[1:2, :]
    high = sources[0].shape[0]
    pick = pick_rows(
        (images * slots, experts * high),
        lambda n: jnp.where(n % slots < experts, n % slots * high + n // slots, -1),
    )
    arrived = jnp.concatenate([source[...] for source in sources], axis=0)
    summed_ref[...] = dot(pick, arrived).astype(BF16)

    def image(i, carry):
        side, gain_sum = carry
        here = rows_of(i, tall)
        group = rows_of(i, slots)
        expert_sum, grad_slots = summed_ref[group, :features], summed_ref[group, features:]
        resid = resid_ref[here, :]
        cot = cot_ref[here, :]
        dispatch, combine = softmaxes(logit_ref[group, :], places, experts)
        output = resid + dot(combine.astype(BF16), expert_sum, TN)
        output_ref[i] = output[:places].astype(BF16)
        normed, factor = normalize(resid)
        act = (normed * gain).astype(BF16)
        grad_comb = dot(expert_sum, cot, NT)
        grad_disp = dot(grad_slots, act, NT)
        grad_logits = combine * (grad_comb - jnp.sum(grad_comb * combine, axis=0, keepdims=True))
        grad_logits = grad_logits + dispatch * (
            grad_disp - jnp.sum(grad_disp * dispatch, axis=1, keepdims=True)
        )
        grad_logits = grad_logits.astype(BF16)
        grad_act = dot(
            jnp.concatenate([dispatch.astype(BF16), grad_logits], axis=0),
            jnp.concatenate([grad_slots, router], axis=0),
            TN,
        )
        att = cot.astype(F32) + norm_back(grad_act * gain, normed, factor)
        att_ref[here, :] = att.astype(BF16)
        return (
            side + dot(grad_logits, act),
            gain_sum + jnp.sum(grad_act * normed, axis=0, keepdims=True),
        )

    together = 6 if images % 6 == 0 else 1

    def some(step, carry):
        for k in range(together):
            carry = image(step * together + k, carry)
        return carry

    carry = (jnp.zeros((slots, features), F32), jnp.zeros((1, features), F32))
    side, gain_sum = lax.fori_loop(0, images // together, some, carry)

    for i in range(images // 2):
        here = rows_of(i, 2 * tall)
        grad_mixed_ref[here, :] = dot(att_ref[here, :], weight[...], NT).astype(BF16)

    part = m0.shape[1]
    grad_w_ref[:part, :] = dot(m0[...], att_ref[...], TN).astype(BF16)
    grad_w_ref[part:, :] = dot(m1[...], att_ref[...], TN).astype(BF16)
    slot = iota((LANES, slots), 0) ^ order_ref[order_ref.shape[0] - 1]
    slot = jnp.where(iota((LANES, slots), 0) < experts, slot, -1)
    fits = jnp.where(slot == iota((LANES, slots), 1), 1.0, 0.0).astype(BF16)
    side = dot(fits, side.astype(BF16))
    side = jnp.where(iota(side.shape, 0) == experts, gain_sum, side)
    grad_side_ref[...] = side.T.astype(BF16)


def back(images, places, experts, order, resid, logits, cot, mixed, w, small, sources):
    total, features = resid.shape
    return call(
        functools.partial(back_body, images, places, experts),
        "back",
        (order, resid, logits, cot, *mixed, w, small, *sources),
        [
            ((images, places, features), BF16),
            ((total, features), BF16),
            ((total, features), BF16),
            ((features, features), BF16),
            ((features, LANES), BF16),
        ],
        [((logits.shape[0], 2 * features), BF16)],
        13,
        8 * total * features * features,
        hbm=(0,),
    )


def attend_back_body(images, extra, offset, order_ref, joint_ref, prob_ref, grad_ref, mixed_ref, act_ref, *refs):
    more, (out_ref, *targets, total) = refs[:extra], refs[extra:]
    width = joint_ref.shape[1]
    tall = joint_ref.shape[0] // images
    third = width // 3
    heads = prob_ref.shape[0] // images
    low = iota((tall, LANES), 1) < LANES // 2

    def back_image(i):
        here = rows_of(i, tall)
        for pair in range(third // LANES):
            query, keys, values = (
                joint_ref[here, part * third + pair * LANES : part * third + (pair + 1) * LANES]
                for part in range(3)
            )
            grad = grad_ref[here, offset + pair * LANES : offset + (pair + 1) * LANES]
            product = grad.astype(F32) * mixed_ref[
                here, pair * LANES : (pair + 1) * LANES
            ].astype(F32)
            query_high, grad_high = query.T, grad.T
            grad_query, grad_keys, grad_values = [], [], []
            for side in range(2):
                mine = low if side == 0 else ~low
                rows = slice(side * LANES // 2, (side + 1) * LANES // 2)
                prob = prob_ref[i * heads + 2 * pair + side]
                inner = jnp.sum(jnp.where(mine, product, 0.0), axis=1, keepdims=True)
                grad_prob = dot(jnp.where(mine, grad, 0), values, NT)
                grad_scores = (prob.astype(F32) * (grad_prob - inner)).astype(BF16)
                grad_query.append(dot(grad_scores, keys))
                grad_keys.append(dot(query_high[rows], grad_scores))
                grad_values.append(dot(grad_high[rows], prob))
            joined = (
                (jnp.where(low, *grad_query) * 0.125).astype(BF16),
                (jnp.concatenate(grad_keys, axis=0) * 0.125).astype(BF16).T,
                jnp.concatenate(grad_values, axis=0).astype(BF16).T,
            )
            for part in range(3):
                out_ref[
                    here, part * third + pair * LANES : part * third + (pair + 1) * LANES
                ] = joined[part]

    each_image(images, 2, back_image)

    step = third
    for start in range(0, width, step):
        total[:, start : start + step] = dot(
            act_ref[...], out_ref[:, start : start + step], TN
        ).astype(BF16)
    store_blocks(order_ref, total, targets, slice(0, width))
    place = width
    for source in more:
        end = place + source.shape[1]
        store_blocks(order_ref, source, targets, slice(place, end))
        place = end


def attend_back(images, offset, order, joint, prob, grad_mixed, mixed, act, splits, more=()):
    total, width = joint.shape
    features = act.shape[1]
    columns = width + sum(m.shape[1] for m in more)
    parts = [((features // n, columns), BF16) for n in splits]
    return call(
        functools.partial(attend_back_body, images, len(more), offset),
        "attend_back",
        (order, joint, prob, grad_mixed, mixed, act, *more),
        [(joint.shape, BF16)] + parts,
        [((features, width), BF16)],
        16,
        2 * total * features * width * 4,
    )


def finish_body(images, places, token_ref, att_ref, j0, j1, s0, s1, small_ref, out_ref):
    total, features = token_ref.shape
    tall = total // images

    @pl.loop(0, images // 2)
    def _(i):
        here = rows_of(i, 2 * tall)
        grad_act = dot(j0[here, :], s0[...], NT) + dot(j1[here, :], s1[...], NT)
        normed, factor = normalize(token_ref[here, :].astype(F32))
        result = att_ref[here, :].astype(F32)
        result = result + norm_back(grad_act * small_ref[0:1, :], normed, factor)
        result = result.astype(BF16)
        out_ref[2 * i] = result[:places]
        out_ref[2 * i + 1] = result[tall : tall + places]


def finish(images, places, tokens, att, joints, weights, small):
    total, features = tokens.shape
    return call(
        functools.partial(finish_body, images, places),
        "finish",
        (tokens, att, *joints, *weights, small),
        [((images, places, features), BF16)],
        [],
        12,
        6 * total * features * features,
        hbm=(0,),
    )[0]


def per_device(
    tokens, cotangent, heads_in, heads_out, slot_router, first_gain, second_gain, expert_in, expert_out
):
    images, places, features = tokens.shape
    experts = slot_router.shape[1]
    group = lax.axis_size("grp")
    reps = lax.axis_size("rep")
    me = lax.axis_index("grp")
    own_rows = heads_in.shape[0]
    chip = me // 2
    odd = lax.axis_index("rep") % 2
    direct = group == 8
    ways = jnp.arange(8, dtype=jnp.int32)
    if direct:
        order = jnp.concatenate([ways ^ me, (ways % 4 * 2 + ways // 4) ^ me, odd[None], chip[None]])
    else:
        order = jnp.concatenate([ways, ways, odd[None], chip[None]])
    tall = -(-places // 16) * 16
    slot_rows = -(-experts // 16) * 16
    part = first_part(features)
    rest = features - part
    wide = 3 * part

    grow = ((0, 0), (0, tall - places), (0, 0))
    source = jnp.pad(tokens, grow).reshape(images * tall, features)
    cot = jnp.pad(cotangent, grow).reshape(images * tall, features)
    if direct:
        rows_in, order = lax.optimization_barrier((heads_in, order))
        small = jnp.concatenate([first_gain[None], second_gain[None], slot_router.T], axis=0)
        extra = -(-small.shape[0] // 16) * 16
        small = jnp.pad(small, ((0, extra - small.shape[0]), (0, LANES - own_rows)))
        h0, h1, t0, t1 = prepare(rows_in, heads_out, small)
        head_first = gather_first((h0, h1))
        head_first = after(head_first, source, cot)
        head_second = gather_second(join((h0, h1), head_first))
        tail_first = gather_first((t0, t1))
        head_second, tail_first = lax.optimization_barrier((head_second, tail_first))
        head = gather_last((h0, h1), head_first, head_second)
        tail_join = join((t0, t1), tail_first)
        source = after(source, *tail_join)
    else:
        thirds = [heads_in[:, k * features : (k + 1) * features] for k in range(3)]
        head_part = jnp.concatenate([t[:, :part] for t in thirds], axis=1)
        tail_part = jnp.concatenate([t[:, part:] for t in thirds] + [heads_out], axis=1)
        small = jnp.concatenate([first_gain[None], second_gain[None], slot_router.T], axis=0)
        extra = -(-small.shape[0] // 16) * 16
        head_part = lax.all_gather(head_part, "grp", axis=0, tiled=True).reshape(8, -1, wide)
        small = lax.all_gather(small, "grp", axis=1, tiled=True).reshape(-1, 8, features // 8)
        small = small.transpose(1, 0, 2)
        small = jnp.pad(small, ((0, 0), (0, extra - small.shape[1]), (0, wide - small.shape[2])))
        head = as_gathered(jnp.concatenate([small, head_part], axis=1), extra + features // 16)
        tail_part = lax.all_gather(tail_part, "grp", axis=0, tiled=True)
        tail = as_gathered(tail_part.reshape(8, -1, 3 * rest + features), features // 16)

    act, small, w_head, joint_head, prob_head, mixed_head = attend(
        True, images, places, order, source, head, wide
    )
    if direct:
        tail_second = after(gather_second(tail_join), mixed_head)
        tail = gather_last((t0, t1), tail_first, tail_second)
    w_out, w_tail, joint_tail, prob_tail, mixed_tail = attend(
        False, images, places, order, act, tail, 3 * rest
    )
    mixes = [mixed_head, mixed_tail]
    resid, logits, *leaving = route(
        images, places, experts, slot_rows, order, source, cot, mixes, w_out, small
    )

    arrived = [leaving[0]] + [swap(leaving[k], "grp", group, 2 * k) for k in range(1, experts)]
    arrived = arrived + [swap(part, "grp", group, 1) for part in arrived]
    piece_in, piece_out = expert_in[0], expert_out[0]
    received, kept, given = expert(images, piece_in, piece_out, arrived)
    both = pair_sum(kept, [swap(given, "grp", group, 1)], experts)
    summed = [both[0]] + [swap(both[k], "grp", group, 2 * k) for k in range(1, experts)]
    received = after(received, *both)
    far = [swap(received, "rep", reps, k) for k in range(1, reps)]
    output, att, grad_mixed, grad_out, grad_side = back(
        images, places, experts, order, resid, logits, cot, mixes, w_out, small, summed
    )
    grad_mixed, far = lax.optimization_barrier((grad_mixed, far))
    grad_joint_tail, keep_tail, give_tail = attend_back(
        images, part, order, joint_tail, prob_tail, grad_mixed, mixed_tail, act, (2, 2), (grad_out, grad_side)
    )
    if direct:
        sums = pair_sum(keep_tail, [swap(give_tail, "grp", group, 1)], 4)
        others = [swap(sums[k], "grp", group, 2 * k) for k in range(1, 4)]
        grad_mixed = after(grad_mixed, *sums)
    grad_joint_head, keep_head, *give_head = attend_back(
        images, 0, order, joint_head, prob_head, grad_mixed, mixed_head, act, (2, 4, 4)
    )
    joints, weights = [grad_joint_head, grad_joint_tail], [w_head, w_tail]
    every = [received] + far
    if direct:
        got = [swap(part, "grp", group, 1) for part in give_head]
        own, others = after((sums[0], others), got)
        mine, give = split_sum(order, own, *others)
        other = swap(give, "rep", reps, 1)
        sums = pair_sum(keep_head, got, 4)
        others = [swap(sums[k], "grp", group, 2 * k) for k in range(1, 4)]
        att = after(att, mine, *sums)
        token_grad = finish(images, places, source, att, joints, weights, small)
        own, others, other = after((sums[0], others, other), token_grad)
        tail_sum = total_sum(mine, other)
        head_sum = total_sum(own, *others)
        every, tail_sum, head_sum = after((every, tail_sum, head_sum), token_grad)
        tail_other = swap(tail_sum, "rep", reps, 2)
        head_other = swap(head_sum, "rep", reps, 1)
        expert_in_grad, expert_out_grad = expert_grad(every, piece_in, piece_out)
        tail_other, head_other = after((tail_other, head_other), expert_in_grad)
        tail_sum, head_sum = total_sum(tail_sum, tail_other), total_sum(head_sum, head_other)
        tail_other = swap(tail_sum, "rep", reps, 1)
        head_other = swap(head_sum, "rep", reps, 3)
        heads_in_grad, heads_out_grad, router_grad, gain_one_grad, gain_two_grad = shares(
            experts, order, head_sum, head_other, tail_sum, tail_other, heads_in, first_gain[None]
        )
        gain_one_grad, gain_two_grad = gain_one_grad[0], gain_two_grad[0]
        router_grad = router_grad.T
    else:
        token_grad = finish(images, places, source, att, joints, weights, small)
        expert_in_grad, expert_out_grad = expert_grad(every, piece_in, piece_out)
        tail_sum = jnp.concatenate([keep_tail, give_tail])
        tail_sum = lax.psum_scatter(tail_sum, "grp", scatter_dimension=0, tiled=True)
        head_sum = jnp.concatenate([keep_head, *give_head])
        head_sum = lax.psum_scatter(head_sum, "grp", scatter_dimension=0, tiled=True)
        tail_sum = lax.psum(tail_sum, "rep").astype(F32)
        head_sum = lax.psum(head_sum, "rep").astype(F32)
        columns = []
        for k in range(3):
            columns.append(head_sum[:, k * part : (k + 1) * part])
            columns.append(tail_sum[:, k * rest : (k + 1) * rest])
        heads_in_grad = jnp.concatenate(columns, axis=1)
        gain_one_grad = jnp.sum(heads_in_grad * heads_in.astype(F32), axis=1)
        gain_one_grad = gain_one_grad / first_gain.astype(F32)
        tail_sum = tail_sum[:, 3 * rest :]
        heads_out_grad, tail_sum = tail_sum[:, :features], tail_sum[:, features:]
        router_grad, gain_two_grad = tail_sum[:, :experts], tail_sum[:, experts]
    return (
        output,
        token_grad,
        heads_in_grad,
        heads_out_grad,
        router_grad,
        gain_one_grad,
        gain_two_grad,
        expert_in_grad[None],
        expert_out_grad[None],
    )


def solution(mesh):
    token_spec = P(("rep", "grp"), None, None)
    matrix, vector, stack = P("grp", None), P("grp"), P("grp", None, None)
    return jax.shard_map(
        per_device,
        mesh=mesh,
        in_specs=(token_spec, token_spec, matrix, matrix, matrix, vector, vector, stack, stack),
        out_specs=(token_spec, token_spec, matrix, matrix, matrix, vector, vector, stack, stack),
        check_vma=False,
    )
```

```python
import functools

import jax
import jax.numpy as jnp
from jax import lax
from jax.experimental import pallas as pl
from jax.experimental.pallas import tpu as pltpu
from jax.sharding import PartitionSpec as P

HEADS = 12
LANES = 128
F32 = jnp.float32
BF16 = jnp.bfloat16
LOW = -1e30

NN = (((1,), (0,)), ((), ()))
NT = (((1,), (1,)), ((), ()))
TN = (((0,), (0,)), ((), ()))


def dot(left, right, form=NN):
    return lax.dot_general(left, right, form, preferred_element_type=F32)


def swap(values, axis, size, bit):
    return lax.ppermute(values, axis, [(place, place ^ bit) for place in range(size)])


def after(values, *others):
    return lax.optimization_barrier((values, others))[0]


def gather_first(own):
    return swap(own[0], "grp", 8, 2), swap(own[1], "grp", 8, 4)


def gather_second(joined):
    return swap(joined[0], "grp", 8, 4), swap(joined[1], "grp", 8, 2)


def gather_last(*stages):
    held = tuple(part for stage in stages for part in stage)
    return held + tuple(swap(part, "grp", 8, 1) for part in held)


def as_gathered(blocks, cut):
    held = []
    for k in range(2):
        own, x, y, far = blocks[k], blocks[k + 2], blocks[k + 4], blocks[k + 6]
        held += [own[:cut], own[cut:], x[:cut], y[cut:]]
        held += [jnp.concatenate([y[:cut], far[:cut]]), jnp.concatenate([x[cut:], far[cut:]])]
    return tuple(held)


def iota(shape, axis):
    return lax.broadcasted_iota(jnp.int32, shape, axis)


def normalize(values):
    center = values - jnp.mean(values, axis=-1, keepdims=True)
    factor = lax.rsqrt(jnp.mean(center * center, axis=-1, keepdims=True) + 1e-06)
    return center * factor, factor


def norm_back(scaled, normed, factor):
    inner = (
        scaled
        - jnp.mean(scaled, axis=-1, keepdims=True)
        - normed * jnp.mean(scaled * normed, axis=-1, keepdims=True)
    )
    return factor * inner


def first_part(features):
    return features // 3


def pieces_of(rows, extra):
    half = rows // 2
    cut = extra + half
    for core in range(2):
        base = 6 * core
        yield base, extra, core, 0
        yield base + 1, 0, core, half
        yield base + 2, extra, core + 2, 0
        yield base + 3, 0, core + 4, half
        yield base + 4, extra, core + 4, 0
        yield base + 4, cut + extra, core + 6, 0
        yield base + 5, 0, core + 2, half
        yield base + 5, half, core + 6, half


def place_pieces(order_ref, pieces, rows, extra, target, columns):
    half = rows // 2
    for n, start, block, offset in pieces_of(rows, extra):
        place = pl.multiple_of(order_ref[block] * rows + offset, 16)
        target[pl.ds(place, half), :] = pieces[n][start : start + half, columns]


def store_blocks(order_ref, source, targets, columns):
    rows = source.shape[0] // 8
    n = 0
    for target in targets:
        for k in range(target.shape[0] // rows):
            start = pl.multiple_of(order_ref[8 + n] * rows, 32)
            target[k * rows : (k + 1) * rows, columns] = source[pl.ds(start, rows), :].astype(BF16)
            n += 1


def gather_small(order_ref, pieces, rows, extra, small_ref):
    total = jnp.zeros(small_ref.shape, F32)
    lane = iota((LANES, small_ref.shape[1]), 0)
    place = iota((LANES, small_ref.shape[1]), 1)
    cut = extra + rows // 2
    for core in range(2):
        for n, start, block in ((0, 0, 0), (2, 0, 2), (4, 0, 4), (4, cut, 6)):
            held = pieces[6 * core + n][start : start + extra, :LANES]
            fits = (place == order_ref[block + core] * rows + lane) & (lane < rows)
            total = total + dot(held, jnp.where(fits, 1.0, 0.0).astype(BF16))
    small_ref[...] = total


def rows_of(place, tall):
    return pl.ds(pl.multiple_of(place * tall, 16), tall)


def each_image(images, together, body):
    if images % together:
        together = 1
    if together == images:
        for i in range(images):
            body(i)
        return

    @pl.loop(0, images // together)
    def _(step):
        for k in range(together):
            body(step * together + k)


VM = pl.BlockSpec(memory_space=pltpu.VMEM)
SM = pl.BlockSpec(memory_space=pltpu.SMEM)


def call(body, name, inputs, outputs, scratch, limit, flops, hbm=()):
    return pl.pallas_call(
        body,
        in_specs=[SM if x.dtype == jnp.int32 else VM for x in inputs],
        out_specs=[VM] * len(outputs),
        out_shape=[
            jax.ShapeDtypeStruct(shape, kind) if n in hbm else pltpu.VMEM(shape, kind)
            for n, (shape, kind) in enumerate(outputs)
        ],
        scratch_shapes=[pltpu.VMEM(shape, kind) for shape, kind in scratch],
        compiler_params=pltpu.CompilerParams(vmem_limit_bytes=(limit if limit == 13 else min(limit, 10)) * 1024 * 1024),
        cost_estimate=pl.CostEstimate(flops=int(flops), bytes_accessed=1000000, transcendentals=0),
        name=name,
    )(*inputs)


def prepare_body(in_hbm, out_hbm, small_ref, h0, h1, t0, t1, in_ref, out_ref, sems):
    rows, features = out_ref.shape
    half = rows // 2
    part = first_part(features)
    rest = features - part
    extra = h0.shape[0] - half
    h0[:extra, :] = jnp.zeros((extra, h0.shape[1]), BF16)
    h0[:extra, :LANES] = small_ref[...]
    copies = [
        pltpu.make_async_copy(source, target, sems.at[k])
        for k, (source, target) in enumerate(((in_hbm, in_ref), (out_hbm, out_ref)))
    ]
    for copy in copies:
        copy.start()
    for copy in copies:
        copy.wait()
    for head, tail, start, here in ((h0, t0, extra, slice(0, half)), (h1, t1, 0, slice(half, rows))):
        for k in range(3):
            base = k * features
            head[start:, k * part : (k + 1) * part] = in_ref[here, base : base + part]
            tail[:, k * rest : (k + 1) * rest] = in_ref[here, base + part : base + features]
        tail[:, 3 * rest :] = out_ref[here, :]


def prepare(heads_in, heads_out, small):
    rows, features = heads_out.shape
    part = first_part(features)
    head, tail = 3 * part, 4 * features - 3 * part
    outputs = [
        (small.shape[0] + rows // 2, head),
        (rows // 2, head),
        (rows // 2, tail),
        (rows // 2, tail),
    ]
    return pl.pallas_call(
        prepare_body,
        in_specs=[pl.BlockSpec(memory_space=pltpu.HBM)] * 2 + [VM],
        out_specs=[VM] * len(outputs),
        out_shape=[pltpu.VMEM(shape, BF16) for shape in outputs],
        scratch_shapes=[
            pltpu.VMEM(heads_in.shape, BF16),
            pltpu.VMEM(heads_out.shape, BF16),
            pltpu.SemaphoreType.DMA((2,)),
        ],
        compiler_params=pltpu.CompilerParams(vmem_limit_bytes=4 * 1024 * 1024),
        name="prepare",
    )(heads_in, heads_out, small)


def join_body(a0, a1, b0, b1, a_ref, b_ref):
    for first, second, target in ((a0, a1, a_ref), (b0, b1, b_ref)):
        target[: first.shape[0], :] = first[...]
        target[first.shape[0] :, :] = second[...]


def join(own, got):
    outputs = [((2 * x.shape[0], x.shape[1]), BF16) for x in own]
    return call(join_body, "join", (own[0], got[0], own[1], got[1]), outputs, [], 4, 1e6)


def attend_body(first, images, places, order_ref, source_ref, *refs):
    pieces, refs = refs[:12], refs[12:]
    features = source_ref.shape[1]
    rows = features // 8
    if first:
        act_ref, small_ref, weight, joint_ref, prob_ref, mixed_ref = refs
        extra = small_ref.shape[0]
    else:
        out_weight, weight, joint_ref, prob_ref, mixed_ref = refs
        act_ref = source_ref
        extra = 0
    tall = source_ref.shape[0] // images
    width = weight.shape[1]
    place_pieces(order_ref, pieces, rows, extra, weight, slice(0, width))
    if first:
        gather_small(order_ref, pieces, rows, extra, small_ref)

        for i in range(images):
            here = rows_of(i, tall)
            normed, _ = normalize(source_ref[here, :].astype(F32))
            act_ref[here, :] = (normed * small_ref[0:1, :]).astype(BF16)
    else:
        place_pieces(order_ref, pieces, rows, 0, out_weight, slice(width, width + features))

    for i in range(images // 2):
        here = rows_of(i, 2 * tall)
        joint_ref[here, :] = dot(act_ref[here, :], weight[...]).astype(BF16)

    third = width // 3
    heads = prob_ref.shape[0] // images
    low = iota((tall, LANES), 1) < LANES // 2
    inside = iota((tall, LANES), 0) < places
    seen = iota((tall, tall), 1) < places

    def attend_image(i):
        here = rows_of(i, tall)
        for pair in range(third // LANES):
            query, keys, values = (
                joint_ref[here, part * third + pair * LANES : part * third + (pair + 1) * LANES]
                for part in range(3)
            )
            query = query * 0.125
            values_ones = jnp.concatenate([values, jnp.ones_like(values)], axis=1)
            outs = []
            for side in range(2):
                mine = low if side == 0 else ~low
                scores = dot(jnp.where(mine, query, 0), keys, NT)
                scores = jnp.where(seen, scores, LOW)
                power = jnp.exp(scores - jnp.max(scores, axis=1, keepdims=True)).astype(BF16)
                got = dot(power, values_ones)
                shrink = 1.0 / got[:, LANES:]
                outs.append(got[:, :LANES] * shrink)
                shrink = jnp.concatenate([shrink, shrink[:, : tall - LANES]], axis=1)
                prob_ref[i * heads + 2 * pair + side] = (power.astype(F32) * shrink).astype(BF16)
            mixed = jnp.where(inside, jnp.where(low, outs[0], outs[1]), 0.0)
            mixed_ref[here, pair * LANES : (pair + 1) * LANES] = mixed.astype(BF16)

    each_image(images, 2, attend_image)


def attend(first, images, places, order, source, pieces, width):
    total, features = source.shape
    tall = total // images
    heads = width // 3 // 64
    extra = pieces[0].shape[0] - features // 16
    outputs = [
        ((features, width), BF16),
        ((total, width), BF16),
        ((images * heads, tall, tall), BF16),
        ((total, width // 3), BF16),
    ]
    if first:
        outputs = [((total, features), BF16), ((extra, features), F32)] + outputs
    else:
        outputs = [((features, features), BF16)] + outputs
    return call(
        functools.partial(attend_body, first, images, places),
        "attend",
        (order, source, *pieces),
        outputs,
        [],
        12,
        1 if first else 2 * total * features * width * 2,
    )


def softmaxes(logits, places, experts):
    rows = iota(logits.shape, 0) < experts
    lanes = iota(logits.shape, 1) < places
    wide = jnp.where(lanes, logits, LOW)
    wide = jnp.exp(wide - jnp.max(wide, axis=1, keepdims=True))
    dispatch = wide / jnp.sum(wide, axis=1, keepdims=True)
    tall = jnp.where(rows, logits, LOW)
    tall = jnp.exp(tall - jnp.max(tall, axis=0, keepdims=True))
    combine = tall / jnp.sum(tall, axis=0, keepdims=True)
    return jnp.where(rows, dispatch, 0.0), combine


def slot_rows_of(experts, order_ref, small_ref, slots):
    rows = small_ref.shape[0]
    slot, row = iota((slots, rows), 0), iota((slots, rows), 1)
    chip = order_ref[order_ref.shape[0] - 1]
    fits = (row == (slot ^ chip) + 2) & (slot < experts)
    return dot(jnp.where(fits, 1.0, 0.0).astype(BF16), small_ref[...].astype(BF16)).astype(BF16)


def pick_rows(shape, wanted):
    row, column = iota(shape, 0), iota(shape, 1)
    return jnp.where(column == wanted(row), 1.0, 0.0).astype(BF16)


def route_body(
    images, places, experts, order_ref, token_ref, cot_ref, m0, m1, weight, small_ref,
    resid_ref, logit_ref, *refs,
):
    out_refs, packed_ref = refs[:-1], refs[-1]
    slots = logit_ref.shape[0] // images
    router = slot_rows_of(experts, order_ref, small_ref, slots)
    tall = token_ref.shape[0] // images
    features = token_ref.shape[1]

    for i in range(images // 2):
        here = rows_of(i, 2 * tall)
        mixed = jnp.concatenate([m0[here, :], m1[here, :]], axis=1)
        resid_ref[here, :] = token_ref[here, :].astype(F32) + dot(mixed, weight[...])

    def route_image(i):
        here = rows_of(i, tall)
        normed, _ = normalize(resid_ref[here, :])
        act = (normed * small_ref[1:2, :]).astype(BF16)
        logits = dot(router, act, NT)
        group = rows_of(i, slots)
        logit_ref[group, :] = logits
        dispatch, combine = softmaxes(logits, places, experts)
        packed_ref[group, :features] = dot(dispatch.astype(BF16), act).astype(BF16)
        packed_ref[group, features:] = dot(combine.astype(BF16), cot_ref[here, :]).astype(BF16)

    each_image(images, 6, route_image)

    high = out_refs[0].shape[0]
    pick = pick_rows(
        (experts * high, images * slots),
        lambda n: jnp.where(n % high < images, n % high * slots + n // high, -1),
    )
    packed = dot(pick, packed_ref[...]).astype(BF16)
    for k, out_ref in enumerate(out_refs):
        out_ref[...] = packed[k * high : (k + 1) * high, :]


def route(images, places, experts, slots, order, tokens, cot, mixed, w, small):
    total, features = tokens.shape
    high = -(-images // 8) * 8
    return call(
        functools.partial(route_body, images, places, experts),
        "route",
        (order, tokens, cot, *mixed, w, small),
        [((total, features), F32), ((images * slots, total // images), F32)]
        + [((high, 2 * features), BF16)] * experts,
        [((images * slots, 2 * features), BF16)],
        10,
        4 * total * features * features,
    )


def gelu_parts(values):
    scale, cubic = 0.7978845608028654, 0.044715
    square = values * values
    bent = jnp.tanh(scale * values * (1.0 + cubic * square))
    half = 0.5 * (1.0 + bent)
    slope = half + 0.5 * values * (1.0 - bent * bent) * scale * (1.0 + 3.0 * cubic * square)
    return values * half, slope


def expert_body(count, images, in_ref, out_ref, *refs):
    sources, (packed_ref, keep_ref, give_ref, rows_ref, back_ref) = refs[:count], refs[count:]
    features = in_ref.shape[0]
    high = sources[0].shape[0]
    for k, source in enumerate(sources):
        rows_ref[k * high : (k + 1) * high, :] = source[...]
    rows, arriving = rows_ref[:, :features], rows_ref[:, features:]
    total = jnp.zeros((rows.shape[0], features), F32)
    grad_total = total
    step = 512
    for start in range(0, in_ref.shape[1], step):
        w_in = in_ref[:, start : start + step]
        w_out = out_ref[start : start + step, :]
        hidden, slope = gelu_parts(dot(rows, w_in))
        grad_pre = (dot(arriving, w_out, NT) * slope).astype(BF16)
        total = total + dot(hidden.astype(BF16), w_out)
        grad_total = grad_total + dot(grad_pre, w_in, NT)
    back_ref[:, :features] = total.astype(BF16)
    back_ref[:, features:] = grad_total.astype(BF16)
    half = keep_ref.shape[0]
    keep_ref[...] = back_ref[:half, :]
    give_ref[...] = back_ref[half:, :]
    pick = pick_rows(
        (packed_ref.shape[0], rows_ref.shape[0]), lambda n: n // images * high + n % images
    )
    packed_ref[...] = dot(pick, rows_ref[...]).astype(BF16)


def expert(images, piece_in, piece_out, sources):
    high, wide = sources[0].shape
    rows = high * len(sources)
    return call(
        functools.partial(expert_body, len(sources), images),
        "expert",
        (piece_in, piece_out, *sources),
        [
            ((images * len(sources), wide), BF16),
            ((rows // 2, wide), BF16),
            ((rows // 2, wide), BF16),
        ],
        [((rows, wide), BF16)] * 2,
        8,
        1e9,
    )


def pair_sum_body(parts, keep_ref, *refs):
    got_refs, out_refs = refs[:parts], refs[parts:]
    rows = out_refs[0].shape[0]
    each = len(out_refs) // parts
    for k, out_ref in enumerate(out_refs):
        kept = keep_ref[k * rows : (k + 1) * rows, :].astype(F32)
        got = got_refs[k // each][k % each * rows : (k % each + 1) * rows, :].astype(F32)
        out_ref[...] = (kept + got).astype(BF16)


def pair_sum(keep, got, count):
    shape = (keep.shape[0] // count, keep.shape[1])
    body = functools.partial(pair_sum_body, len(got))
    return call(body, "pair_sum", (keep, *got), [(shape, BF16)] * count, [], 4, 1e6)


def total_body(*refs):
    refs[-1][...] = sum(ref[...].astype(F32) for ref in refs[:-1]).astype(BF16)


def total_sum(*terms):
    return call(total_body, "total_sum", terms, [(terms[0].shape, BF16)], [], 4, 1e6)[0]


def split_sum_body(order_ref, *refs):
    terms, (mine_ref, give_ref, scratch) = refs[:-3], refs[-3:]
    scratch[...] = sum(ref[...].astype(F32) for ref in terms)
    half = mine_ref.shape[0]
    odd = order_ref[order_ref.shape[0] - 2]
    mine = pl.multiple_of(odd * half, 16)
    other = pl.multiple_of((1 - odd) * half, 16)
    mine_ref[...] = scratch[pl.ds(mine, half), :].astype(BF16)
    give_ref[...] = scratch[pl.ds(other, half), :].astype(BF16)


def split_sum(order, *terms):
    rows, wide = terms[0].shape
    shape = (rows // 2, wide)
    return call(
        split_sum_body, "split_sum", (order, *terms), [(shape, BF16)] * 2, [((rows, wide), F32)], 8, 1e6
    )


def shares_body(
    experts, order_ref, head_ref, head_other, tail_ref, tail_other, w_ref, gain_ref,
    in_ref, out_ref, router_ref, gain_one_ref, gain_two_ref, tail,
):
    rows, features = out_ref.shape
    half = rows // 2
    odd = order_ref[order_ref.shape[0] - 2]
    tail[pl.ds(pl.multiple_of(odd * half, 16), half), :] = tail_ref[...].astype(F32)
    tail[pl.ds(pl.multiple_of((1 - odd) * half, 16), half), :] = tail_other[...].astype(F32)
    part = first_part(features)
    left = features - part
    for k in range(3):
        here = slice(k * part, (k + 1) * part)
        in_ref[:, k * features : k * features + part] = (
            head_ref[:, here].astype(F32) + head_other[:, here].astype(F32)
        )
        in_ref[:, k * features + part : (k + 1) * features] = tail[:, k * left : (k + 1) * left]
    out_ref[...] = tail[:, 3 * left : 3 * left + features]
    rest = tail[:, 3 * left + features :]
    rest = rest.T
    router_ref[...] = rest[:experts, :]
    gain_two_ref[...] = rest[experts : experts + 1, :]
    gain_one = jnp.sum(in_ref[...] * w_ref[...].astype(F32), axis=1, keepdims=True)
    gain_one = jnp.broadcast_to(gain_one, (rows, LANES)).T[:1, :]
    gain_one_ref[...] = gain_one / gain_ref[...].astype(F32)


def shares(experts, order, head, head_other, tail, tail_other, w, gain):
    rows, features = w.shape[0], w.shape[1] // 3
    return call(
        functools.partial(shares_body, experts),
        "shares",
        (order, head, head_other, tail, tail_other, w, gain),
        [
            (w.shape, F32),
            ((rows, features), F32),
            ((experts, rows), F32),
            ((1, rows), F32),
            ((1, rows), F32),
        ],
        [((rows, tail.shape[1]), F32)],
        8,
        1e6,
        hbm=range(5),
    )


def expert_grad_body(count, *refs):
    sources, (in_ref, out_ref, grad_in_ref, grad_out_ref) = refs[:count], refs[count:]
    features = in_ref.shape[0]
    every = jnp.concatenate([source[...] for source in sources], axis=0)
    rows, arriving = every[:, :features], every[:, features:]
    hidden, slope = gelu_parts(dot(rows, in_ref[...]))
    grad_pre = (dot(arriving, out_ref[...], NT) * slope).astype(BF16)
    grad_in_ref[...] = dot(rows, grad_pre, TN)
    grad_out_ref[...] = dot(hidden.astype(BF16), arriving, TN)


def expert_grad(sources, piece_in, piece_out):
    features, hidden = piece_in.shape
    step = 256
    wide = pl.BlockSpec((features, step), lambda i: (0, i))
    high = pl.BlockSpec((step, features), lambda i: (i, 0))
    return pl.pallas_call(
        functools.partial(expert_grad_body, len(sources)),
        grid=(hidden // step,),
        in_specs=[pl.BlockSpec(x.shape, lambda i: (0, 0)) for x in sources] + [wide, high],
        out_specs=[wide, high],
        out_shape=[
            jax.ShapeDtypeStruct(piece_in.shape, F32),
            jax.ShapeDtypeStruct(piece_out.shape, F32),
        ],
        compiler_params=pltpu.CompilerParams(vmem_limit_bytes=16 * 1024 * 1024),
        cost_estimate=pl.CostEstimate(
            flops=1600 * piece_in.size, bytes_accessed=14000000, transcendentals=0
        ),
        name="expert_grad",
    )(*sources, piece_in, piece_out)


def back_body(
    images, places, experts, order_ref, resid_ref, logit_ref, cot_ref, m0, m1, weight, small_ref, *refs
):
    sources, refs = refs[:experts], refs[experts:]
    output_ref, att_ref, grad_mixed_ref, grad_w_ref, grad_side_ref, summed_ref = refs
    slots = logit_ref.shape[0] // images
    router = slot_rows_of(experts, order_ref, small_ref, slots)
    total, features = resid_ref.shape
    tall = total // images
    gain = small_ref[1:2, :]
    high = sources[0].shape[0]
    pick = pick_rows(
        (images * slots, experts * high),
        lambda n: jnp.where(n % slots < experts, n % slots * high + n // slots, -1),
    )
    arrived = jnp.concatenate([source[...] for source in sources], axis=0)
    summed_ref[...] = dot(pick, arrived).astype(BF16)

    def image(i, carry):
        side, gain_sum = carry
        here = rows_of(i, tall)
        group = rows_of(i, slots)
        expert_sum, grad_slots = summed_ref[group, :features], summed_ref[group, features:]
        resid = resid_ref[here, :]
        cot = cot_ref[here, :]
        dispatch, combine = softmaxes(logit_ref[group, :], places, experts)
        output = resid + dot(combine.astype(BF16), expert_sum, TN)
        output_ref[i] = output[:places].astype(BF16)
        normed, factor = normalize(resid)
        act = (normed * gain).astype(BF16)
        grad_comb = dot(expert_sum, cot, NT)
        grad_disp = dot(grad_slots, act, NT)
        grad_logits = combine * (grad_comb - jnp.sum(grad_comb * combine, axis=0, keepdims=True))
        grad_logits = grad_logits + dispatch * (
            grad_disp - jnp.sum(grad_disp * dispatch, axis=1, keepdims=True)
        )
        grad_logits = grad_logits.astype(BF16)
        grad_act = dot(
            jnp.concatenate([dispatch.astype(BF16), grad_logits], axis=0),
            jnp.concatenate([grad_slots, router], axis=0),
            TN,
        )
        att = cot.astype(F32) + norm_back(grad_act * gain, normed, factor)
        att_ref[here, :] = att.astype(BF16)
        return (
            side + dot(grad_logits, act),
            gain_sum + jnp.sum(grad_act * normed, axis=0, keepdims=True),
        )

    together = 6 if images % 6 == 0 else 1

    def some(step, carry):
        for k in range(together):
            carry = image(step * together + k, carry)
        return carry

    carry = (jnp.zeros((slots, features), F32), jnp.zeros((1, features), F32))
    side, gain_sum = lax.fori_loop(0, images // together, some, carry)

    for i in range(images // 2):
        here = rows_of(i, 2 * tall)
        grad_mixed_ref[here, :] = dot(att_ref[here, :], weight[...], NT).astype(BF16)

    part = m0.shape[1]
    grad_w_ref[:part, :] = dot(m0[...], att_ref[...], TN).astype(BF16)
    grad_w_ref[part:, :] = dot(m1[...], att_ref[...], TN).astype(BF16)
    slot = iota((LANES, slots), 0) ^ order_ref[order_ref.shape[0] - 1]
    slot = jnp.where(iota((LANES, slots), 0) < experts, slot, -1)
    fits = jnp.where(slot == iota((LANES, slots), 1), 1.0, 0.0).astype(BF16)
    side = dot(fits, side.astype(BF16))
    side = jnp.where(iota(side.shape, 0) == experts, gain_sum, side)
    grad_side_ref[...] = side.T.astype(BF16)


def back(images, places, experts, order, resid, logits, cot, mixed, w, small, sources):
    total, features = resid.shape
    return call(
        functools.partial(back_body, images, places, experts),
        "back",
        (order, resid, logits, cot, *mixed, w, small, *sources),
        [
            ((images, places, features), BF16),
            ((total, features), BF16),
            ((total, features), BF16),
            ((features, features), BF16),
            ((features, LANES), BF16),
        ],
        [((logits.shape[0], 2 * features), BF16)],
        13,
        8 * total * features * features,
        hbm=(0,),
    )


def attend_back_body(images, extra, offset, order_ref, joint_ref, prob_ref, grad_ref, mixed_ref, act_ref, *refs):
    more, (out_ref, *targets, total) = refs[:extra], refs[extra:]
    width = joint_ref.shape[1]
    tall = joint_ref.shape[0] // images
    third = width // 3
    heads = prob_ref.shape[0] // images
    low = iota((tall, LANES), 1) < LANES // 2

    def back_image(i):
        here = rows_of(i, tall)
        for pair in range(third // LANES):
            query, keys, values = (
                joint_ref[here, part * third + pair * LANES : part * third + (pair + 1) * LANES]
                for part in range(3)
            )
            grad = grad_ref[here, offset + pair * LANES : offset + (pair + 1) * LANES]
            product = grad.astype(F32) * mixed_ref[
                here, pair * LANES : (pair + 1) * LANES
            ].astype(F32)
            query_high, grad_high = query.T, grad.T
            grad_query, grad_keys, grad_values = [], [], []
            for side in range(2):
                mine = low if side == 0 else ~low
                rows = slice(side * LANES // 2, (side + 1) * LANES // 2)
                prob = prob_ref[i * heads + 2 * pair + side]
                inner = jnp.sum(jnp.where(mine, product, 0.0), axis=1, keepdims=True)
                grad_prob = dot(jnp.where(mine, grad, 0), values, NT)
                grad_scores = (prob.astype(F32) * (grad_prob - inner)).astype(BF16)
                grad_query.append(dot(grad_scores, keys))
                grad_keys.append(dot(query_high[rows], grad_scores))
                grad_values.append(dot(grad_high[rows], prob))
            joined = (
                (jnp.where(low, *grad_query) * 0.125).astype(BF16),
                (jnp.concatenate(grad_keys, axis=0) * 0.125).astype(BF16).T,
                jnp.concatenate(grad_values, axis=0).astype(BF16).T,
            )
            for part in range(3):
                out_ref[
                    here, part * third + pair * LANES : part * third + (pair + 1) * LANES
                ] = joined[part]

    each_image(images, 2, back_image)

    step = third
    for start in range(0, width, step):
        total[:, start : start + step] = dot(
            act_ref[...], out_ref[:, start : start + step], TN
        ).astype(BF16)
    store_blocks(order_ref, total, targets, slice(0, width))
    place = width
    for source in more:
        end = place + source.shape[1]
        store_blocks(order_ref, source, targets, slice(place, end))
        place = end


def attend_back(images, offset, order, joint, prob, grad_mixed, mixed, act, splits, more=()):
    total, width = joint.shape
    features = act.shape[1]
    columns = width + sum(m.shape[1] for m in more)
    parts = [((features // n, columns), BF16) for n in splits]
    return call(
        functools.partial(attend_back_body, images, len(more), offset),
        "attend_back",
        (order, joint, prob, grad_mixed, mixed, act, *more),
        [(joint.shape, BF16)] + parts,
        [((features, width), BF16)],
        16,
        2 * total * features * width * 4,
    )


def finish_body(images, places, token_ref, att_ref, j0, j1, s0, s1, small_ref, out_ref):
    total, features = token_ref.shape
    tall = total // images

    @pl.loop(0, images // 2)
    def _(i):
        here = rows_of(i, 2 * tall)
        grad_act = dot(j0[here, :], s0[...], NT) + dot(j1[here, :], s1[...], NT)
        normed, factor = normalize(token_ref[here, :].astype(F32))
        result = att_ref[here, :].astype(F32)
        result = result + norm_back(grad_act * small_ref[0:1, :], normed, factor)
        result = result.astype(BF16)
        out_ref[2 * i] = result[:places]
        out_ref[2 * i + 1] = result[tall : tall + places]


def finish(images, places, tokens, att, joints, weights, small):
    total, features = tokens.shape
    return call(
        functools.partial(finish_body, images, places),
        "finish",
        (tokens, att, *joints, *weights, small),
        [((images, places, features), BF16)],
        [],
        12,
        6 * total * features * features,
        hbm=(0,),
    )[0]


def per_device(
    tokens, cotangent, heads_in, heads_out, slot_router, first_gain, second_gain, expert_in, expert_out
):
    images, places, features = tokens.shape
    experts = slot_router.shape[1]
    group = lax.axis_size("grp")
    reps = lax.axis_size("rep")
    me = lax.axis_index("grp")
    own_rows = heads_in.shape[0]
    chip = me // 2
    odd = lax.axis_index("rep") % 2
    direct = group == 8
    ways = jnp.arange(8, dtype=jnp.int32)
    if direct:
        order = jnp.concatenate([ways ^ me, (ways % 4 * 2 + ways // 4) ^ me, odd[None], chip[None]])
    else:
        order = jnp.concatenate([ways, ways, odd[None], chip[None]])
    tall = -(-places // 16) * 16
    slot_rows = -(-experts // 16) * 16
    part = first_part(features)
    rest = features - part
    wide = 3 * part

    grow = ((0, 0), (0, tall - places), (0, 0))
    source = jnp.pad(tokens, grow).reshape(images * tall, features)
    cot = jnp.pad(cotangent, grow).reshape(images * tall, features)
    if direct:
        rows_in, order = lax.optimization_barrier((heads_in, order))
        small = jnp.concatenate([first_gain[None], second_gain[None], slot_router.T], axis=0)
        extra = -(-small.shape[0] // 16) * 16
        small = jnp.pad(small, ((0, extra - small.shape[0]), (0, LANES - own_rows)))
        h0, h1, t0, t1 = prepare(rows_in, heads_out, small)
        head_first = gather_first((h0, h1))
        head_first = after(head_first, source, cot)
        head_second = gather_second(join((h0, h1), head_first))
        tail_first = gather_first((t0, t1))
        head_second, tail_first = lax.optimization_barrier((head_second, tail_first))
        head = gather_last((h0, h1), head_first, head_second)
        tail_join = join((t0, t1), tail_first)
        source = after(source, *tail_join)
    else:
        thirds = [heads_in[:, k * features : (k + 1) * features] for k in range(3)]
        head_part = jnp.concatenate([t[:, :part] for t in thirds], axis=1)
        tail_part = jnp.concatenate([t[:, part:] for t in thirds] + [heads_out], axis=1)
        small = jnp.concatenate([first_gain[None], second_gain[None], slot_router.T], axis=0)
        extra = -(-small.shape[0] // 16) * 16
        head_part = lax.all_gather(head_part, "grp", axis=0, tiled=True).reshape(8, -1, wide)
        small = lax.all_gather(small, "grp", axis=1, tiled=True).reshape(-1, 8, features // 8)
        small = small.transpose(1, 0, 2)
        small = jnp.pad(small, ((0, 0), (0, extra - small.shape[1]), (0, wide - small.shape[2])))
        head = as_gathered(jnp.concatenate([small, head_part], axis=1), extra + features // 16)
        tail_part = lax.all_gather(tail_part, "grp", axis=0, tiled=True)
        tail = as_gathered(tail_part.reshape(8, -1, 3 * rest + features), features // 16)

    act, small, w_head, joint_head, prob_head, mixed_head = attend(
        True, images, places, order, source, head, wide
    )
    if direct:
        tail_second = after(gather_second(tail_join), mixed_head)
        tail = gather_last((t0, t1), tail_first, tail_second)
    w_out, w_tail, joint_tail, prob_tail, mixed_tail = attend(
        False, images, places, order, act, tail, 3 * rest
    )
    mixes = [mixed_head, mixed_tail]
    resid, logits, *leaving = route(
        images, places, experts, slot_rows, order, source, cot, mixes, w_out, small
    )

    arrived = [leaving[0]] + [swap(leaving[k], "grp", group, 2 * k) for k in range(1, experts)]
    arrived = arrived + [swap(part, "grp", group, 1) for part in arrived]
    piece_in, piece_out = expert_in[0], expert_out[0]
    received, kept, given = expert(images, piece_in, piece_out, arrived)
    both = pair_sum(kept, [swap(given, "grp", group, 1)], experts)
    summed = [both[0]] + [swap(both[k], "grp", group, 2 * k) for k in range(1, experts)]
    received = after(received, *both)
    far = [swap(received, "rep", reps, k) for k in range(1, reps)]
    output, att, grad_mixed, grad_out, grad_side = back(
        images, places, experts, order, resid, logits, cot, mixes, w_out, small, summed
    )
    grad_mixed, near = lax.optimization_barrier((grad_mixed, far[:1]))
    grad_joint_tail, keep_tail, give_tail = attend_back(
        images, part, order, joint_tail, prob_tail, grad_mixed, mixed_tail, act, (2, 2), (grad_out, grad_side)
    )
    if direct:
        sums = pair_sum(keep_tail, [swap(give_tail, "grp", group, 1)], 4)
        others = [swap(sums[k], "grp", group, 2 * k) for k in range(1, 4)]
        grad_mixed = after(grad_mixed, *sums)
    grad_joint_head, keep_head, *give_head = attend_back(
        images, 0, order, joint_head, prob_head, grad_mixed, mixed_head, act, (2, 4, 4)
    )
    joints, weights = [grad_joint_head, grad_joint_tail], [w_head, w_tail]
    every = [received] + near + after(far[1:], grad_joint_tail)
    if direct:
        got = [swap(part, "grp", group, 1) for part in give_head]
        own, others = after((sums[0], others), got)
        mine, give = split_sum(order, own, *others)
        other = swap(give, "rep", reps, 1)
        sums = pair_sum(keep_head, got, 4)
        others = [swap(sums[k], "grp", group, 2 * k) for k in range(1, 4)]
        att = after(att, mine, *sums)
        token_grad = finish(images, places, source, att, joints, weights, small)
        own, others, other = after((sums[0], others, other), token_grad)
        tail_sum = total_sum(mine, other)
        head_sum = total_sum(own, *others)
        every, tail_sum, head_sum = after((every, tail_sum, head_sum), token_grad)
        tail_other = swap(tail_sum, "rep", reps, 2)
        head_other = swap(head_sum, "rep", reps, 1)
        expert_in_grad, expert_out_grad = expert_grad(every, piece_in, piece_out)
        tail_other, head_other = after((tail_other, head_other), expert_in_grad)
        tail_sum, head_sum = total_sum(tail_sum, tail_other), total_sum(head_sum, head_other)
        tail_other = swap(tail_sum, "rep", reps, 1)
        head_other = swap(head_sum, "rep", reps, 3)
        heads_in_grad, heads_out_grad, router_grad, gain_one_grad, gain_two_grad = shares(
            experts, order, head_sum, head_other, tail_sum, tail_other, heads_in, first_gain[None]
        )
        gain_one_grad, gain_two_grad = gain_one_grad[0], gain_two_grad[0]
        router_grad = router_grad.T
    else:
        token_grad = finish(images, places, source, att, joints, weights, small)
        expert_in_grad, expert_out_grad = expert_grad(every, piece_in, piece_out)
        tail_sum = jnp.concatenate([keep_tail, give_tail])
        tail_sum = lax.psum_scatter(tail_sum, "grp", scatter_dimension=0, tiled=True)
        head_sum = jnp.concatenate([keep_head, *give_head])
        head_sum = lax.psum_scatter(head_sum, "grp", scatter_dimension=0, tiled=True)
        tail_sum = lax.psum(tail_sum, "rep").astype(F32)
        head_sum = lax.psum(head_sum, "rep").astype(F32)
        columns = []
        for k in range(3):
            columns.append(head_sum[:, k * part : (k + 1) * part])
            columns.append(tail_sum[:, k * rest : (k + 1) * rest])
        heads_in_grad = jnp.concatenate(columns, axis=1)
        gain_one_grad = jnp.sum(heads_in_grad * heads_in.astype(F32), axis=1)
        gain_one_grad = gain_one_grad / first_gain.astype(F32)
        tail_sum = tail_sum[:, 3 * rest :]
        heads_out_grad, tail_sum = tail_sum[:, :features], tail_sum[:, features:]
        router_grad, gain_two_grad = tail_sum[:, :experts], tail_sum[:, experts]
    return (
        output,
        token_grad,
        heads_in_grad,
        heads_out_grad,
        router_grad,
        gain_one_grad,
        gain_two_grad,
        expert_in_grad[None],
        expert_out_grad[None],
    )


def solution(mesh):
    token_spec = P(("rep", "grp"), None, None)
    matrix, vector, stack = P("grp", None), P("grp"), P("grp", None, None)
    return jax.shard_map(
        per_device,
        mesh=mesh,
        in_specs=(token_spec, token_spec, matrix, matrix, matrix, vector, vector, stack, stack),
        out_specs=(token_spec, token_spec, matrix, matrix, matrix, vector, vector, stack, stack),
        check_vma=False,
    )
```
